32 devices in a mesh: groups: 2 (over x), seq: 16 (over z, y, core).
Axes of the slice: x: 2, y: 2, z: 4, core: 2. Of those that a mesh axis runs over, the one named last changes fastest.
Arguments:
- queries: bfloat16 [6, 16, 16, 2560], P('groups', 'seq'), parts along dimension 0, may hold values from -6 to 6
- keys: bfloat16 [6, 16, 16, 2560], P('groups', 'seq'), parts along dimension 0, may hold values from -6 to 6
- values: bfloat16 [6, 16, 16, 2560], P('groups', 'seq'), parts along dimension 0, may hold values from -6 to 6
- stream: bfloat16 [6, 16, 16, 2560], P('groups', 'seq'), parts along dimension 0, may hold values from -3 to 3
- head_weight: bfloat16 [2560, 64], replicated, may hold values from -0.125 to 0.125
- conv_in_weight: bfloat16 [3, 3, 3, 16, 384], replicated, may hold values from -0.3125 to 0.3125
- norm_gain: float32 [384], replicated, may hold values from 0.5 to 1.5
- norm_shift: float32 [384], replicated, may hold values from -3 to 3
- conv_mid_weight: bfloat16 [3, 3, 3, 384, 384], replicated, may hold values from -0.0625 to 0.0625
Outputs:
- decoded: bfloat16 [6, 32, 32, 384], P('groups', 'seq'), parts along dimension 0
The draws below stay inside these ranges and needn't reach their ends.
There are 2 independent parts, one for each index of `groups`. The reference program is written for one: setup_inputs(seed, part) draws one part's arguments, and reference() takes and returns one part's arrays. A program takes and returns all parts, laid end to end along the dimension named above; an argument that names none is the same for every part. Nothing has to cross between parts.
All inputs are finite; a program needn't handle non-finite values.
Results may differ from the reference program's by a relative error of at most 0.01.
Values may be sent and summed in bfloat16 or wider, within the bound.
No kernel may reach another device: no remote copies, remote signals or barrier semaphores. Data moves between devices by JAX's collectives and lax.ppermute only.
A program may use at most 128 MiB of HBM per device.

```python
import jax
import jax.numpy as jnp
from jax import lax

HEADS = 20
HD = 128
LAT = 16
CH = 384
GROUPS = 32
FR = 3
COLS = 16
TROWS = 16


def drawn_field(key, factor):
    drawn = jax.random.normal(key, (FR, TROWS, COLS, HEADS, HD), jnp.float32)
    return jnp.clip(drawn * factor, -6.0, 6.0)


def draw_queries(key, part):
    field = drawn_field(jax.random.fold_in(key, 1), 2.0)
    return field.reshape(FR, TROWS, COLS, HEADS * HD).astype(jnp.bfloat16)


def draw_keys(key, part):
    field = drawn_field(jax.random.fold_in(key, 2), 1.0)
    return field.reshape(FR, TROWS, COLS, HEADS * HD).astype(jnp.bfloat16)


def draw_stream(key, part):
    width = HEADS * HD
    noise_key = jax.random.fold_in(key, 7)
    common_key = jax.random.fold_in(key, 8)
    place = jnp.arange(TROWS, dtype=jnp.float32) / max(TROWS - 1, 1)
    noise = jnp.clip(jax.random.normal(noise_key, (FR, TROWS, COLS, width), jnp.float32), -6.0, 6.0)
    rising = 0.5 + 2.5 * place
    common = jnp.clip(jax.random.normal(common_key, (width,), jnp.float32), -3.0, 3.0)
    field = rising[None, :, None, None] * (0.05 * noise + 0.15 * common)
    return field.astype(jnp.bfloat16)


def steps_of(rng, dims, cuts, low, high):
    factor_of, own = 1.0, jax.random.fold_in(rng, 6)
    for axis_at, shards_of in cuts:
        steps = jnp.exp(jax.random.uniform(jax.random.fold_in(own, axis_at), (shards_of,), jnp.float32, low / len(cuts), high / len(cuts)))
        factor_of = factor_of * jnp.repeat(steps, dims[axis_at] // shards_of).reshape([-1 if axis == axis_at else 1 for axis in range(len(dims))])
    return factor_of


def centred(own_key, dims, deviation, limit, shards=(), kind=jnp.bfloat16):
    values = jax.random.normal(own_key, dims, jnp.float32) * deviation
    if len(shards) > 0:
        values = steps_of(own_key, dims, shards, -0.22, 0.18) * values
    return jnp.clip(values, min=-limit, max=limit).astype(kind)


def setup_inputs(seed: int = 0, part: int = 0) -> dict:
    streams_of = jax.random.split(jax.random.key(seed), 10)
    own_keys = jax.random.split(jax.random.fold_in(streams_of[9], part), 10)
    return {
        "queries": draw_queries(jax.random.fold_in(jax.random.fold_in(streams_of[9], part), 71), part),
        "keys": draw_keys(jax.random.fold_in(jax.random.fold_in(streams_of[9], part), 71), part),
        "values": centred(own_keys[2], (FR, TROWS, COLS, HEADS * HD), 1.0, 6.0, ((1, 16),)),
        "stream": draw_stream(jax.random.fold_in(jax.random.fold_in(streams_of[9], part), 71), part),
        "head_weight": centred(streams_of[4], (HEADS * HD, 4 * LAT), (HEADS * HD) ** -0.5, 0.125),
        "conv_in_weight": centred(streams_of[5], (3, 3, 3, LAT, CH), (27 * LAT) ** -0.5, 0.3125),
        "norm_gain": jnp.clip(1.0 + 0.1 * jax.random.normal(streams_of[6], (CH,), jnp.float32), 0.5, 1.5),
        "norm_shift": centred(streams_of[7], (CH,), 0.5, 3.0, (), jnp.float32),
        "conv_mid_weight": centred(streams_of[8], (3, 3, 3, CH, CH), (27 * CH) ** -0.5, 0.0625),
    }


def conv_taps(padded, weight, frames, rows, cols):
    inner = padded.shape[-1]
    total = jnp.zeros((frames * rows * cols, weight.shape[-1]), jnp.float32)
    for step_t in range(3):
        for step_h in range(3):
            for step_w in range(3):
                piece = padded[step_t:step_t + frames, step_h:step_h + rows, step_w:step_w + cols, :].reshape(-1, inner)
                total = total + jnp.dot(piece, weight[step_t, step_h, step_w], preferred_element_type=jnp.float32)
    return total.reshape(frames, rows, cols, -1)

def pad_causal(field):
    return jnp.pad(field, ((2, 0), (1, 1), (1, 1), (0, 0)))

def reference(queries, keys, values, stream, head_weight, conv_in_weight, norm_gain, norm_shift, conv_mid_weight):
    frames, trows, cols, width = queries.shape
    depth = width // HEADS
    query_flat = queries.reshape(-1, HEADS, depth)
    key_flat = keys.reshape(-1, HEADS, depth)
    value_flat = values.reshape(-1, HEADS, depth)
    scale = 1.0 / depth ** 0.5

    def one_head(head):
        query_head = lax.dynamic_index_in_dim(query_flat, head, 1, keepdims=False)
        key_head = lax.dynamic_index_in_dim(key_flat, head, 1, keepdims=False)
        value_head = lax.dynamic_index_in_dim(value_flat, head, 1, keepdims=False)
        scores = jnp.dot(query_head, key_head.T, preferred_element_type=jnp.float32) * scale
        top = lax.optimization_barrier(jnp.max(scores, axis=-1, keepdims=True))
        expo = jnp.exp(scores - top)
        total = lax.optimization_barrier(jnp.sum(expo, axis=-1, keepdims=True))
        summed = jnp.dot(expo.astype(jnp.bfloat16), value_head, preferred_element_type=jnp.float32)
        return (summed / total).astype(jnp.bfloat16)
    heads_out = lax.map(one_head, jnp.arange(HEADS, dtype=jnp.int32))
    attended = jnp.transpose(heads_out, (1, 0, 2)).reshape(-1, width)
    latent = jnp.dot(stream.reshape(-1, width), head_weight, preferred_element_type=jnp.float32) + jnp.dot(attended, head_weight, preferred_element_type=jnp.float32)
    latent = latent.reshape(frames, trows, cols, 2, 2, -1).transpose(0, 1, 3, 2, 4, 5)
    latent = latent.reshape(frames, 2 * trows, 2 * cols, -1).astype(jnp.bfloat16)
    rows, wide = (2 * trows, 2 * cols)
    first = conv_taps(pad_causal(latent), conv_in_weight, frames, rows, wide)
    grouped = first.reshape(frames, rows, wide, GROUPS, -1)
    mean = lax.optimization_barrier(jnp.mean(grouped, axis=(0, 1, 2, 4)))
    centered = grouped - mean[:, None]
    variance = lax.optimization_barrier(jnp.mean(centered * centered, axis=(0, 1, 2, 4)))
    normed = (centered / jnp.sqrt(variance + 1e-06)[:, None]).reshape(frames, rows, wide, -1)
    active = jax.nn.silu(normed * norm_gain + norm_shift).astype(jnp.bfloat16)
    second = conv_taps(pad_causal(active), conv_mid_weight, frames, rows, wide)
    return (first + second).astype(jnp.bfloat16)
```

```python
import functools

import jax
import jax.numpy as jnp
from jax import lax
from jax.experimental import pallas as pl
from jax.experimental.pallas import tpu as pltpu
from jax.sharding import PartitionSpec as P

HEADS = 20
GROUPS = 32
SPLIT = 4
EPS = 1e-06

VMEM = pl.BlockSpec(memory_space=pltpu.VMEM)
SMEM = pl.BlockSpec(memory_space=pltpu.SMEM)
ANY = pl.BlockSpec(memory_space=pl.ANY)


def exchanged(value, mask):
    pairs = [(source, source ^ mask) for source in range(lax.axis_size("seq"))]
    return lax.ppermute(value, "seq", pairs)


def rest_mask(member):
    return (member & 3) | ((member >> 2) << 4)


def dot(left, right):
    return jnp.dot(left, right, preferred_element_type=jnp.float32)


def prepare_kernel(depth, heads, index, q, k, v, s, w, *refs):
    kv_out, q_out, stream_out, projected = refs[:SPLIT], refs[SPLIT : 2 * SPLIT], refs[-2], refs[-1]
    tokens = q.shape[0]
    group = heads * depth
    place = (index[0] >> 2) & 3
    twice = jnp.concatenate([w[...], w[...]], axis=1)
    low = lax.broadcasted_iota(jnp.int32, (tokens, 2 * w.shape[1]), 1) < w.shape[1]

    def through(head):
        return dot(v[:, head * depth : (head + 1) * depth], twice[head * depth : (head + 1) * depth])

    wide = twice.shape[1]
    for owner in range(SPLIT):
        for pair in range((heads + 1) // 2):
            first = owner * heads + 2 * pair
            both = through(first)
            if 2 * pair + 1 < heads:
                both = jnp.where(low, both, through(first + 1))
            projected[owner, :, pair * wide : (pair + 1) * wide] = both.astype(jnp.bfloat16)
    for step in range(SPLIT):
        owner = place ^ step
        columns = pl.ds(pl.multiple_of(owner * group, 128), group)
        kv_out[step][:, :group] = k[:, columns]
        kv_out[step][:, group:] = projected[owner]
        q_out[step][...] = q[:, columns]
    stream_out[...] = dot(s[...], twice)


def attend_kernel(depth, heads, *refs):
    q, kv, stream, out = refs[:SPLIT], refs[SPLIT:-2], refs[-2], refs[-1]
    tokens = q[0].shape[0]
    wide = stream.shape[1]
    factor = 1.4426950408889634 / depth**0.5
    rows = SPLIT * tokens
    low = lax.broadcasted_iota(jnp.int32, (rows, wide), 1) < wide // 2
    total_out = jnp.zeros((rows, wide), jnp.float32)
    for head in range(heads):
        columns = slice(head * depth, (head + 1) * depth)
        query = jnp.concatenate([piece[:, columns] for piece in q], axis=0)
        key = jnp.concatenate([piece[:, columns] for piece in kv], axis=0)
        at = heads * depth + (head // 2) * wide
        value = jnp.concatenate([piece[:, at : at + wide] for piece in kv], axis=0)
        scores = lax.dot_general(query, key, (((1,), (1,)), ((), ())), preferred_element_type=jnp.float32)
        top = jnp.max(scores, axis=1, keepdims=True)
        expo = jnp.exp2((scores - top) * factor)
        total = jnp.sum(expo, axis=1, keepdims=True)
        mixed = dot(expo.astype(jnp.bfloat16), value) * (1.0 / total)
        mine = low if head % 2 == 0 else jnp.logical_not(low)
        total_out = total_out + jnp.where(mine, mixed, 0.0)
    total_out = total_out + pltpu.roll(total_out, wide // 2, 1)
    half = rows // 2
    upper = total_out[:half]
    upper = jnp.concatenate([upper[:tokens] + stream[...], upper[tokens:]], axis=0)
    out[...] = jnp.where(low[:half], upper, total_out[half:])


def gather_kernel(cols, own, one, two, three, chosen, out):
    rows, wide = own.shape
    half = rows // 2

    def swap_rows(x):
        return jnp.concatenate([x[half:], x[:half]], axis=0)

    far = two[...] + swap_rows(three[...])
    latent = (own[...] + swap_rows(one[...])) + pltpu.roll(far, wide // 2, 1)
    latent = latent.astype(jnp.bfloat16).astype(jnp.float32)
    column = lax.broadcasted_iota(jnp.int32, (rows, wide), 0) % cols
    before = jnp.where(column == 0, 0.0, pltpu.roll(latent, 1, 0))
    after = jnp.where(column == cols - 1, 0.0, pltpu.roll(latent, rows - 1, 0))
    row = jnp.concatenate([before, latent, after], axis=1).astype(jnp.bfloat16)
    out[...] = dot(row, chosen[...]).astype(jnp.bfloat16)


def finish_kernel(frames, n, cols, index, *refs):
    members = n // SPLIT
    patches, refs = refs[:members], refs[members:]
    (in_weight, mid_weight, grouped, gain, shift, out, grid, stacked, first, taps, held, merged, sem) = refs
    channels = gain.shape[1]
    wide = grid.shape[-1]
    half = wide // 2
    me = index[0]
    copies = [
        pltpu.make_async_copy(mid_weight.at[a], held.at[a], sem.at[a]) for a in range(mid_weight.shape[0])
    ]
    for copy in copies:
        copy.start()

    grid[:, 0] = jnp.zeros((frames, cols, wide), jnp.bfloat16)
    grid[:, n + 1] = jnp.zeros((frames, cols, wide), jnp.bfloat16)
    tokens = frames * cols
    for member in range(members):
        for step in range(SPLIT):
            row = me ^ (rest_mask(member) | (step << 2))
            at, lanes = (step % 2) * tokens, (step // 2) * wide
            for t in range(frames):
                grid[t, row + 1] = patches[member][at + t * cols : at + (t + 1) * cols, lanes : lanes + wide]

    cells = n * cols
    chunk = min(cells, 256)
    rows_in = chunk // cols
    upper = lax.broadcasted_iota(jnp.int32, (rows_in, cols, wide), 2) < half
    depth = 2 * wide
    for t in range(frames):
        for r in range(0, n, rows_in):
            near = grid[t, r + 1 : r + 1 + rows_in]
            far = jnp.where(upper, grid[t, r + 2 : r + 2 + rows_in], grid[t, r : r + rows_in])
            stacked[r * cols : r * cols + chunk, t * depth : t * depth + wide] = near.reshape(chunk, wide)
            stacked[r * cols : r * cols + chunk, t * depth + wide : (t + 1) * depth] = far.reshape(chunk, wide)

    sums = jnp.zeros((8, channels), jnp.float32)
    for t in range(frames):
        for r in range(0, n, rows_in):
            for part in range(4):
                lanes = slice(part * channels, (part + 1) * channels)
                here = dot(
                    stacked[r * cols : r * cols + chunk, : (t + 1) * depth],
                    in_weight[(frames - 1 - t) * depth :, lanes],
                )
                first[t, r : r + rows_in, :, lanes] = here.reshape(rows_in, cols, channels)
                sums = sums + jnp.sum(here.reshape(chunk // 8, 8, channels), axis=0)
    counted = 4.0 * frames * cells * (channels // GROUPS)

    def over_group(eight):
        line = jnp.sum(eight, axis=0, keepdims=True)
        return jnp.dot(line, grouped[...], precision=lax.Precision.HIGHEST, preferred_element_type=jnp.float32)

    mean = over_group(sums) / counted
    squares = jnp.zeros((8, channels), jnp.float32)
    for t in range(frames):
        for r in range(0, n, rows_in):
            for part in range(4):
                lanes = slice(part * channels, (part + 1) * channels)
                off = first[t, r : r + rows_in, :, lanes].reshape(chunk, channels) - mean
                squares = squares + jnp.sum((off * off).reshape(chunk // 8, 8, channels), axis=0)
    variance = over_group(squares) / counted
    slope = gain[...] * (1.0 / jnp.sqrt(variance + EPS))
    bias = shift[...]

    place = lax.broadcasted_iota(jnp.int32, (cols, channels), 0)
    for t in range(frames):
        for line in range(4):
            sub = 1 if line in (0, 2) else 0
            token_row = me - 1 if line == 0 else (me + 1 if line == 3 else me)
            inside = jnp.logical_and(token_row >= 0, token_row < n)
            token_row = jnp.clip(token_row, 0, n - 1)
            keep = jnp.where(inside, 1.0, 0.0)
            pair = []
            for side in range(2):
                part = sub * 2 + side
                x = first[t, token_row, :, part * channels : (part + 1) * channels]
                y = (x - mean) * slope + bias
                pair.append(y / (1.0 + jnp.exp(-y)) * keep)
            even, odd = pair
            taps[t, line, 0] = jnp.where(place == 0, 0.0, pltpu.roll(odd, 1, 0)).astype(jnp.bfloat16)
            taps[t, line, 1] = even.astype(jnp.bfloat16)
            taps[t, line, 2] = odd.astype(jnp.bfloat16)
            taps[t, line, 3] = jnp.where(place == cols - 1, 0.0, pltpu.roll(even, cols - 1, 0)).astype(jnp.bfloat16)

    for copy in copies:
        copy.wait()
    here = 4 * cols
    totals = [jnp.zeros((here, channels), jnp.float32) for _ in range(frames)]
    for a in range(frames):
        valid = a + 1
        for b in range(3):
            left = jnp.concatenate(
                [taps[:valid, b : b + 2, w : w + 2].reshape(valid * here, channels) for w in range(3)], axis=1
            )
            got = dot(left, held[a, b].reshape(3 * channels, channels))
            for t in range(valid):
                totals[frames - 1 - a + t] = totals[frames - 1 - a + t] + got[t * here : (t + 1) * here]
    for t in range(frames):
        for part in range(4):
            kept = first[t, me, :, part * channels : (part + 1) * channels]
            block = totals[t][part * cols : (part + 1) * cols] + kept
            for lane in range(channels // 128):
                tile = block[:, lane * 128 : (lane + 1) * 128]
                merged[t, part // 2, lane, pl.ds(part % 2, cols, stride=2), :] = tile
    for t in range(frames):
        for sub in range(2):
            for lane in range(channels // 128):
                out[t, sub, :, lane * 128 : (lane + 1) * 128] = merged[t, sub, lane].astype(jnp.bfloat16)


def widened(weight):
    blocks = []
    for row in range(2):
        for col in range(2):
            blocks.append(jnp.pad(weight, ((0, 0), (row, 1 - row), (col, 1 - col), (0, 0), (0, 0))))
    whole = jnp.concatenate(blocks, axis=-1)
    whole = jnp.concatenate([whole[:, 1:], whole[:, :1]], axis=1)
    return whole.reshape(-1, whole.shape[-1])


def chooser(latent):
    source = jnp.arange(3 * 8 * latent)
    target = jnp.arange(2 * 8 * latent)
    offset, lane = source // (8 * latent), source % (8 * latent)
    side, lane = lane // (4 * latent), lane % (4 * latent)
    row, col, channel = lane // (2 * latent), lane // latent % 2, lane % latent
    cell = 2 * (offset - 1) + col + 1
    to_side, to_lane = target // (8 * latent), target % (8 * latent)
    to_row, to_cell, to_channel = to_lane // (4 * latent), to_lane // latent % 4, to_lane % latent
    same = (
        (side[:, None] == to_side)
        & (row[:, None] == to_row)
        & (cell[:, None] == to_cell)
        & (channel[:, None] == to_channel)
    )
    return same.astype(jnp.bfloat16)


def shards(
    queries, keys, values, stream, head_weight, conv_in_weight, norm_gain, norm_shift, conv_mid_weight
):
    frames, _, cols, width = queries.shape
    n = lax.axis_size("seq")
    members = n // SPLIT
    depth = width // HEADS
    heads = HEADS // SPLIT
    tokens = frames * cols
    group = heads * depth
    latent = head_weight.shape[1] // 4
    wide = 2 * head_weight.shape[1]
    channels = norm_gain.shape[0]
    pairs = (heads + 1) // 2
    index = lax.axis_index("seq").astype(jnp.int32).reshape(1)
    bf16, f32 = jnp.bfloat16, jnp.float32

    prepared = pl.pallas_call(
        functools.partial(prepare_kernel, depth, heads),
        out_shape=[jax.ShapeDtypeStruct((tokens, group + pairs * wide), bf16)] * SPLIT
        + [jax.ShapeDtypeStruct((tokens, group), bf16)] * SPLIT
        + [jax.ShapeDtypeStruct((tokens, wide), f32)],
        in_specs=[SMEM] + [VMEM] * 5,
        out_specs=[VMEM] * (2 * SPLIT + 1),
        scratch_shapes=[pltpu.VMEM((SPLIT, tokens, pairs * wide), bf16)],
        compiler_params=pltpu.CompilerParams(vmem_limit_bytes=16 * 2**20),
        name="prepare",
    )(
        index,
        queries.reshape(tokens, width),
        keys.reshape(tokens, width),
        values.reshape(tokens, width),
        stream.reshape(tokens, width),
        head_weight,
    )
    kv, q, streamed = prepared[:SPLIT], prepared[SPLIT : 2 * SPLIT], prepared[-1]
    kv = [kv[0]] + [exchanged(kv[step], step << 2) for step in range(1, SPLIT)]
    q = [q[0]] + [exchanged(q[step], step << 2) for step in range(1, SPLIT)]
    mine = jnp.concatenate(kv, axis=0)
    blocks = [mine]
    for member in range(1, members):
        if member & 1 == 0 or member == 1:
            blocks.append(exchanged(mine, rest_mask(member)))
        else:
            blocks.append(exchanged(blocks[member - 1], 1))

    part = pl.pallas_call(
        functools.partial(attend_kernel, depth, heads),
        out_shape=jax.ShapeDtypeStruct((SPLIT * tokens // 2, wide), f32),
        in_specs=[VMEM] * (SPLIT + members + 1),
        out_specs=VMEM,
        compiler_params=pltpu.CompilerParams(vmem_limit_bytes=(16 + 2 * members // 4 * 4) * 2**20),
        name="attend",
    )(*q, *blocks, streamed)

    others = [exchanged(part, step << 2) for step in range(1, SPLIT)]
    patch = pl.pallas_call(
        functools.partial(gather_kernel, cols),
        out_shape=jax.ShapeDtypeStruct((part.shape[0], 2 * wide), bf16),
        in_specs=[VMEM] * 5,
        out_specs=VMEM,
        name="gather",
    )(part, *others, chooser(latent))
    patches = [patch] + [exchanged(patch, rest_mask(member)) for member in range(1, members)]

    in_weight = widened(conv_in_weight)
    lane = jnp.arange(channels) // (channels // GROUPS)
    grouped = (lane[:, None] == lane[None, :]).astype(f32)
    return pl.pallas_call(
        functools.partial(finish_kernel, frames, n, cols),
        out_shape=jax.ShapeDtypeStruct((frames, 2, 2 * cols, channels), bf16),
        in_specs=[SMEM] + [VMEM] * members + [VMEM, ANY, VMEM, VMEM, VMEM],
        out_specs=VMEM,
        scratch_shapes=[
            pltpu.VMEM((frames, n + 2, cols, wide), bf16),
            pltpu.VMEM((n * cols, frames * 2 * wide), bf16),
            pltpu.VMEM((frames, n, cols, 4 * channels), f32),
            pltpu.VMEM((frames, 4, 4, cols, channels), bf16),
            pltpu.VMEM(conv_mid_weight.shape, bf16),
            pltpu.VMEM((frames, 2, channels // 128, 2 * cols, 128), f32),
            pltpu.SemaphoreType.DMA((conv_mid_weight.shape[0],)),
        ],
        compiler_params=pltpu.CompilerParams(vmem_limit_bytes=(30 if n <= 16 else 52) * 2**20),
        name="finish",
    )(
        index,
        *patches,
        in_weight,
        conv_mid_weight,
        grouped,
        norm_gain.reshape(1, channels),
        norm_shift.reshape(1, channels),
    )


def solution(mesh):
    placed = (
        P("groups", "seq", None, None),
        P("groups", "seq", None, None),
        P("groups", "seq", None, None),
        P("groups", "seq", None, None),
        P(),
        P(),
        P(),
        P(),
        P(),
    )
    return jax.shard_map(
        shards,
        mesh=mesh,
        in_specs=placed,
        out_specs=P("groups", "seq", None, None),
        check_vma=False,
    )
```

```python
import functools

import jax
import jax.numpy as jnp
from jax import lax
from jax.experimental import pallas as pl
from jax.experimental.pallas import tpu as pltpu
from jax.sharding import PartitionSpec as P

HEADS = 20
GROUPS = 32
SPLIT = 4
EPS = 1e-06

VMEM = pl.BlockSpec(memory_space=pltpu.VMEM)
SMEM = pl.BlockSpec(memory_space=pltpu.SMEM)
HBM = pl.BlockSpec(memory_space=pltpu.HBM)


def exchanged(value, mask):
    pairs = [(source, source ^ mask) for source in range(lax.axis_size("seq"))]
    return lax.ppermute(value, "seq", pairs)


def rest_mask(member):
    return (member & 3) | ((member >> 2) << 4)


def dot(left, right):
    return jnp.dot(left, right, preferred_element_type=jnp.float32)


def prepare_kernel(depth, heads, index, q, k, v, s, w, *refs):
    out, refs = refs[:SPLIT], refs[SPLIT:]
    stream_out, v_here, s_here, w_here, projected, sem = refs
    tokens = q.shape[0]
    group = heads * depth
    place = (index[0] >> 2) & 3
    whole = [
        pltpu.make_async_copy(source, target, sem.at[at])
        for at, (source, target) in enumerate(((v, v_here), (w, w_here), (s, s_here)))
    ]
    parts = []
    for step in range(SPLIT):
        columns = pl.ds(pl.multiple_of((place ^ step) * group, 128), group)
        at = len(whole) + 2 * step
        parts.append(pltpu.make_async_copy(k.at[:, columns], out[step].at[:, :group], sem.at[at]))
        parts.append(pltpu.make_async_copy(q.at[:, columns], out[step].at[:, -group:], sem.at[at + 1]))
    for copy in whole + parts:
        copy.start()
    half = w.shape[0]
    wide = 2 * half
    low = lax.broadcasted_iota(jnp.int32, (tokens, wide), 1) < half

    def through(rows, columns):
        weight = w_here[:, columns]
        return lax.dot_general(
            rows[:, columns],
            jnp.concatenate([weight, weight], axis=0),
            (((1,), (1,)), ((), ())),
            preferred_element_type=jnp.float32,
        )

    def head_through(head):
        return through(v_here, slice(head * depth, (head + 1) * depth))

    whole[0].wait()
    whole[1].wait()
    for owner in range(SPLIT):
        for pair in range((heads + 1) // 2):
            first = owner * heads + 2 * pair
            both = head_through(first)
            if 2 * pair + 1 < heads:
                both = jnp.where(low, both, head_through(first + 1))
            projected[owner, :, pair * wide : (pair + 1) * wide] = both.astype(jnp.bfloat16)
    for step in range(SPLIT):
        out[step][:, group:-group] = projected[place ^ step]
    whole[2].wait()
    stream_out[...] = through(s_here, slice(None))
    for copy in parts:
        copy.wait()


def attend_kernel(depth, heads, last, *refs):
    q, refs = refs[:SPLIT], refs[SPLIT:]
    if last:
        kv, (stream, top_in, total_in, mixed_in, out) = refs[:-5], refs[-5:]
    else:
        kv, (top_out, total_out, mixed_out) = refs[:-3], refs[-3:]
    tokens = q[0].shape[0]
    group = heads * depth
    wide = 128
    factor = 1.4426950408889634 / depth**0.5
    rows = SPLIT * tokens
    low = lax.broadcasted_iota(jnp.int32, (rows, wide), 1) < wide // 2
    summed = jnp.zeros((rows, wide), jnp.float32)
    for head in range(heads):
        columns = slice(head * depth, (head + 1) * depth)
        at = q[0].shape[1] - group + head * depth
        query = jnp.concatenate([piece[:, at : at + depth] for piece in q], axis=0)
        key = jnp.concatenate([piece[:, columns] for piece in kv], axis=0)
        at = group + (head // 2) * wide
        value = jnp.concatenate([piece[:, at : at + wide] for piece in kv], axis=0)
        scores = lax.dot_general(query, key, (((1,), (1,)), ((), ())), preferred_element_type=jnp.float32)
        top = jnp.max(scores, axis=1, keepdims=True)
        if last:
            before = top_in[head]
            top = jnp.maximum(top, before[:, :1])
        expo = jnp.exp2((scores - top) * factor)
        total = jnp.sum(expo, axis=1, keepdims=True)
        mixed = dot(expo.astype(jnp.bfloat16), value)
        if not last:
            top_out[head] = jnp.broadcast_to(top, (rows, wide))
            total_out[head] = jnp.broadcast_to(total, (rows, wide))
            mixed_out[head] = mixed
            continue
        decay = jnp.exp2((before - top) * factor)
        mixed = (mixed + mixed_in[head] * decay) * (1.0 / (total + total_in[head] * decay))
        mine = low if head % 2 == 0 else jnp.logical_not(low)
        summed = summed + jnp.where(mine, mixed, 0.0)
    if not last:
        return
    summed = summed + pltpu.roll(summed, wide // 2, 1)
    half = rows // 2
    upper = summed[:half]
    upper = jnp.concatenate([upper[:tokens] + stream[...], upper[tokens:]], axis=0)
    out[...] = jnp.where(low[:half], upper, summed[half:])


def gather_kernel(own, one, two, three, out):
    rows, wide = own.shape
    half = rows // 2

    def swap_rows(x):
        return jnp.concatenate([x[half:], x[:half]], axis=0)

    far = two[...] + swap_rows(three[...])
    latent = (own[...] + swap_rows(one[...])) + pltpu.roll(far, wide // 2, 1)
    out[...] = latent.astype(jnp.bfloat16)


def finish_kernel(frames, n, cols, index, *refs):
    members = n // SPLIT
    patches, refs = refs[:members], refs[members:]
    (chosen, in_weight, held, grouped, gain, shift, out, grid, stacked, first, taps, merged) = refs
    channels = gain.shape[1]
    wide = grid.shape[-1]
    half = wide // 2
    me = index[0]
    grid[:, 0] = jnp.zeros((frames, cols, wide), jnp.bfloat16)
    grid[:, n + 1] = jnp.zeros((frames, cols, wide), jnp.bfloat16)
    tokens = frames * cols
    for member in range(members):
        latent = patches[member][...].astype(jnp.float32)
        rows = latent.shape[0]
        column = lax.broadcasted_iota(jnp.int32, latent.shape, 0) % cols
        before = jnp.where(column == 0, 0.0, pltpu.roll(latent, 1, 0))
        after = jnp.where(column == cols - 1, 0.0, pltpu.roll(latent, rows - 1, 0))
        around = jnp.concatenate([before, latent, after], axis=1).astype(jnp.bfloat16)
        patch = dot(around, chosen[...]).astype(jnp.bfloat16)
        for step in range(SPLIT):
            row = me ^ (rest_mask(member) | (step << 2))
            at, lanes = (step % 2) * tokens, (step // 2) * wide
            for t in range(frames):
                grid[t, row + 1] = patch[at + t * cols : at + (t + 1) * cols, lanes : lanes + wide]

    cells = n * cols
    chunk = min(cells, 256)
    rows_in = chunk // cols
    upper = lax.broadcasted_iota(jnp.int32, (rows_in, cols, wide), 2) < half
    depth = 2 * wide
    for t in range(frames):
        for r in range(0, n, rows_in):
            near = grid[t, r + 1 : r + 1 + rows_in]
            far = jnp.where(upper, grid[t, r + 2 : r + 2 + rows_in], grid[t, r : r + rows_in])
            stacked[r * cols : r * cols + chunk, t * depth : t * depth + wide] = near.reshape(chunk, wide)
            stacked[r * cols : r * cols + chunk, t * depth + wide : (t + 1) * depth] = far.reshape(chunk, wide)

    sums = jnp.zeros((8, channels), jnp.float32)
    for t in range(frames):
        for r in range(0, n, rows_in):
            for part in range(4):
                lanes = slice(part * channels, (part + 1) * channels)
                here = dot(
                    stacked[r * cols : r * cols + chunk, : (t + 1) * depth],
                    in_weight[(frames - 1 - t) * depth :, lanes],
                )
                first[t, r : r + rows_in, :, lanes] = here.reshape(rows_in, cols, channels)
                sums = sums + jnp.sum(here.reshape(chunk // 8, 8, channels), axis=0)
    counted = 4.0 * frames * cells * (channels // GROUPS)

    def over_group(eight):
        line = jnp.sum(eight, axis=0, keepdims=True)
        return jnp.dot(line, grouped[...], precision=lax.Precision.HIGHEST, preferred_element_type=jnp.float32)

    mean = over_group(sums) / counted
    squares = jnp.zeros((8, channels), jnp.float32)
    for t in range(frames):
        for r in range(0, n, rows_in):
            for part in range(4):
                lanes = slice(part * channels, (part + 1) * channels)
                off = first[t, r : r + rows_in, :, lanes].reshape(chunk, channels) - mean
                squares = squares + jnp.sum((off * off).reshape(chunk // 8, 8, channels), axis=0)
    variance = over_group(squares) / counted
    slope = gain[...] * (1.0 / jnp.sqrt(variance + EPS))
    bias = shift[...]

    place = lax.broadcasted_iota(jnp.int32, (cols, channels), 0)
    for t in range(frames):
        for line in range(4):
            sub = 1 if line in (0, 2) else 0
            token_row = me - 1 if line == 0 else (me + 1 if line == 3 else me)
            inside = jnp.logical_and(token_row >= 0, token_row < n)
            token_row = jnp.clip(token_row, 0, n - 1)
            keep = jnp.where(inside, 1.0, 0.0)
            pair = []
            for side in range(2):
                part = sub * 2 + side
                x = first[t, token_row, :, part * channels : (part + 1) * channels]
                y = (x - mean) * slope + bias
                pair.append(y / (1.0 + jnp.exp(-y)) * keep)
            even, odd = pair
            taps[t, line, 0] = jnp.where(place == 0, 0.0, pltpu.roll(odd, 1, 0)).astype(jnp.bfloat16)
            taps[t, line, 1] = even.astype(jnp.bfloat16)
            taps[t, line, 2] = odd.astype(jnp.bfloat16)
            taps[t, line, 3] = jnp.where(place == cols - 1, 0.0, pltpu.roll(even, cols - 1, 0)).astype(jnp.bfloat16)

    here = 4 * cols
    totals = [jnp.zeros((here, channels), jnp.float32) for _ in range(frames)]
    for a in range(frames):
        valid = a + 1
        for b in range(3):
            left = jnp.concatenate(
                [taps[:valid, b : b + 2, w : w + 2].reshape(valid * here, channels) for w in range(3)], axis=1
            )
            got = dot(left, held[a, b].reshape(3 * channels, channels))
            for t in range(valid):
                totals[frames - 1 - a + t] = totals[frames - 1 - a + t] + got[t * here : (t + 1) * here]
    for t in range(frames):
        for part in range(4):
            kept = first[t, me, :, part * channels : (part + 1) * channels]
            block = totals[t][part * cols : (part + 1) * cols] + kept
            for lane in range(channels // 128):
                tile = block[:, lane * 128 : (lane + 1) * 128]
                merged[t, part // 2, lane, pl.ds(part % 2, cols, stride=2), :] = tile
    for t in range(frames):
        for sub in range(2):
            for lane in range(channels // 128):
                out[t, sub, :, lane * 128 : (lane + 1) * 128] = merged[t, sub, lane].astype(jnp.bfloat16)


def widened(weight):
    blocks = []
    for row in range(2):
        for col in range(2):
            blocks.append(jnp.pad(weight, ((0, 0), (row, 1 - row), (col, 1 - col), (0, 0), (0, 0))))
    whole = jnp.concatenate(blocks, axis=-1)
    whole = jnp.concatenate([whole[:, 1:], whole[:, :1]], axis=1)
    return whole.reshape(-1, whole.shape[-1])


def chooser(latent):
    source = jnp.arange(3 * 8 * latent)
    target = jnp.arange(2 * 8 * latent)
    offset, lane = source // (8 * latent), source % (8 * latent)
    side, lane = lane // (4 * latent), lane % (4 * latent)
    row, col, channel = lane // (2 * latent), lane // latent % 2, lane % latent
    cell = 2 * (offset - 1) + col + 1
    to_side, to_lane = target // (8 * latent), target % (8 * latent)
    to_row, to_cell, to_channel = to_lane // (4 * latent), to_lane // latent % 4, to_lane % latent
    same = (
        (side[:, None] == to_side)
        & (row[:, None] == to_row)
        & (cell[:, None] == to_cell)
        & (channel[:, None] == to_channel)
    )
    return same.astype(jnp.bfloat16)


def shards(
    queries, keys, values, stream, head_weight, conv_in_weight, norm_gain, norm_shift, conv_mid_weight
):
    frames, _, cols, width = queries.shape
    n = lax.axis_size("seq")
    members = n // SPLIT
    depth = width // HEADS
    heads = HEADS // SPLIT
    tokens = frames * cols
    group = heads * depth
    latent = head_weight.shape[1] // 4
    wide = 2 * head_weight.shape[1]
    channels = norm_gain.shape[0]
    pairs = (heads + 1) // 2
    index = lax.axis_index("seq").astype(jnp.int32).reshape(1)
    bf16, f32 = jnp.bfloat16, jnp.float32

    prepared = pl.pallas_call(
        functools.partial(prepare_kernel, depth, heads),
        out_shape=[jax.ShapeDtypeStruct((tokens, 2 * group + pairs * wide), bf16)] * SPLIT
        + [jax.ShapeDtypeStruct((tokens, wide), f32)],
        in_specs=[SMEM] + [HBM] * 5,
        out_specs=[VMEM] * (SPLIT + 1),
        scratch_shapes=[
            pltpu.VMEM((tokens, width), bf16),
            pltpu.VMEM((tokens, width), bf16),
            pltpu.VMEM((wide // 2, width), bf16),
            pltpu.VMEM((SPLIT, tokens, pairs * wide), bf16),
            pltpu.SemaphoreType.DMA((3 + 2 * SPLIT,)),
        ],
        compiler_params=pltpu.CompilerParams(vmem_limit_bytes=int(53.2 * 2**20)),
        name="prepare",
    )(
        index,
        queries.reshape(tokens, width),
        keys.reshape(tokens, width),
        values.reshape(tokens, width),
        stream.reshape(tokens, width),
        head_weight.T,
    )
    mine, streamed = prepared[:SPLIT], prepared[-1]
    mine = [mine[0]] + [exchanged(mine[step], step << 2) for step in range(1, SPLIT)]

    def spread(pieces):
        blocks = [jnp.concatenate([piece[:, :-group] for piece in pieces], axis=0)]
        for member in range(1, members):
            if member & 1 == 0 or member == 1:
                blocks.append(exchanged(blocks[0], rest_mask(member)))
            else:
                blocks.append(exchanged(blocks[member - 1], 1))
        return blocks

    near, far = spread(mine[:2]), spread(mine[2:])
    limit = pltpu.CompilerParams(vmem_limit_bytes=(12 + 2 * members // 4 * 4) * 2**20)
    state = jax.ShapeDtypeStruct((heads, SPLIT * tokens, wide), f32)
    carried = pl.pallas_call(
        functools.partial(attend_kernel, depth, heads, False),
        out_shape=[state] * 3,
        in_specs=[VMEM] * (SPLIT + members),
        out_specs=[VMEM] * 3,
        compiler_params=limit,
        name="attend_near",
    )(*mine, *near)
    part = pl.pallas_call(
        functools.partial(attend_kernel, depth, heads, True),
        out_shape=jax.ShapeDtypeStruct((SPLIT * tokens // 2, wide), f32),
        in_specs=[VMEM] * (SPLIT + members + 4),
        out_specs=VMEM,
        compiler_params=limit,
        name="attend_far",
    )(*mine, *far, streamed, *carried)

    others = [exchanged(part, step << 2) for step in range(1, SPLIT)]
    patch = pl.pallas_call(
        gather_kernel,
        out_shape=jax.ShapeDtypeStruct(part.shape, bf16),
        in_specs=[VMEM] * 4,
        out_specs=VMEM,
        compiler_params=pltpu.CompilerParams(vmem_limit_bytes=4 * 2**20),
        name="gather",
    )(part, *others)
    patches = [patch] + [exchanged(patch, rest_mask(member)) for member in range(1, members)]

    in_weight = widened(conv_in_weight)
    lane = jnp.arange(channels) // (channels // GROUPS)
    grouped = (lane[:, None] == lane[None, :]).astype(f32)
    return pl.pallas_call(
        functools.partial(finish_kernel, frames, n, cols),
        out_shape=jax.ShapeDtypeStruct((frames, 2, 2 * cols, channels), bf16),
        in_specs=[SMEM] + [VMEM] * (members + 6),
        out_specs=VMEM,
        scratch_shapes=[
            pltpu.VMEM((frames, n + 2, cols, wide), bf16),
            pltpu.VMEM((n * cols, frames * 2 * wide), bf16),
            pltpu.VMEM((frames, n, cols, 4 * channels), f32),
            pltpu.VMEM((frames, 4, 4, cols, channels), bf16),
            pltpu.VMEM((frames, 2, channels // 128, 2 * cols, 128), f32),
        ],
        compiler_params=pltpu.CompilerParams(vmem_limit_bytes=(16 if n <= 16 else 40) * 2**20),
        name="finish",
    )(
        index,
        *patches,
        chooser(latent),
        in_weight,
        conv_mid_weight,
        grouped,
        norm_gain.reshape(1, channels),
        norm_shift.reshape(1, channels),
    )


def solution(mesh):
    placed = (
        P("groups", "seq", None, None),
        P("groups", "seq", None, None),
        P("groups", "seq", None, None),
        P("groups", "seq", None, None),
        P(),
        P(),
        P(),
        P(),
        P(),
    )
    return jax.shard_map(
        shards,
        mesh=mesh,
        in_specs=placed,
        out_specs=P("groups", "seq", None, None),
        check_vma=False,
    )
```

```python
import functools

import jax
import jax.numpy as jnp
from jax import lax
from jax.experimental import pallas as pl
from jax.experimental.pallas import tpu as pltpu
from jax.sharding import PartitionSpec as P

HEADS = 20
GROUPS = 32
SPLIT = 4
EPS = 1e-06

VMEM = pl.BlockSpec(memory_space=pltpu.VMEM)
SMEM = pl.BlockSpec(memory_space=pltpu.SMEM)
HBM = pl.BlockSpec(memory_space=pltpu.HBM)


def exchanged(value, mask):
    pairs = [(source, source ^ mask) for source in range(lax.axis_size("seq"))]
    return lax.ppermute(value, "seq", pairs)


def rest_mask(member):
    return (member & 3) | ((member >> 2) << 4)


def dot(left, right):
    return jnp.dot(left, right, preferred_element_type=jnp.float32)


def through_twice(rows, weight, columns):
    part = weight[:, columns]
    return lax.dot_general(
        rows[:, columns],
        jnp.concatenate([part, part], axis=0),
        (((1,), (1,)), ((), ())),
        preferred_element_type=jnp.float32,
    )


def prepare_kernel(depth, heads, index, q, k, v, w, *refs):
    kv_out, q_out, refs = refs[:SPLIT], refs[SPLIT : 2 * SPLIT], refs[2 * SPLIT :]
    v_here, w_here, projected, sem = refs
    tokens = q.shape[0]
    group = heads * depth
    place = (index[0] >> 2) & 3
    whole = [
        pltpu.make_async_copy(source, target, sem.at[at])
        for at, (source, target) in enumerate(((v, v_here), (w, w_here)))
    ]
    parts = []
    for step in range(SPLIT):
        columns = pl.ds(pl.multiple_of((place ^ step) * group, 128), group)
        at = len(whole) + 2 * step
        parts.append(pltpu.make_async_copy(k.at[:, columns], kv_out[step].at[:, :group], sem.at[at]))
        parts.append(pltpu.make_async_copy(q.at[:, columns], q_out[step], sem.at[at + 1]))
    for copy in whole + parts:
        copy.start()
    half = w.shape[0]
    wide = 2 * half
    low = lax.broadcasted_iota(jnp.int32, (tokens, wide), 1) < half

    def head_through(head):
        return through_twice(v_here, w_here, slice(head * depth, (head + 1) * depth))

    for copy in whole:
        copy.wait()
    for owner in range(SPLIT):
        for pair in range((heads + 1) // 2):
            first = owner * heads + 2 * pair
            both = head_through(first)
            if 2 * pair + 1 < heads:
                both = jnp.where(low, both, head_through(first + 1))
            projected[owner, :, pair * wide : (pair + 1) * wide] = both.astype(jnp.bfloat16)
    for step in range(SPLIT):
        kv_out[step][:, group:] = projected[place ^ step]
    for copy in parts:
        copy.wait()


def stream_kernel(s, w, out):
    out[...] = through_twice(s, w, slice(None))


def attend_kernel(depth, heads, last, *refs):
    q, refs = refs[:SPLIT], refs[SPLIT:]
    if last:
        kv, (stream, top_in, mixed_in, out) = refs[:-4], refs[-4:]
    else:
        kv, (top_out, mixed_out) = refs[:-2], refs[-2:]
    tokens = q[0].shape[0]
    group = heads * depth
    wide = 128
    factor = 1.4426950408889634 / depth**0.5
    rows = SPLIT * tokens
    half = rows // 2
    low = lax.broadcasted_iota(jnp.int32, (rows, wide), 1) < wide // 2
    keys = sum(piece.shape[0] for piece in kv)
    ones = jnp.ones((keys, wide), jnp.bfloat16)

    def scores_of(head):
        columns = slice(head * depth, (head + 1) * depth)
        at = q[0].shape[1] - group + head * depth
        query = jnp.concatenate([piece[:, at : at + depth] for piece in q], axis=0)
        key = jnp.concatenate([piece[:, columns] for piece in kv], axis=0)
        return lax.dot_general(query, key, (((1,), (1,)), ((), ())), preferred_element_type=jnp.float32)

    summed = jnp.zeros((rows, wide), jnp.float32)
    upcoming = scores_of(0)
    for head in range(heads):
        scores = upcoming
        if head + 1 < heads:
            upcoming = scores_of(head + 1)
        top = jnp.broadcast_to(jnp.max(scores, axis=1, keepdims=True), (rows, wide))
        if last:
            before = top_in[head]
            top = jnp.maximum(top, before)
        expo = jnp.concatenate(
            [
                jnp.exp2((scores[:, at : at + wide] - top) * factor).astype(jnp.bfloat16)
                for at in range(0, keys, wide)
            ],
            axis=1,
        )
        at = group + (head // 2) * wide
        value = jnp.concatenate([piece[:, at : at + wide] for piece in kv], axis=0)
        mixed = dot(expo, jnp.concatenate([value, ones], axis=1))
        if not last:
            top_out[head] = top
            mixed_out[head] = mixed
            continue
        decay = jnp.exp2((before - top) * factor)
        weighed = mixed[:, :wide] + mixed_in[head, :, :wide] * decay
        total = mixed[:, wide:] + mixed_in[head, :, wide:] * decay
        mine = low if head % 2 == 0 else jnp.logical_not(low)
        summed = summed + jnp.where(mine, weighed / total, 0.0)
    if not last:
        return
    summed = summed + pltpu.roll(summed, wide // 2, 1)
    upper = summed[:half]
    upper = jnp.concatenate([upper[:tokens] + stream[...], upper[tokens:]], axis=0)
    out[...] = jnp.where(low[:half], upper, summed[half:]).astype(out.dtype)


def gather_kernel(own, one, two, three, out):
    rows, wide = own.shape
    half = rows // 2

    def swap_rows(x):
        return jnp.concatenate([x[half:], x[:half]], axis=0)

    own, one, two, three = (ref[...].astype(jnp.float32) for ref in (own, one, two, three))
    far = two + swap_rows(three)
    latent = (own + swap_rows(one)) + pltpu.roll(far, wide // 2, 1)
    out[...] = latent.astype(jnp.bfloat16)


def finish_kernel(frames, n, cols, index, *refs):
    members = n // SPLIT
    patches, refs = refs[:members], refs[members:]
    (chosen, in_weight, held, grouped, gain, shift, out, grid, stacked, first, taps, merged) = refs
    channels = gain.shape[1]
    wide = grid.shape[-1]
    half = wide // 2
    me = index[0]
    grid[:, 0] = jnp.zeros((frames, cols, wide), jnp.bfloat16)
    grid[:, n + 1] = jnp.zeros((frames, cols, wide), jnp.bfloat16)
    tokens = frames * cols
    for member in range(members):
        latent = patches[member][...].astype(jnp.float32)
        rows = latent.shape[0]
        column = lax.broadcasted_iota(jnp.int32, latent.shape, 0) % cols
        before = jnp.where(column == 0, 0.0, pltpu.roll(latent, 1, 0))
        after = jnp.where(column == cols - 1, 0.0, pltpu.roll(latent, rows - 1, 0))
        around = jnp.concatenate([before, latent, after], axis=1).astype(jnp.bfloat16)
        patch = dot(around, chosen[...]).astype(jnp.bfloat16)
        for step in range(SPLIT):
            row = me ^ (rest_mask(member) | (step << 2))
            at, lanes = (step % 2) * tokens, (step // 2) * wide
            for t in range(frames):
                grid[t, row + 1] = patch[at + t * cols : at + (t + 1) * cols, lanes : lanes + wide]

    cells = n * cols
    chunk = min(cells, 256)
    rows_in = chunk // cols
    upper = lax.broadcasted_iota(jnp.int32, (rows_in, cols, wide), 2) < half
    depth = 2 * wide
    for t in range(frames):
        for r in range(0, n, rows_in):
            near = grid[t, r + 1 : r + 1 + rows_in]
            far = jnp.where(upper, grid[t, r + 2 : r + 2 + rows_in], grid[t, r : r + rows_in])
            stacked[r * cols : r * cols + chunk, t * depth : t * depth + wide] = near.reshape(chunk, wide)
            stacked[r * cols : r * cols + chunk, t * depth + wide : (t + 1) * depth] = far.reshape(chunk, wide)

    counted = 4.0 * frames * cells
    members_of = channels // GROUPS
    sums = jnp.zeros((8, channels), jnp.float32)
    squares = jnp.zeros((8, channels), jnp.float32)
    pivot = None
    for t in range(frames):
        for r in range(0, n, rows_in):
            for part in range(4):
                lanes = slice(part * channels, (part + 1) * channels)
                here = dot(
                    stacked[r * cols : r * cols + chunk, : (t + 1) * depth],
                    in_weight[(frames - 1 - t) * depth :, lanes],
                )
                first[t, r : r + rows_in, :, lanes] = here.reshape(rows_in, cols, channels)
                if pivot is None:
                    pivot = jnp.sum(here, axis=0, keepdims=True) / chunk
                off = (here - pivot).reshape(chunk // 8, 8, channels)
                sums = sums + jnp.sum(off, axis=0)
                squares = squares + jnp.sum(off * off, axis=0)

    def over_group(line):
        high = line.astype(jnp.bfloat16)
        rest = line - high.astype(jnp.float32)
        middle = rest.astype(jnp.bfloat16)
        lower = (rest - middle.astype(jnp.float32)).astype(jnp.bfloat16)
        none = jnp.zeros((13, channels), jnp.bfloat16)
        terms = jnp.concatenate([high, middle, lower, none], axis=0)
        return jnp.sum(dot(terms, grouped[...])[:8], axis=0, keepdims=True)

    offset = jnp.sum(sums, axis=0, keepdims=True) / counted
    channel_mean = pivot + offset
    mean = over_group(channel_mean) / members_of
    apart = channel_mean - mean
    within = jnp.sum(squares, axis=0, keepdims=True) / counted - offset * offset
    variance = over_group(within + apart * apart) / members_of
    slope = gain[...] / jnp.sqrt(variance + EPS)
    bias = shift[...]

    place = lax.broadcasted_iota(jnp.int32, (cols, channels), 0)
    for t in range(frames):
        for line in range(4):
            sub = 1 if line in (0, 2) else 0
            token_row = me - 1 if line == 0 else (me + 1 if line == 3 else me)
            inside = jnp.logical_and(token_row >= 0, token_row < n)
            token_row = jnp.clip(token_row, 0, n - 1)
            keep = jnp.where(inside, 0.5, 0.0)
            pair = []
            for side in range(2):
                part = sub * 2 + side
                x = first[t, token_row, :, part * channels : (part + 1) * channels]
                y = (x - mean) * slope + bias
                pair.append((y * keep) * (1.0 + jnp.tanh(0.5 * y)))
            even, odd = pair
            taps[t, line, 0] = jnp.where(place == 0, 0.0, pltpu.roll(odd, 1, 0)).astype(jnp.bfloat16)
            taps[t, line, 1] = even.astype(jnp.bfloat16)
            taps[t, line, 2] = odd.astype(jnp.bfloat16)
            taps[t, line, 3] = jnp.where(place == cols - 1, 0.0, pltpu.roll(even, cols - 1, 0)).astype(jnp.bfloat16)

    here = 4 * cols
    totals = [jnp.zeros((here, channels), jnp.float32) for _ in range(frames)]
    for a in range(frames):
        valid = a + 1
        for b in range(3):
            left = jnp.concatenate(
                [taps[:valid, b : b + 2, w : w + 2].reshape(valid * here, channels) for w in range(3)], axis=1
            )
            got = dot(left, held[a, b].reshape(3 * channels, channels))
            for t in range(valid):
                totals[frames - 1 - a + t] = totals[frames - 1 - a + t] + got[t * here : (t + 1) * here]
    for t in range(frames):
        for part in range(4):
            kept = first[t, me, :, part * channels : (part + 1) * channels]
            block = totals[t][part * cols : (part + 1) * cols] + kept
            for lane in range(channels // 128):
                tile = block[:, lane * 128 : (lane + 1) * 128]
                merged[t, part // 2, lane, pl.ds(part % 2, cols, stride=2), :] = tile
    for t in range(frames):
        for sub in range(2):
            for lane in range(channels // 128):
                out[t, sub, :, lane * 128 : (lane + 1) * 128] = merged[t, sub, lane].astype(jnp.bfloat16)


def widened(weight):
    blocks = []
    for row in range(2):
        for col in range(2):
            blocks.append(jnp.pad(weight, ((0, 0), (row, 1 - row), (col, 1 - col), (0, 0), (0, 0))))
    whole = jnp.concatenate(blocks, axis=-1)
    whole = jnp.concatenate([whole[:, 1:], whole[:, :1]], axis=1)
    return whole.reshape(-1, whole.shape[-1])


def chooser(latent):
    source = jnp.arange(3 * 8 * latent)
    target = jnp.arange(2 * 8 * latent)
    offset, lane = source // (8 * latent), source % (8 * latent)
    side, lane = lane // (4 * latent), lane % (4 * latent)
    row, col, channel = lane // (2 * latent), lane // latent % 2, lane % latent
    cell = 2 * (offset - 1) + col + 1
    to_side, to_lane = target // (8 * latent), target % (8 * latent)
    to_row, to_cell, to_channel = to_lane // (4 * latent), to_lane // latent % 4, to_lane % latent
    same = (
        (side[:, None] == to_side)
        & (row[:, None] == to_row)
        & (cell[:, None] == to_cell)
        & (channel[:, None] == to_channel)
    )
    return same.astype(jnp.bfloat16)


def shards(
    queries, keys, values, stream, head_weight, conv_in_weight, norm_gain, norm_shift, conv_mid_weight
):
    frames, _, cols, width = queries.shape
    n = lax.axis_size("seq")
    members = n // SPLIT
    depth = width // HEADS
    heads = HEADS // SPLIT
    tokens = frames * cols
    group = heads * depth
    latent = head_weight.shape[1] // 4
    wide = 2 * head_weight.shape[1]
    channels = norm_gain.shape[0]
    pairs = (heads + 1) // 2
    index = lax.axis_index("seq").astype(jnp.int32).reshape(1)
    bf16, f32 = jnp.bfloat16, jnp.float32

    head_lanes = head_weight.T
    prepared = pl.pallas_call(
        functools.partial(prepare_kernel, depth, heads),
        out_shape=[jax.ShapeDtypeStruct((tokens, group + pairs * wide), bf16)] * SPLIT
        + [jax.ShapeDtypeStruct((tokens, group), bf16)] * SPLIT,
        in_specs=[SMEM] + [HBM] * 4,
        out_specs=[VMEM] * (2 * SPLIT),
        scratch_shapes=[
            pltpu.VMEM((tokens, width), bf16),
            pltpu.VMEM((wide // 2, width), bf16),
            pltpu.VMEM((SPLIT, tokens, pairs * wide), bf16),
            pltpu.SemaphoreType.DMA((2 + 2 * SPLIT,)),
        ],
        compiler_params=pltpu.CompilerParams(vmem_limit_bytes=int(53.2 * 2**20)),
        name="prepare",
    )(
        index,
        queries.reshape(tokens, width),
        keys.reshape(tokens, width),
        values.reshape(tokens, width),
        head_lanes,
    )
    streamed = pl.pallas_call(
        stream_kernel,
        out_shape=jax.ShapeDtypeStruct((tokens, wide), f32),
        in_specs=[VMEM] * 2,
        out_specs=VMEM,
        compiler_params=pltpu.CompilerParams(vmem_limit_bytes=4 * 2**20),
        cost_estimate=pl.CostEstimate(flops=2 * 10**8, bytes_accessed=10**6, transcendentals=0),
        name="stream",
    )(stream.reshape(tokens, width), head_lanes)
    kv, q = prepared[:SPLIT], prepared[SPLIT:]
    kv = [kv[0]] + [exchanged(kv[step], step << 2) for step in range(1, SPLIT)]
    pass
    q = [q[0]] + [exchanged(q[step], step << 2) for step in range(1, SPLIT)]

    def spread(pieces):
        blocks = [jnp.concatenate(pieces, axis=0)]
        for member in range(1, members):
            if member & 1 == 0 or member == 1:
                blocks.append(exchanged(blocks[0], rest_mask(member)))
            else:
                blocks.append(exchanged(blocks[member - 1], 1))
        return blocks

    near = spread(kv[:2])
    far = spread(kv[2:])
    limit = pltpu.CompilerParams(vmem_limit_bytes=(12 + 2 * members // 4 * 4) * 2**20)
    state = [jax.ShapeDtypeStruct((heads, SPLIT * tokens, size), f32) for size in (wide, 2 * wide)]
    carried = pl.pallas_call(
        functools.partial(attend_kernel, depth, heads, False),
        out_shape=state,
        in_specs=[VMEM] * (SPLIT + members),
        out_specs=[VMEM] * 2,
        compiler_params=limit,
        cost_estimate=pl.CostEstimate(flops=10**9, bytes_accessed=4 * 10**6, transcendentals=4 * 10**5),
        name="attend_near",
    )(*q, *near)
    part = pl.pallas_call(
        functools.partial(attend_kernel, depth, heads, True),
        out_shape=jax.ShapeDtypeStruct((SPLIT * tokens // 2, wide), bf16),
        in_specs=[VMEM] * (SPLIT + members + 3),
        out_specs=VMEM,
        compiler_params=limit,
        name="attend_far",
    )(*q, *far, streamed, *carried)

    others = [exchanged(part, step << 2) for step in range(1, SPLIT)]
    patch = pl.pallas_call(
        gather_kernel,
        out_shape=jax.ShapeDtypeStruct(part.shape, bf16),
        in_specs=[VMEM] * 4,
        out_specs=VMEM,
        compiler_params=pltpu.CompilerParams(vmem_limit_bytes=4 * 2**20),
        name="gather",
    )(part, *others)
    patches = [patch] + [exchanged(patch, rest_mask(member)) for member in range(1, members)]

    lane = jnp.arange(channels) // (channels // GROUPS)
    in_weight = widened(conv_in_weight)
    grouped = (lane[:, None] == lane[None, :]).astype(bf16)
    return pl.pallas_call(
        functools.partial(finish_kernel, frames, n, cols),
        out_shape=jax.ShapeDtypeStruct((frames, 2, 2 * cols, channels), bf16),
        in_specs=[SMEM] + [VMEM] * (members + 6),
        out_specs=VMEM,
        scratch_shapes=[
            pltpu.VMEM((frames, n + 2, cols, wide), bf16),
            pltpu.VMEM((n * cols, frames * 2 * wide), bf16),
            pltpu.VMEM((frames, n, cols, 4 * channels), f32),
            pltpu.VMEM((frames, 4, 4, cols, channels), bf16),
            pltpu.VMEM((frames, 2, channels // 128, 2 * cols, 128), f32),
        ],
        compiler_params=pltpu.CompilerParams(vmem_limit_bytes=(16 if n <= 16 else 40) * 2**20),
        name="finish",
    )(
        index,
        *patches,
        chooser(latent),
        in_weight,
        conv_mid_weight,
        grouped,
        norm_gain.reshape(1, channels),
        norm_shift.reshape(1, channels),
    )


def solution(mesh):
    placed = (
        P("groups", "seq", None, None),
        P("groups", "seq", None, None),
        P("groups", "seq", None, None),
        P("groups", "seq", None, None),
        P(),
        P(),
        P(),
        P(),
        P(),
    )
    return jax.shard_map(
        shards,
        mesh=mesh,
        in_specs=placed,
        out_specs=P("groups", "seq", None, None),
        check_vma=False,
    )
```

```python
import functools

import jax
import jax.numpy as jnp
from jax import lax
from jax.experimental import pallas as pl
from jax.experimental.pallas import tpu as pltpu
from jax.sharding import PartitionSpec as P

HEADS = 20
GROUPS = 32
SPLIT = 4
EPS = 1e-06

VMEM = pl.BlockSpec(memory_space=pltpu.VMEM)
SMEM = pl.BlockSpec(memory_space=pltpu.SMEM)
HBM = pl.BlockSpec(memory_space=pltpu.HBM)


def exchanged(value, mask):
    pairs = [(source, source ^ mask) for source in range(lax.axis_size("seq"))]
    return lax.ppermute(value, "seq", pairs)


def rest_mask(member):
    return (member & 3) | ((member >> 2) << 4)


def dot(left, right):
    return jnp.dot(left, right, preferred_element_type=jnp.float32)


def through_twice(rows, weight, columns):
    part = weight[:, columns]
    return lax.dot_general(
        rows[:, columns],
        jnp.concatenate([part, part], axis=0),
        (((1,), (1,)), ((), ())),
        preferred_element_type=jnp.float32,
    )


def prepare_kernel(depth, heads, index, q, k, v, w, *refs):
    kv_out, q_out, refs = refs[:SPLIT], refs[SPLIT : 2 * SPLIT], refs[2 * SPLIT :]
    v_here, w_here, projected, sem = refs
    tokens = q.shape[0]
    group = heads * depth
    place = (index[0] >> 2) & 3
    whole = [
        pltpu.make_async_copy(source, target, sem.at[at])
        for at, (source, target) in enumerate(((v, v_here), (w, w_here)))
    ]
    parts = []
    for step in range(SPLIT):
        columns = pl.ds(pl.multiple_of((place ^ step) * group, 128), group)
        at = len(whole) + 2 * step
        parts.append(pltpu.make_async_copy(k.at[:, columns], kv_out[step].at[:, :group], sem.at[at]))
        parts.append(pltpu.make_async_copy(q.at[:, columns], q_out[step], sem.at[at + 1]))
    for copy in whole + parts:
        copy.start()
    half = w.shape[0]
    wide = 2 * half
    low = lax.broadcasted_iota(jnp.int32, (tokens, wide), 1) < half

    def head_through(head):
        return through_twice(v_here, w_here, slice(head * depth, (head + 1) * depth))

    for copy in whole:
        copy.wait()
    for owner in range(SPLIT):
        for pair in range((heads + 1) // 2):
            first = owner * heads + 2 * pair
            both = head_through(first)
            if 2 * pair + 1 < heads:
                both = jnp.where(low, both, head_through(first + 1))
            projected[owner, :, pair * wide : (pair + 1) * wide] = both.astype(jnp.bfloat16)
    for step in range(SPLIT):
        kv_out[step][:, group:] = projected[place ^ step]
    for copy in parts:
        copy.wait()


def stream_kernel(s, w, out):
    out[...] = through_twice(s, w, slice(None))


def attend_kernel(depth, heads, last, *refs):
    q, refs = refs[0], refs[1:]
    if last:
        kv, (stream, top_in, mixed_in, out) = refs[:-4], refs[-4:]
    else:
        kv, (top_out, mixed_out) = refs[:-2], refs[-2:]
    group = heads * depth
    wide = 128
    factor = 1.4426950408889634 / depth**0.5
    rows = q.shape[0]
    tokens = rows // SPLIT
    half = rows // 2
    low = lax.broadcasted_iota(jnp.int32, (rows, wide), 1) < wide // 2
    keys = sum(piece.shape[0] for piece in kv)
    ones = jnp.ones((keys, wide), jnp.bfloat16)

    def scores_of(head):
        columns = slice(head * depth, (head + 1) * depth)
        query = q[:, columns]
        key = jnp.concatenate([piece[:, columns] for piece in kv], axis=0)
        return lax.dot_general(query, key, (((1,), (1,)), ((), ())), preferred_element_type=jnp.float32)

    summed = jnp.zeros((rows, wide), jnp.float32)
    upcoming = scores_of(0)
    for head in range(heads):
        scores = upcoming
        if head + 1 < heads:
            upcoming = scores_of(head + 1)
        top = jnp.broadcast_to(jnp.max(scores, axis=1, keepdims=True), (rows, wide))
        if last:
            before = top_in[head]
            top = jnp.maximum(top, before)
        expo = jnp.concatenate(
            [
                jnp.exp2((scores[:, at : at + wide] - top) * factor).astype(jnp.bfloat16)
                for at in range(0, keys, wide)
            ],
            axis=1,
        )
        at = group + (head // 2) * wide
        value = jnp.concatenate([piece[:, at : at + wide] for piece in kv], axis=0)
        mixed = dot(expo, jnp.concatenate([value, ones], axis=1))
        if not last:
            top_out[head] = top
            mixed_out[head] = mixed
            continue
        decay = jnp.exp2((before - top) * factor)
        weighed = mixed[:, :wide] + mixed_in[head, :, :wide] * decay
        total = mixed[:, wide:] + mixed_in[head, :, wide:] * decay
        mine = low if head % 2 == 0 else jnp.logical_not(low)
        summed = summed + jnp.where(mine, weighed / total, 0.0)
    if not last:
        return
    summed = summed + pltpu.roll(summed, wide // 2, 1)
    upper = summed[:half]
    upper = jnp.concatenate([upper[:tokens] + stream[...], upper[tokens:]], axis=0)
    out[...] = jnp.where(low[:half], upper, summed[half:]).astype(out.dtype)


def collect_kernel(*refs):
    pieces, out = refs[:-1], refs[-1]
    tokens = pieces[0].shape[0]
    for at, piece in enumerate(pieces):
        out[at * tokens : (at + 1) * tokens, :] = piece[...]


def gather_kernel(own, three, two, one, out):
    rows, wide = own.shape
    half = rows // 2

    def swap_rows(x):
        return jnp.concatenate([x[half:], x[:half]], axis=0)

    own, one, two, three = (ref[...].astype(jnp.float32) for ref in (own, one, two, three))
    far = two + swap_rows(three)
    latent = (own + swap_rows(one)) + pltpu.roll(far, wide // 2, 1)
    out[...] = latent.astype(jnp.bfloat16)


def finish_kernel(frames, n, cols, index, *refs):
    members = n // SPLIT
    patches, refs = refs[:members], refs[members:]
    (chosen, in_weight, held, grouped, gain, shift, out, grid, stacked, first, taps, merged) = refs
    channels = gain.shape[1]
    wide = grid.shape[-1]
    half = wide // 2
    me = index[0]
    grid[:, 0] = jnp.zeros((frames, cols, wide), jnp.bfloat16)
    grid[:, n + 1] = jnp.zeros((frames, cols, wide), jnp.bfloat16)
    tokens = frames * cols
    for member in range(members):
        latent = patches[member][...].astype(jnp.float32)
        rows = latent.shape[0]
        column = lax.broadcasted_iota(jnp.int32, latent.shape, 0) % cols
        before = jnp.where(column == 0, 0.0, pltpu.roll(latent, 1, 0))
        after = jnp.where(column == cols - 1, 0.0, pltpu.roll(latent, rows - 1, 0))
        around = jnp.concatenate([before, latent, after], axis=1).astype(jnp.bfloat16)
        patch = dot(around, chosen[...]).astype(jnp.bfloat16)
        for step in range(SPLIT):
            row = me ^ (rest_mask(member) | (step << 2))
            at, lanes = (step % 2) * tokens, (step // 2) * wide
            for t in range(frames):
                grid[t, row + 1] = patch[at + t * cols : at + (t + 1) * cols, lanes : lanes + wide]

    cells = n * cols
    chunk = min(cells, 256)
    rows_in = chunk // cols
    upper = lax.broadcasted_iota(jnp.int32, (rows_in, cols, wide), 2) < half
    depth = 2 * wide
    for t in range(frames):
        for r in range(0, n, rows_in):
            near = grid[t, r + 1 : r + 1 + rows_in]
            far = jnp.where(upper, grid[t, r + 2 : r + 2 + rows_in], grid[t, r : r + rows_in])
            stacked[r * cols : r * cols + chunk, t * depth : t * depth + wide] = near.reshape(chunk, wide)
            stacked[r * cols : r * cols + chunk, t * depth + wide : (t + 1) * depth] = far.reshape(chunk, wide)

    counted = 4.0 * frames * cells
    members_of = channels // GROUPS
    sums = jnp.zeros((8, channels), jnp.float32)
    squares = jnp.zeros((8, channels), jnp.float32)
    pivot = None
    for t in range(frames):
        for r in range(0, n, rows_in):
            for part in range(4):
                lanes = slice(part * channels, (part + 1) * channels)
                here = dot(
                    stacked[r * cols : r * cols + chunk, : (t + 1) * depth],
                    in_weight[(frames - 1 - t) * depth :, lanes],
                )
                first[t, r : r + rows_in, :, lanes] = here.reshape(rows_in, cols, channels)
                if pivot is None:
                    pivot = jnp.sum(here, axis=0, keepdims=True) / chunk
                off = (here - pivot).reshape(chunk // 8, 8, channels)
                sums = sums + jnp.sum(off, axis=0)
                squares = squares + jnp.sum(off * off, axis=0)

    def over_group(line):
        high = line.astype(jnp.bfloat16)
        rest = line - high.astype(jnp.float32)
        middle = rest.astype(jnp.bfloat16)
        lower = (rest - middle.astype(jnp.float32)).astype(jnp.bfloat16)
        none = jnp.zeros((13, channels), jnp.bfloat16)
        terms = jnp.concatenate([high, middle, lower, none], axis=0)
        return jnp.sum(dot(terms, grouped[...])[:8], axis=0, keepdims=True)

    offset = jnp.sum(sums, axis=0, keepdims=True) / counted
    channel_mean = pivot + offset
    mean = over_group(channel_mean) / members_of
    apart = channel_mean - mean
    within = jnp.sum(squares, axis=0, keepdims=True) / counted - offset * offset
    variance = over_group(within + apart * apart) / members_of
    slope = gain[...] / jnp.sqrt(variance + EPS)
    bias = shift[...]

    place = lax.broadcasted_iota(jnp.int32, (cols, channels), 0)
    for t in range(frames):
        for line in range(4):
            sub = 1 if line in (0, 2) else 0
            token_row = me - 1 if line == 0 else (me + 1 if line == 3 else me)
            inside = jnp.logical_and(token_row >= 0, token_row < n)
            token_row = jnp.clip(token_row, 0, n - 1)
            keep = jnp.where(inside, 0.5, 0.0)
            pair = []
            for side in range(2):
                part = sub * 2 + side
                x = first[t, token_row, :, part * channels : (part + 1) * channels]
                y = (x - mean) * slope + bias
                pair.append((y * keep) * (1.0 + jnp.tanh(0.5 * y)))
            even, odd = pair
            taps[t, line, 0] = jnp.where(place == 0, 0.0, pltpu.roll(odd, 1, 0)).astype(jnp.bfloat16)
            taps[t, line, 1] = even.astype(jnp.bfloat16)
            taps[t, line, 2] = odd.astype(jnp.bfloat16)
            taps[t, line, 3] = jnp.where(place == cols - 1, 0.0, pltpu.roll(even, cols - 1, 0)).astype(jnp.bfloat16)

    here = 4 * cols
    totals = [jnp.zeros((here, channels), jnp.float32) for _ in range(frames)]
    for a in range(frames):
        valid = a + 1
        for b in range(3):
            left = jnp.concatenate(
                [taps[:valid, b : b + 2, w : w + 2].reshape(valid * here, channels) for w in range(3)], axis=1
            )
            got = dot(left, held[a, b].reshape(3 * channels, channels))
            for t in range(valid):
                totals[frames - 1 - a + t] = totals[frames - 1 - a + t] + got[t * here : (t + 1) * here]
    for t in range(frames):
        for part in range(4):
            kept = first[t, me, :, part * channels : (part + 1) * channels]
            block = totals[t][part * cols : (part + 1) * cols] + kept
            for lane in range(channels // 128):
                tile = block[:, lane * 128 : (lane + 1) * 128]
                merged[t, part // 2, lane, pl.ds(part % 2, cols, stride=2), :] = tile
    for t in range(frames):
        for sub in range(2):
            for lane in range(channels // 128):
                out[t, sub, :, lane * 128 : (lane + 1) * 128] = merged[t, sub, lane].astype(jnp.bfloat16)


def widened(weight):
    blocks = []
    for row in range(2):
        for col in range(2):
            blocks.append(jnp.pad(weight, ((0, 0), (row, 1 - row), (col, 1 - col), (0, 0), (0, 0))))
    whole = jnp.concatenate(blocks, axis=-1)
    whole = jnp.concatenate([whole[:, 1:], whole[:, :1]], axis=1)
    return whole.reshape(-1, whole.shape[-1])


def chooser(latent):
    source = jnp.arange(3 * 8 * latent)
    target = jnp.arange(2 * 8 * latent)
    offset, lane = source // (8 * latent), source % (8 * latent)
    side, lane = lane // (4 * latent), lane % (4 * latent)
    row, col, channel = lane // (2 * latent), lane // latent % 2, lane % latent
    cell = 2 * (offset - 1) + col + 1
    to_side, to_lane = target // (8 * latent), target % (8 * latent)
    to_row, to_cell, to_channel = to_lane // (4 * latent), to_lane // latent % 4, to_lane % latent
    same = (
        (side[:, None] == to_side)
        & (row[:, None] == to_row)
        & (cell[:, None] == to_cell)
        & (channel[:, None] == to_channel)
    )
    return same.astype(jnp.bfloat16)


def shards(
    queries, keys, values, stream, head_weight, conv_in_weight, norm_gain, norm_shift, conv_mid_weight
):
    frames, _, cols, width = queries.shape
    n = lax.axis_size("seq")
    members = n // SPLIT
    depth = width // HEADS
    heads = HEADS // SPLIT
    tokens = frames * cols
    group = heads * depth
    latent = head_weight.shape[1] // 4
    wide = 2 * head_weight.shape[1]
    channels = norm_gain.shape[0]
    pairs = (heads + 1) // 2
    index = lax.axis_index("seq").astype(jnp.int32).reshape(1)
    bf16, f32 = jnp.bfloat16, jnp.float32

    head_lanes = head_weight.T
    prepared = pl.pallas_call(
        functools.partial(prepare_kernel, depth, heads),
        out_shape=[jax.ShapeDtypeStruct((tokens, group + pairs * wide), bf16)] * SPLIT
        + [jax.ShapeDtypeStruct((tokens, group), bf16)] * SPLIT,
        in_specs=[SMEM] + [HBM] * 4,
        out_specs=[VMEM] * (2 * SPLIT),
        scratch_shapes=[
            pltpu.VMEM((tokens, width), bf16),
            pltpu.VMEM((wide // 2, width), bf16),
            pltpu.VMEM((SPLIT, tokens, pairs * wide), bf16),
            pltpu.SemaphoreType.DMA((2 + 2 * SPLIT,)),
        ],
        compiler_params=pltpu.CompilerParams(vmem_limit_bytes=int(53.2 * 2**20)),
        name="prepare",
    )(
        index,
        queries.reshape(tokens, width),
        keys.reshape(tokens, width),
        values.reshape(tokens, width),
        head_lanes,
    )
    streamed = pl.pallas_call(
        stream_kernel,
        out_shape=jax.ShapeDtypeStruct((tokens, wide), f32),
        in_specs=[VMEM] * 2,
        out_specs=VMEM,
        compiler_params=pltpu.CompilerParams(vmem_limit_bytes=4 * 2**20),
        cost_estimate=pl.CostEstimate(flops=2 * 10**8, bytes_accessed=10**6, transcendentals=0),
        name="stream",
    )(stream.reshape(tokens, width), head_lanes)
    kv, q = list(prepared[:SPLIT]), list(prepared[SPLIT:])
    both = exchanged(jnp.concatenate([kv[1], q[1]], axis=1), 1 << 2)
    kv[1], q[1] = both[:, : kv[1].shape[1]], both[:, kv[1].shape[1] :]
    for step in range(2, SPLIT):
        kv[step] = exchanged(kv[step], step << 2)
    q[2:] = lax.optimization_barrier((q[2:], both))[0]
    for step in range(2, SPLIT):
        q[step] = exchanged(q[step], step << 2)

    def spread(pieces):
        block = jnp.concatenate(pieces, axis=0)
        return [block] + [exchanged(block, rest_mask(member)) for member in range(2, members, 2)]

    near = jnp.concatenate(spread(kv[:2]), axis=0)
    near = [near, exchanged(near, 1)]
    far = spread(lax.optimization_barrier((kv[2:], near[0]))[0])
    limit = pltpu.CompilerParams(vmem_limit_bytes=(12 + 2 * members // 4 * 4) * 2**20)
    state = [jax.ShapeDtypeStruct((heads, SPLIT * tokens, size), f32) for size in (wide, 2 * wide)]
    queried = pl.pallas_call(
        collect_kernel,
        out_shape=jax.ShapeDtypeStruct((SPLIT * tokens, group), bf16),
        in_specs=[VMEM] * SPLIT,
        out_specs=VMEM,
        compiler_params=pltpu.CompilerParams(vmem_limit_bytes=4 * 2**20),
        cost_estimate=pl.CostEstimate(flops=5 * 10**9, bytes_accessed=10**6, transcendentals=0),
        name="collect",
    )(*q)
    carried = pl.pallas_call(
        functools.partial(attend_kernel, depth, heads, False),
        out_shape=state,
        in_specs=[VMEM] * (1 + len(near)),
        out_specs=[VMEM] * 2,
        compiler_params=limit,
        cost_estimate=pl.CostEstimate(flops=1000000000, bytes_accessed=4 * 10**6, transcendentals=4 * 10**5),
        name="attend_near",
    )(queried, *near)
    passed = lax.optimization_barrier((far[1:], carried))[0]
    far = far + [exchanged(block, 1) for block in [far[0]] + passed]
    part = pl.pallas_call(
        functools.partial(attend_kernel, depth, heads, True),
        out_shape=jax.ShapeDtypeStruct((SPLIT * tokens // 2, wide), bf16),
        in_specs=[VMEM] * (1 + len(far) + 3),
        out_specs=VMEM,
        compiler_params=limit,
        name="attend_far",
    )(queried, *far, streamed, *carried)

    others = [exchanged(part, step << 2) for step in (3, 2, 1)]
    patch = pl.pallas_call(
        gather_kernel,
        out_shape=jax.ShapeDtypeStruct(part.shape, bf16),
        in_specs=[VMEM] * 4,
        out_specs=VMEM,
        compiler_params=pltpu.CompilerParams(vmem_limit_bytes=4 * 2**20),
        name="gather",
    )(part, *others)
    patches = [patch] + [exchanged(patch, rest_mask(member)) for member in range(1, members)]

    lane = jnp.arange(channels) // (channels // GROUPS)
    in_weight = widened(conv_in_weight)
    grouped = (lane[:, None] == lane[None, :]).astype(bf16)
    return pl.pallas_call(
        functools.partial(finish_kernel, frames, n, cols),
        out_shape=jax.ShapeDtypeStruct((frames, 2, 2 * cols, channels), bf16),
        in_specs=[SMEM] + [VMEM] * (members + 6),
        out_specs=VMEM,
        scratch_shapes=[
            pltpu.VMEM((frames, n + 2, cols, wide), bf16),
            pltpu.VMEM((n * cols, frames * 2 * wide), bf16),
            pltpu.VMEM((frames, n, cols, 4 * channels), f32),
            pltpu.VMEM((frames, 4, 4, cols, channels), bf16),
            pltpu.VMEM((frames, 2, channels // 128, 2 * cols, 128), f32),
        ],
        compiler_params=pltpu.CompilerParams(vmem_limit_bytes=(16 if n <= 16 else 40) * 2**20),
        name="finish",
    )(
        index,
        *patches,
        chooser(latent),
        in_weight,
        conv_mid_weight,
        grouped,
        norm_gain.reshape(1, channels),
        norm_shift.reshape(1, channels),
    )


def solution(mesh):
    placed = (
        P("groups", "seq", None, None),
        P("groups", "seq", None, None),
        P("groups", "seq", None, None),
        P("groups", "seq", None, None),
        P(),
        P(),
        P(),
        P(),
        P(),
    )
    return jax.shard_map(
        shards,
        mesh=mesh,
        in_specs=placed,
        out_specs=P("groups", "seq", None, None),
        check_vma=False,
    )
```

```python
import functools

import jax
import jax.numpy as jnp
from jax import lax
from jax.experimental import pallas as pl
from jax.experimental.pallas import tpu as pltpu
from jax.sharding import PartitionSpec as P

HEADS = 20
GROUPS = 32
SPLIT = 4
EPS = 1e-06

VMEM = pl.BlockSpec(memory_space=pltpu.VMEM)
SMEM = pl.BlockSpec(memory_space=pltpu.SMEM)
HBM = pl.BlockSpec(memory_space=pltpu.HBM)


def exchanged(value, mask):
    pairs = [(source, source ^ mask) for source in range(lax.axis_size("seq"))]
    return lax.ppermute(value, "seq", pairs)


def rest_mask(member):
    return (member & 3) | ((member >> 2) << 4)


def dot(left, right):
    return jnp.dot(left, right, preferred_element_type=jnp.float32)


def through_twice(rows, weight, columns):
    part = weight[:, columns]
    return lax.dot_general(
        rows[:, columns],
        jnp.concatenate([part, part], axis=0),
        (((1,), (1,)), ((), ())),
        preferred_element_type=jnp.float32,
    )


def prepare_kernel(depth, heads, index, q, k, v, w, *refs):
    kv_out, q_out, refs = refs[:SPLIT], refs[SPLIT : 2 * SPLIT], refs[2 * SPLIT :]
    v_here, w_here, projected, sem = refs
    tokens = q.shape[0]
    group = heads * depth
    place = (index[0] >> 2) & 3
    whole = [
        pltpu.make_async_copy(source, target, sem.at[at])
        for at, (source, target) in enumerate(((v, v_here), (w, w_here)))
    ]
    parts = []
    for step in range(SPLIT):
        columns = pl.ds(pl.multiple_of((place ^ step) * group, 128), group)
        at = len(whole) + 2 * step
        parts.append(pltpu.make_async_copy(k.at[:, columns], kv_out[step].at[:, :group], sem.at[at]))
        parts.append(pltpu.make_async_copy(q.at[:, columns], q_out[step], sem.at[at + 1]))
    for copy in whole + parts:
        copy.start()
    half = w.shape[0]
    wide = 2 * half
    low = lax.broadcasted_iota(jnp.int32, (tokens, wide), 1) < half

    def head_through(head):
        return through_twice(v_here, w_here, slice(head * depth, (head + 1) * depth))

    for copy in whole:
        copy.wait()
    for owner in range(SPLIT):
        for pair in range((heads + 1) // 2):
            first = owner * heads + 2 * pair
            both = head_through(first)
            if 2 * pair + 1 < heads:
                both = jnp.where(low, both, head_through(first + 1))
            projected[owner, :, pair * wide : (pair + 1) * wide] = both.astype(jnp.bfloat16)
    for step in range(SPLIT):
        kv_out[step][:, group:] = projected[place ^ step]
    for copy in parts:
        copy.wait()


def stream_kernel(s, w, out):
    out[...] = through_twice(s, w, slice(None))


def attend_kernel(depth, heads, first, last, *refs):
    q, refs = refs[0], refs[1:]
    if last:
        refs, out = refs[:-1], refs[-1]
        refs, stream = refs[:-1], refs[-1]
    else:
        refs, (top_out, mixed_out) = refs[:-2], refs[-2:]
    if first:
        kv = refs
    else:
        kv, (top_in, mixed_in) = refs[:-2], refs[-2:]
    group = heads * depth
    wide = 128
    factor = 1.4426950408889634 / depth**0.5
    rows = q.shape[0]
    tokens = rows // SPLIT
    half = rows // 2
    low = lax.broadcasted_iota(jnp.int32, (rows, wide), 1) < wide // 2
    keys = sum(piece.shape[0] for piece in kv)
    ones = jnp.ones((keys, wide), jnp.bfloat16)

    def scores_of(head):
        columns = slice(head * depth, (head + 1) * depth)
        query = q[:, columns]
        key = jnp.concatenate([piece[:, columns] for piece in kv], axis=0)
        return lax.dot_general(query, key, (((1,), (1,)), ((), ())), preferred_element_type=jnp.float32)

    summed = jnp.zeros((rows, wide), jnp.float32)
    upcoming = scores_of(0)
    for head in range(heads):
        scores = upcoming
        if head + 1 < heads:
            upcoming = scores_of(head + 1)
        top = jnp.broadcast_to(jnp.max(scores, axis=1, keepdims=True), (rows, wide))
        if not first:
            before = top_in[head]
            top = jnp.maximum(top, before)
        expo = jnp.concatenate(
            [
                jnp.exp2((scores[:, at : at + wide] - top[:, : min(wide, keys - at)]) * factor).astype(jnp.bfloat16)
                for at in range(0, keys, wide)
            ],
            axis=1,
        )
        at = group + (head // 2) * wide
        value = jnp.concatenate([piece[:, at : at + wide] for piece in kv], axis=0)
        mixed = dot(expo, jnp.concatenate([value, ones], axis=1))
        weighed, total = mixed[:, :wide], mixed[:, wide:]
        if not first:
            decay = jnp.exp2((before - top) * factor)
            weighed = weighed + mixed_in[head, :, :wide] * decay
            total = total + mixed_in[head, :, wide:] * decay
        if not last:
            top_out[head] = top
            mixed_out[head, :, :wide] = weighed
            mixed_out[head, :, wide:] = total
            continue
        mine = low if head % 2 == 0 else jnp.logical_not(low)
        summed = summed + jnp.where(mine, weighed / total, 0.0)
    if not last:
        return
    summed = summed + pltpu.roll(summed, wide // 2, 1)
    upper = summed[:half]
    upper = jnp.concatenate([upper[:tokens] + stream[...], upper[tokens:]], axis=0)
    out[...] = jnp.where(low[:half], upper, summed[half:]).astype(out.dtype)


def collect_kernel(*refs):
    pieces, out = refs[:-1], refs[-1]
    tokens = pieces[0].shape[0]
    for at, piece in enumerate(pieces):
        out[at * tokens : (at + 1) * tokens, :] = piece[...]


def gather_kernel(own, three, two, one, out):
    rows, wide = own.shape
    half = rows // 2

    def swap_rows(x):
        return jnp.concatenate([x[half:], x[:half]], axis=0)

    own, one, two, three = (ref[...].astype(jnp.float32) for ref in (own, one, two, three))
    far = two + swap_rows(three)
    latent = (own + swap_rows(one)) + pltpu.roll(far, wide // 2, 1)
    out[...] = latent.astype(jnp.bfloat16)


def finish_kernel(frames, n, cols, order, index, *refs):
    members = n // SPLIT
    patches, refs = refs[:members], refs[members:]
    (chosen, in_weight, held, grouped, gain, shift, out, grid, stacked, first, taps, merged) = refs
    channels = gain.shape[1]
    wide = grid.shape[-1]
    half = wide // 2
    me = index[0]
    grid[:, 0] = jnp.zeros((frames, cols, wide), jnp.bfloat16)
    grid[:, n + 1] = jnp.zeros((frames, cols, wide), jnp.bfloat16)
    tokens = frames * cols
    for member in range(members):
        latent = patches[member][...].astype(jnp.float32)
        rows = latent.shape[0]
        column = lax.broadcasted_iota(jnp.int32, latent.shape, 0) % cols
        before = jnp.where(column == 0, 0.0, pltpu.roll(latent, 1, 0))
        after = jnp.where(column == cols - 1, 0.0, pltpu.roll(latent, rows - 1, 0))
        around = jnp.concatenate([before, latent, after], axis=1).astype(jnp.bfloat16)
        patch = dot(around, chosen[...]).astype(jnp.bfloat16)
        for step in range(SPLIT):
            row = me ^ (rest_mask(order[member]) | (step << 2))
            at, lanes = (step % 2) * tokens, (step // 2) * wide
            for t in range(frames):
                grid[t, row + 1] = patch[at + t * cols : at + (t + 1) * cols, lanes : lanes + wide]

    cells = n * cols
    chunk = min(cells, 256)
    rows_in = chunk // cols
    upper = lax.broadcasted_iota(jnp.int32, (rows_in, cols, wide), 2) < half
    depth = 2 * wide
    for t in range(frames):
        for r in range(0, n, rows_in):
            near = grid[t, r + 1 : r + 1 + rows_in]
            far = jnp.where(upper, grid[t, r + 2 : r + 2 + rows_in], grid[t, r : r + rows_in])
            stacked[r * cols : r * cols + chunk, t * depth : t * depth + wide] = near.reshape(chunk, wide)
            stacked[r * cols : r * cols + chunk, t * depth + wide : (t + 1) * depth] = far.reshape(chunk, wide)

    counted = 4.0 * frames * cells
    members_of = channels // GROUPS
    sums = jnp.zeros((8, channels), jnp.float32)
    squares = jnp.zeros((8, channels), jnp.float32)
    pivot = None
    for t in range(frames):
        for r in range(0, n, rows_in):
            for row in range(2):
                lanes = slice(row * 2 * channels, (row + 1) * 2 * channels)
                both = dot(
                    stacked[r * cols : r * cols + chunk, : (t + 1) * depth],
                    in_weight[(frames - 1 - t) * depth :, lanes],
                )
                first[t, r : r + rows_in, :, lanes] = both.reshape(rows_in, cols, 2 * channels)
                for here in (both[:, :channels], both[:, channels:]):
                    if pivot is None:
                        pivot = jnp.sum(here, axis=0, keepdims=True) / chunk
                    off = (here - pivot).reshape(chunk // 8, 8, channels)
                    sums = sums + jnp.sum(off, axis=0)
                    squares = squares + jnp.sum(off * off, axis=0)

    def over_group(line):
        high = line.astype(jnp.bfloat16)
        rest = line - high.astype(jnp.float32)
        middle = rest.astype(jnp.bfloat16)
        lower = (rest - middle.astype(jnp.float32)).astype(jnp.bfloat16)
        none = jnp.zeros((13, channels), jnp.bfloat16)
        terms = jnp.concatenate([high, middle, lower, none], axis=0)
        return jnp.sum(dot(terms, grouped[...])[:8], axis=0, keepdims=True)

    offset = jnp.sum(sums, axis=0, keepdims=True) / counted
    channel_mean = pivot + offset
    mean = over_group(channel_mean) / members_of
    apart = channel_mean - mean
    within = jnp.sum(squares, axis=0, keepdims=True) / counted - offset * offset
    variance = over_group(within + apart * apart) / members_of
    slope = gain[...] / jnp.sqrt(variance + EPS)
    bias = shift[...]

    place = lax.broadcasted_iota(jnp.int32, (cols, channels), 0)
    for t in range(frames):
        for line in range(4):
            sub = 1 if line in (0, 2) else 0
            token_row = me - 1 if line == 0 else (me + 1 if line == 3 else me)
            inside = jnp.logical_and(token_row >= 0, token_row < n)
            token_row = jnp.clip(token_row, 0, n - 1)
            keep = jnp.where(inside, 0.5, 0.0)
            pair = []
            for side in range(2):
                part = sub * 2 + side
                x = first[t, token_row, :, part * channels : (part + 1) * channels]
                y = (x - mean) * slope + bias
                pair.append((y * keep) * (1.0 + jnp.tanh(0.5 * y)))
            even, odd = pair
            taps[t, line, 0] = jnp.where(place == 0, 0.0, pltpu.roll(odd, 1, 0)).astype(jnp.bfloat16)
            taps[t, line, 1] = even.astype(jnp.bfloat16)
            taps[t, line, 2] = odd.astype(jnp.bfloat16)
            taps[t, line, 3] = jnp.where(place == cols - 1, 0.0, pltpu.roll(even, cols - 1, 0)).astype(jnp.bfloat16)

    here = 4 * cols
    totals = [jnp.zeros((here, channels), jnp.float32) for _ in range(frames)]
    left = jnp.concatenate(
        [taps[:, b : b + 2, w : w + 2].reshape(frames * here, channels) for b in range(3) for w in range(3)], axis=1
    )
    deep = 9 * channels
    now = held[2].reshape(deep, channels)
    then = held[1].reshape(deep, channels)
    got = dot(left, jnp.concatenate([now, then], axis=1))
    first_got = dot(left[:here], held[0].reshape(deep, channels))
    for t in range(frames):
        totals[t] = totals[t] + got[t * here : (t + 1) * here, :channels]
        if t + 1 < frames:
            totals[t + 1] = totals[t + 1] + got[t * here : (t + 1) * here, channels:]
    totals[2] = totals[2] + first_got
    for t in range(frames):
        for part in range(4):
            kept = first[t, me, :, part * channels : (part + 1) * channels]
            block = totals[t][part * cols : (part + 1) * cols] + kept
            for lane in range(channels // 128):
                tile = block[:, lane * 128 : (lane + 1) * 128]
                merged[t, part // 2, lane, pl.ds(part % 2, cols, stride=2), :] = tile
    for t in range(frames):
        for sub in range(2):
            for lane in range(channels // 128):
                out[t, sub, :, lane * 128 : (lane + 1) * 128] = merged[t, sub, lane].astype(jnp.bfloat16)


def widened(weight):
    blocks = []
    for row in range(2):
        for col in range(2):
            blocks.append(jnp.pad(weight, ((0, 0), (row, 1 - row), (col, 1 - col), (0, 0), (0, 0))))
    whole = jnp.concatenate(blocks, axis=-1)
    whole = jnp.concatenate([whole[:, 1:], whole[:, :1]], axis=1)
    return whole.reshape(-1, whole.shape[-1])


def chooser(latent):
    source = jnp.arange(3 * 8 * latent)
    target = jnp.arange(2 * 8 * latent)
    offset, lane = source // (8 * latent), source % (8 * latent)
    side, lane = lane // (4 * latent), lane % (4 * latent)
    row, col, channel = lane // (2 * latent), lane // latent % 2, lane % latent
    cell = 2 * (offset - 1) + col + 1
    to_side, to_lane = target // (8 * latent), target % (8 * latent)
    to_row, to_cell, to_channel = to_lane // (4 * latent), to_lane // latent % 4, to_lane % latent
    same = (
        (side[:, None] == to_side)
        & (row[:, None] == to_row)
        & (cell[:, None] == to_cell)
        & (channel[:, None] == to_channel)
    )
    return same.astype(jnp.bfloat16)


def shards(
    queries, keys, values, stream, head_weight, conv_in_weight, norm_gain, norm_shift, conv_mid_weight
):
    frames, _, cols, width = queries.shape
    n = lax.axis_size("seq")
    members = n // SPLIT
    depth = width // HEADS
    heads = HEADS // SPLIT
    tokens = frames * cols
    group = heads * depth
    latent = head_weight.shape[1] // 4
    wide = 2 * head_weight.shape[1]
    channels = norm_gain.shape[0]
    pairs = (heads + 1) // 2
    index = lax.axis_index("seq").astype(jnp.int32).reshape(1)
    bf16, f32 = jnp.bfloat16, jnp.float32

    head_lanes = head_weight.T
    prepared = pl.pallas_call(
        functools.partial(prepare_kernel, depth, heads),
        out_shape=[jax.ShapeDtypeStruct((tokens, group + pairs * wide), bf16)] * SPLIT
        + [jax.ShapeDtypeStruct((tokens, group), bf16)] * SPLIT,
        in_specs=[SMEM] + [HBM] * 4,
        out_specs=[VMEM] * (2 * SPLIT),
        scratch_shapes=[
            pltpu.VMEM((tokens, width), bf16),
            pltpu.VMEM((wide // 2, width), bf16),
            pltpu.VMEM((SPLIT, tokens, pairs * wide), bf16),
            pltpu.SemaphoreType.DMA((2 + 2 * SPLIT,)),
        ],
        compiler_params=pltpu.CompilerParams(vmem_limit_bytes=int(53.2 * 2**20)),
        name="prepare",
    )(
        index,
        queries.reshape(tokens, width),
        keys.reshape(tokens, width),
        values.reshape(tokens, width),
        head_lanes,
    )
    streamed = pl.pallas_call(
        stream_kernel,
        out_shape=jax.ShapeDtypeStruct((tokens, wide), f32),
        in_specs=[VMEM] * 2,
        out_specs=VMEM,
        compiler_params=pltpu.CompilerParams(vmem_limit_bytes=4 * 2**20),
        cost_estimate=pl.CostEstimate(flops=2 * 10**8, bytes_accessed=10**6, transcendentals=0),
        name="stream",
    )(stream.reshape(tokens, width), head_lanes)
    kv, q = list(prepared[:SPLIT]), list(prepared[SPLIT:])
    both = exchanged(jnp.concatenate([kv[1], q[1]], axis=1), 1 << 2)
    kv[1], q[1] = both[:, : kv[1].shape[1]], both[:, kv[1].shape[1] :]
    for step in range(2, SPLIT):
        kv[step] = exchanged(kv[step], step << 2)
    q[2:] = lax.optimization_barrier((q[2:], both))[0]
    for step in range(2, SPLIT):
        q[step] = exchanged(q[step], step << 2)

    def spread(pieces):
        block = jnp.concatenate(pieces, axis=0)
        return [block] + [exchanged(block, rest_mask(member)) for member in range(2, members, 2)]

    near = jnp.concatenate(spread(kv[:2]), axis=0)
    near = [near, exchanged(near, 1)]
    far = spread(lax.optimization_barrier((kv[2:], near[0]))[0])
    limit = pltpu.CompilerParams(vmem_limit_bytes=(12 + 2 * members // 4 * 4) * 2**20)
    queried = pl.pallas_call(
        collect_kernel,
        out_shape=jax.ShapeDtypeStruct((SPLIT * tokens, group), bf16),
        in_specs=[VMEM] * SPLIT,
        out_specs=VMEM,
        compiler_params=pltpu.CompilerParams(vmem_limit_bytes=4 * 2**20),
        cost_estimate=pl.CostEstimate(flops=5 * 10**9, bytes_accessed=10**6, transcendentals=0),
        name="collect",
    )(*q)
    state = [jax.ShapeDtypeStruct((heads, SPLIT * tokens, size), f32) for size in (wide, 2 * wide)]

    def attended(blocks, carried, last, name):
        return pl.pallas_call(
            functools.partial(attend_kernel, depth, heads, not carried, bool(last)),
            out_shape=jax.ShapeDtypeStruct((SPLIT * tokens // 2, wide), bf16) if last else state,
            in_specs=[VMEM] * (1 + len(blocks) + len(carried) + len(last)),
            out_specs=VMEM if last else [VMEM] * 2,
            compiler_params=limit,
            cost_estimate=pl.CostEstimate(flops=10**9, bytes_accessed=4 * 10**6, transcendentals=4 * 10**5),
            name=name,
        )(queried, *blocks, *carried, *last)

    carried = attended(near, [], [], "attend_near")
    beside = exchanged(far[0], 1)
    middle = carried
    carried = attended([far[0], beside], carried, [], "attend_middle")
    passed = lax.optimization_barrier((far[1:], middle))[0]
    far = passed + [exchanged(block, 1) for block in passed]
    part = attended(far, carried, [streamed], "attend_far")

    others = [exchanged(part, step << 2) for step in (3, 2, 1)]
    patch = pl.pallas_call(
        gather_kernel,
        out_shape=jax.ShapeDtypeStruct(part.shape, bf16),
        in_specs=[VMEM] * 4,
        out_specs=VMEM,
        compiler_params=pltpu.CompilerParams(vmem_limit_bytes=4 * 2**20),
        name="gather",
    )(part, *others)
    order = sorted(range(1, members), key=lambda member: -member)
    patches = [patch] + [exchanged(patch, rest_mask(member)) for member in order]

    lane = jnp.arange(channels) // (channels // GROUPS)
    in_weight = widened(conv_in_weight)
    grouped = (lane[:, None] == lane[None, :]).astype(bf16)
    return pl.pallas_call(
        functools.partial(finish_kernel, frames, n, cols, [0] + order),
        out_shape=jax.ShapeDtypeStruct((frames, 2, 2 * cols, channels), bf16),
        in_specs=[SMEM] + [VMEM] * (members + 6),
        out_specs=VMEM,
        scratch_shapes=[
            pltpu.VMEM((frames, n + 2, cols, wide), bf16),
            pltpu.VMEM((n * cols, frames * 2 * wide), bf16),
            pltpu.VMEM((frames, n, cols, 4 * channels), f32),
            pltpu.VMEM((frames, 4, 4, cols, channels), bf16),
            pltpu.VMEM((frames, 2, channels // 128, 2 * cols, 128), f32),
        ],
        compiler_params=pltpu.CompilerParams(vmem_limit_bytes=(16 if n <= 16 else 40) * 2**20),
        name="finish",
    )(
        index,
        *patches,
        chooser(latent),
        in_weight,
        conv_mid_weight,
        grouped,
        norm_gain.reshape(1, channels),
        norm_shift.reshape(1, channels),
    )


def solution(mesh):
    placed = (
        P("groups", "seq", None, None),
        P("groups", "seq", None, None),
        P("groups", "seq", None, None),
        P("groups", "seq", None, None),
        P(),
        P(),
        P(),
        P(),
        P(),
    )
    return jax.shard_map(
        shards,
        mesh=mesh,
        in_specs=placed,
        out_specs=P("groups", "seq", None, None),
        check_vma=False,
    )
```

```python
import functools

import jax
import jax.numpy as jnp
from jax import lax
from jax.experimental import pallas as pl
from jax.experimental.pallas import tpu as pltpu
from jax.sharding import PartitionSpec as P

HEADS = 20
GROUPS = 32
SPLIT = 4
EPS = 1e-06

VMEM = pl.BlockSpec(memory_space=pltpu.VMEM)
SMEM = pl.BlockSpec(memory_space=pltpu.SMEM)
HBM = pl.BlockSpec(memory_space=pltpu.HBM)


def exchanged(value, mask):
    pairs = [(source, source ^ mask) for source in range(lax.axis_size("seq"))]
    return lax.ppermute(value, "seq", pairs)


def rest_mask(member):
    return (member & 3) | ((member >> 2) << 4)


def dot(left, right):
    return jnp.dot(left, right, preferred_element_type=jnp.float32)


def through_twice(rows, weight, columns):
    part = weight[:, columns]
    return lax.dot_general(
        rows[:, columns],
        jnp.concatenate([part, part], axis=0),
        (((1,), (1,)), ((), ())),
        preferred_element_type=jnp.float32,
    )


def prepare_kernel(depth, heads, index, q, k, v, w, *refs):
    kv_out, q_out, refs = refs[:SPLIT], refs[SPLIT : 2 * SPLIT], refs[2 * SPLIT :]
    v_here, w_here, projected, sem = refs
    tokens = q.shape[0]
    group = heads * depth
    place = (index[0] >> 2) & 3
    whole = [
        pltpu.make_async_copy(source, target, sem.at[at])
        for at, (source, target) in enumerate(((v, v_here), (w, w_here)))
    ]
    parts = []
    for step in range(SPLIT):
        columns = pl.ds(pl.multiple_of((place ^ step) * group, 128), group)
        at = len(whole) + 2 * step
        parts.append(pltpu.make_async_copy(k.at[:, columns], kv_out[step].at[:, :group], sem.at[at]))
        parts.append(pltpu.make_async_copy(q.at[:, columns], q_out[step], sem.at[at + 1]))
    for copy in whole + parts:
        copy.start()
    half = w.shape[0]
    wide = 2 * half
    low = lax.broadcasted_iota(jnp.int32, (tokens, wide), 1) < half

    def head_through(head):
        return through_twice(v_here, w_here, slice(head * depth, (head + 1) * depth))

    for copy in whole:
        copy.wait()
    for owner in range(SPLIT):
        for pair in range((heads + 1) // 2):
            first = owner * heads + 2 * pair
            both = head_through(first)
            if 2 * pair + 1 < heads:
                both = jnp.where(low, both, head_through(first + 1))
            projected[owner, :, pair * wide : (pair + 1) * wide] = both.astype(jnp.bfloat16)
    for step in range(SPLIT):
        kv_out[step][:, group:] = projected[place ^ step]
    for copy in parts:
        copy.wait()


def stream_kernel(s, w, out):
    out[...] = through_twice(s, w, slice(None))


def attend_kernel(depth, heads, first, last, *refs):
    q, refs = refs[0], refs[1:]
    if last:
        refs, out = refs[:-1], refs[-1]
        refs, stream = refs[:-1], refs[-1]
    else:
        refs, (top_out, mixed_out) = refs[:-2], refs[-2:]
    if first:
        kv = refs
    else:
        kv, (top_in, mixed_in) = refs[:-2], refs[-2:]
    group = heads * depth
    wide = 128
    factor = 1.4426950408889634 / depth**0.5
    rows = q.shape[0]
    tokens = rows // SPLIT
    half = rows // 2
    low = lax.broadcasted_iota(jnp.int32, (rows, wide), 1) < wide // 2
    keys = sum(piece.shape[0] for piece in kv)
    ones = jnp.ones((keys, wide), jnp.bfloat16)

    def scores_of(head):
        columns = slice(head * depth, (head + 1) * depth)
        query = q[:, columns]
        key = jnp.concatenate([piece[:, columns] for piece in kv], axis=0)
        return lax.dot_general(query, key, (((1,), (1,)), ((), ())), preferred_element_type=jnp.float32)

    summed = jnp.zeros((rows, wide), jnp.float32)
    upcoming = scores_of(0)
    for head in range(heads):
        scores = upcoming
        if head + 1 < heads:
            upcoming = scores_of(head + 1)
        top = jnp.broadcast_to(jnp.max(scores, axis=1, keepdims=True), (rows, wide))
        if not first:
            before = top_in[head]
            top = jnp.maximum(top, before)
        expo = jnp.concatenate(
            [
                jnp.exp2((scores[:, at : at + wide] - top[:, : min(wide, keys - at)]) * factor).astype(jnp.bfloat16)
                for at in range(0, keys, wide)
            ],
            axis=1,
        )
        at = group + (head // 2) * wide
        value = jnp.concatenate([piece[:, at : at + wide] for piece in kv], axis=0)
        mixed = dot(expo, jnp.concatenate([value, ones], axis=1))
        weighed, total = mixed[:, :wide], mixed[:, wide:]
        if not first:
            decay = jnp.exp2((before - top) * factor)
            weighed = weighed + mixed_in[head, :, :wide] * decay
            total = total + mixed_in[head, :, wide:] * decay
        if not last:
            top_out[head] = top
            mixed_out[head, :, :wide] = weighed
            mixed_out[head, :, wide:] = total
            continue
        mine = low if head % 2 == 0 else jnp.logical_not(low)
        summed = summed + jnp.where(mine, weighed / total, 0.0)
    if not last:
        return
    summed = summed + pltpu.roll(summed, wide // 2, 1)
    upper = summed[:half]
    upper = jnp.concatenate([upper[:tokens] + stream[...], upper[tokens:]], axis=0)
    out[...] = jnp.where(low[:half], upper, summed[half:]).astype(out.dtype)


def collect_kernel(*refs):
    pieces, out = refs[:-1], refs[-1]
    tokens = pieces[0].shape[0]
    for at, piece in enumerate(pieces):
        out[at * tokens : (at + 1) * tokens, :] = piece[...]


def gather_kernel(own, three, two, one, out):
    rows, wide = own.shape
    half = rows // 2

    def swap_rows(x):
        return jnp.concatenate([x[half:], x[:half]], axis=0)

    own, one, two, three = (ref[...].astype(jnp.float32) for ref in (own, one, two, three))
    far = two + swap_rows(three)
    latent = (own + swap_rows(one)) + pltpu.roll(far, wide // 2, 1)
    out[...] = latent.astype(jnp.bfloat16)


def finish_kernel(frames, n, cols, order, index, *refs):
    members = n // SPLIT
    patches, refs = refs[:members], refs[members:]
    (chosen, in_weight, held, grouped, gain, shift, out, grid, stacked, first, taps, merged) = refs
    channels = gain.shape[1]
    wide = grid.shape[-1]
    half = wide // 2
    me = index[0]
    grid[:, 0] = jnp.zeros((frames, cols, wide), jnp.bfloat16)
    grid[:, n + 1] = jnp.zeros((frames, cols, wide), jnp.bfloat16)
    tokens = frames * cols
    for member in range(members):
        latent = patches[member][...].astype(jnp.float32)
        rows = latent.shape[0]
        column = lax.broadcasted_iota(jnp.int32, latent.shape, 0) % cols
        before = jnp.where(column == 0, 0.0, pltpu.roll(latent, 1, 0))
        after = jnp.where(column == cols - 1, 0.0, pltpu.roll(latent, rows - 1, 0))
        around = jnp.concatenate([before, latent, after], axis=1).astype(jnp.bfloat16)
        patch = dot(around, chosen[...]).astype(jnp.bfloat16)
        for step in range(SPLIT):
            row = me ^ (rest_mask(order[member]) | (step << 2))
            at, lanes = (step % 2) * tokens, (step // 2) * wide
            for t in range(frames):
                grid[t, row + 1] = patch[at + t * cols : at + (t + 1) * cols, lanes : lanes + wide]

    cells = n * cols
    chunk = min(cells, 256)
    rows_in = chunk // cols
    upper = lax.broadcasted_iota(jnp.int32, (rows_in, cols, wide), 2) < half
    depth = 2 * wide
    for t in range(frames):
        for r in range(0, n, rows_in):
            near = grid[t, r + 1 : r + 1 + rows_in]
            far = jnp.where(upper, grid[t, r + 2 : r + 2 + rows_in], grid[t, r : r + rows_in])
            stacked[r * cols : r * cols + chunk, t * depth : t * depth + wide] = near.reshape(chunk, wide)
            stacked[r * cols : r * cols + chunk, t * depth + wide : (t + 1) * depth] = far.reshape(chunk, wide)

    counted = 4.0 * frames * cells
    members_of = channels // GROUPS
    sums = jnp.zeros((8, channels), jnp.float32)
    squares = jnp.zeros((8, channels), jnp.float32)
    pivot = None
    for t in range(frames):
        for r in range(0, n, rows_in):
            for row in range(2):
                lanes = slice(row * 2 * channels, (row + 1) * 2 * channels)
                both = dot(
                    stacked[r * cols : r * cols + chunk, : (t + 1) * depth],
                    in_weight[(frames - 1 - t) * depth :, lanes],
                )
                first[t, r : r + rows_in, :, lanes] = both.reshape(rows_in, cols, 2 * channels)
                for here in (both[:, :channels], both[:, channels:]):
                    if pivot is None:
                        pivot = jnp.sum(here, axis=0, keepdims=True) / chunk
                    off = (here - pivot).reshape(chunk // 8, 8, channels)
                    sums = sums + jnp.sum(off, axis=0)
                    squares = squares + jnp.sum(off * off, axis=0)

    def over_group(line):
        high = line.astype(jnp.bfloat16)
        rest = line - high.astype(jnp.float32)
        middle = rest.astype(jnp.bfloat16)
        lower = (rest - middle.astype(jnp.float32)).astype(jnp.bfloat16)
        none = jnp.zeros((13, channels), jnp.bfloat16)
        terms = jnp.concatenate([high, middle, lower, none], axis=0)
        return jnp.sum(dot(terms, grouped[...])[:8], axis=0, keepdims=True)

    offset = jnp.sum(sums, axis=0, keepdims=True) / counted
    channel_mean = pivot + offset
    mean = over_group(channel_mean) / members_of
    apart = channel_mean - mean
    within = jnp.sum(squares, axis=0, keepdims=True) / counted - offset * offset
    variance = over_group(within + apart * apart) / members_of
    slope = gain[...] / jnp.sqrt(variance + EPS)
    bias = shift[...]

    place = lax.broadcasted_iota(jnp.int32, (cols, channels), 0)
    for t in range(frames):
        for line in range(4):
            sub = 1 if line in (0, 2) else 0
            token_row = me - 1 if line == 0 else (me + 1 if line == 3 else me)
            inside = jnp.logical_and(token_row >= 0, token_row < n)
            token_row = jnp.clip(token_row, 0, n - 1)
            keep = jnp.where(inside, 0.5, 0.0)
            pair = []
            for side in range(2):
                part = sub * 2 + side
                x = first[t, token_row, :, part * channels : (part + 1) * channels]
                y = (x - mean) * slope + bias
                pair.append((y * keep) * (1.0 + jnp.tanh(0.5 * y)))
            even, odd = pair
            taps[t, line, 0] = jnp.where(place == 0, 0.0, pltpu.roll(odd, 1, 0)).astype(jnp.bfloat16)
            taps[t, line, 1] = even.astype(jnp.bfloat16)
            taps[t, line, 2] = odd.astype(jnp.bfloat16)
            taps[t, line, 3] = jnp.where(place == cols - 1, 0.0, pltpu.roll(even, cols - 1, 0)).astype(jnp.bfloat16)

    here = 4 * cols
    totals = [jnp.zeros((here, channels), jnp.float32) for _ in range(frames)]
    left = jnp.concatenate(
        [taps[:, b : b + 2, w : w + 2].reshape(frames * here, channels) for b in range(3) for w in range(3)], axis=1
    )
    deep = 9 * channels
    now = held[2].reshape(deep, channels)
    then = held[1].reshape(deep, channels)
    got = dot(left, jnp.concatenate([now, then], axis=1))
    first_got = dot(left[:here], held[0].reshape(deep, channels))
    for t in range(frames):
        totals[t] = totals[t] + got[t * here : (t + 1) * here, :channels]
        if t + 1 < frames:
            totals[t + 1] = totals[t + 1] + got[t * here : (t + 1) * here, channels:]
    totals[2] = totals[2] + first_got
    for t in range(frames):
        for part in range(4):
            kept = first[t, me, :, part * channels : (part + 1) * channels]
            block = totals[t][part * cols : (part + 1) * cols] + kept
            for lane in range(channels // 128):
                tile = block[:, lane * 128 : (lane + 1) * 128]
                merged[t, part // 2, lane, pl.ds(part % 2, cols, stride=2), :] = tile
    for t in range(frames):
        for sub in range(2):
            for lane in range(channels // 128):
                out[t, sub, :, lane * 128 : (lane + 1) * 128] = merged[t, sub, lane].astype(jnp.bfloat16)


def widened(weight):
    blocks = []
    for row in range(2):
        for col in range(2):
            blocks.append(jnp.pad(weight, ((0, 0), (row, 1 - row), (col, 1 - col), (0, 0), (0, 0))))
    whole = jnp.concatenate(blocks, axis=-1)
    whole = jnp.concatenate([whole[:, 1:], whole[:, :1]], axis=1)
    return whole.reshape(-1, whole.shape[-1])


def chooser(latent):
    source = jnp.arange(3 * 8 * latent)
    target = jnp.arange(2 * 8 * latent)
    offset, lane = source // (8 * latent), source % (8 * latent)
    side, lane = lane // (4 * latent), lane % (4 * latent)
    row, col, channel = lane // (2 * latent), lane // latent % 2, lane % latent
    cell = 2 * (offset - 1) + col + 1
    to_side, to_lane = target // (8 * latent), target % (8 * latent)
    to_row, to_cell, to_channel = to_lane // (4 * latent), to_lane // latent % 4, to_lane % latent
    same = (
        (side[:, None] == to_side)
        & (row[:, None] == to_row)
        & (cell[:, None] == to_cell)
        & (channel[:, None] == to_channel)
    )
    return same.astype(jnp.bfloat16)


def shards(
    queries, keys, values, stream, head_weight, conv_in_weight, norm_gain, norm_shift, conv_mid_weight
):
    frames, _, cols, width = queries.shape
    n = lax.axis_size("seq")
    members = n // SPLIT
    depth = width // HEADS
    heads = HEADS // SPLIT
    tokens = frames * cols
    group = heads * depth
    latent = head_weight.shape[1] // 4
    wide = 2 * head_weight.shape[1]
    channels = norm_gain.shape[0]
    pairs = (heads + 1) // 2
    index = lax.axis_index("seq").astype(jnp.int32).reshape(1)
    bf16, f32 = jnp.bfloat16, jnp.float32

    head_lanes = head_weight.T
    prepared = pl.pallas_call(
        functools.partial(prepare_kernel, depth, heads),
        out_shape=[jax.ShapeDtypeStruct((tokens, group + pairs * wide), bf16)] * SPLIT
        + [jax.ShapeDtypeStruct((tokens, group), bf16)] * SPLIT,
        in_specs=[SMEM] + [HBM] * 4,
        out_specs=[VMEM] * (2 * SPLIT),
        scratch_shapes=[
            pltpu.VMEM((tokens, width), bf16),
            pltpu.VMEM((wide // 2, width), bf16),
            pltpu.VMEM((SPLIT, tokens, pairs * wide), bf16),
            pltpu.SemaphoreType.DMA((2 + 2 * SPLIT,)),
        ],
        compiler_params=pltpu.CompilerParams(vmem_limit_bytes=int(53.2 * 2**20)),
        name="prepare",
    )(
        index,
        queries.reshape(tokens, width),
        keys.reshape(tokens, width),
        values.reshape(tokens, width),
        head_lanes,
    )
    streamed = pl.pallas_call(
        stream_kernel,
        out_shape=jax.ShapeDtypeStruct((tokens, wide), f32),
        in_specs=[VMEM] * 2,
        out_specs=VMEM,
        compiler_params=pltpu.CompilerParams(vmem_limit_bytes=4 * 2**20),
        cost_estimate=pl.CostEstimate(flops=2 * 10**8, bytes_accessed=10**6, transcendentals=0),
        name="stream",
    )(stream.reshape(tokens, width), head_lanes)
    kv, q = list(prepared[:SPLIT]), list(prepared[SPLIT:])
    both = exchanged(jnp.concatenate([kv[1], q[1]], axis=1), 1 << 2)
    kv[1], q[1] = both[:, : kv[1].shape[1]], both[:, kv[1].shape[1] :]
    for step in range(2, SPLIT):
        kv[step] = exchanged(kv[step], step << 2)
    q[2:] = lax.optimization_barrier((q[2:], kv[2]))[0]
    for step in range(2, SPLIT):
        q[step] = exchanged(q[step], step << 2)

    def spread(pieces):
        block = jnp.concatenate(pieces, axis=0)
        return [block] + [exchanged(block, rest_mask(member)) for member in range(2, members, 2)]

    near = jnp.concatenate(spread(kv[:2]), axis=0)
    near = [near, exchanged(near, 1)]
    waited = [kv[2]] + lax.optimization_barrier((kv[3:], near[0]))[0]
    far = [exchanged(piece, rest_mask(member)) for piece in waited for member in range(2, members, 2)]
    held = jnp.concatenate(waited, axis=0)
    limit = pltpu.CompilerParams(vmem_limit_bytes=(12 + 2 * members // 4 * 4) * 2**20)
    queried = pl.pallas_call(
        collect_kernel,
        out_shape=jax.ShapeDtypeStruct((SPLIT * tokens, group), bf16),
        in_specs=[VMEM] * SPLIT,
        out_specs=VMEM,
        compiler_params=pltpu.CompilerParams(vmem_limit_bytes=4 * 2**20),
        cost_estimate=pl.CostEstimate(flops=5 * 10**9, bytes_accessed=10**6, transcendentals=0),
        name="collect",
    )(*q)
    state = [jax.ShapeDtypeStruct((heads, SPLIT * tokens, size), f32) for size in (wide, 2 * wide)]

    def attended(blocks, carried, last, name):
        return pl.pallas_call(
            functools.partial(attend_kernel, depth, heads, not carried, bool(last)),
            out_shape=jax.ShapeDtypeStruct((SPLIT * tokens // 2, wide), bf16) if last else state,
            in_specs=[VMEM] * (1 + len(blocks) + len(carried) + len(last)),
            out_specs=VMEM if last else [VMEM] * 2,
            compiler_params=limit,
            cost_estimate=pl.CostEstimate(flops=10**9, bytes_accessed=4 * 10**6, transcendentals=4 * 10**5),
            name=name,
        )(queried, *blocks, *carried, *last)

    carried = attended(near, [], [], "attend_near")
    beside = exchanged(held, 1)
    middle = carried
    carried = attended([held, beside], carried, [], "attend_middle")
    passed = lax.optimization_barrier((far, middle))[0]
    far = passed
    far = far + [exchanged(block, 1) for block in far]
    part = attended(far, carried, [streamed], "attend_far")

    others = [exchanged(part, step << 2) for step in (3, 2, 1)]
    patch = pl.pallas_call(
        gather_kernel,
        out_shape=jax.ShapeDtypeStruct(part.shape, bf16),
        in_specs=[VMEM] * 4,
        out_specs=VMEM,
        compiler_params=pltpu.CompilerParams(vmem_limit_bytes=4 * 2**20),
        name="gather",
    )(part, *others)
    order = sorted(range(1, members), key=lambda member: -member)
    patches = [patch] + [exchanged(patch, rest_mask(member)) for member in order]

    lane = jnp.arange(channels) // (channels // GROUPS)
    in_weight = widened(conv_in_weight)
    grouped = (lane[:, None] == lane[None, :]).astype(bf16)
    return pl.pallas_call(
        functools.partial(finish_kernel, frames, n, cols, [0] + order),
        out_shape=jax.ShapeDtypeStruct((frames, 2, 2 * cols, channels), bf16),
        in_specs=[SMEM] + [VMEM] * (members + 6),
        out_specs=VMEM,
        scratch_shapes=[
            pltpu.VMEM((frames, n + 2, cols, wide), bf16),
            pltpu.VMEM((n * cols, frames * 2 * wide), bf16),
            pltpu.VMEM((frames, n, cols, 4 * channels), f32),
            pltpu.VMEM((frames, 4, 4, cols, channels), bf16),
            pltpu.VMEM((frames, 2, channels // 128, 2 * cols, 128), f32),
        ],
        compiler_params=pltpu.CompilerParams(vmem_limit_bytes=(16 if n <= 16 else 40) * 2**20),
        name="finish",
    )(
        index,
        *patches,
        chooser(latent),
        in_weight,
        conv_mid_weight,
        grouped,
        norm_gain.reshape(1, channels),
        norm_shift.reshape(1, channels),
    )


def solution(mesh):
    placed = (
        P("groups", "seq", None, None),
        P("groups", "seq", None, None),
        P("groups", "seq", None, None),
        P("groups", "seq", None, None),
        P(),
        P(),
        P(),
        P(),
        P(),
    )
    return jax.shard_map(
        shards,
        mesh=mesh,
        in_specs=placed,
        out_specs=P("groups", "seq", None, None),
        check_vma=False,
    )
```

```python
import functools

import jax
import jax.numpy as jnp
from jax import lax
from jax.experimental import pallas as pl
from jax.experimental.pallas import tpu as pltpu
from jax.sharding import PartitionSpec as P

HEADS = 20
GROUPS = 32
SPLIT = 4
EPS = 1e-06

VMEM = pl.BlockSpec(memory_space=pltpu.VMEM)
SMEM = pl.BlockSpec(memory_space=pltpu.SMEM)
HBM = pl.BlockSpec(memory_space=pltpu.HBM)


def exchanged(value, mask):
    pairs = [(source, source ^ mask) for source in range(lax.axis_size("seq"))]
    return lax.ppermute(value, "seq", pairs)


def rest_mask(member):
    return (member & 3) | ((member >> 2) << 4)


def dot(left, right):
    return jnp.dot(left, right, preferred_element_type=jnp.float32)


def through_twice(rows, weight, columns):
    part = weight[:, columns]
    return lax.dot_general(
        rows[:, columns],
        jnp.concatenate([part, part], axis=0),
        (((1,), (1,)), ((), ())),
        preferred_element_type=jnp.float32,
    )


def prepare_kernel(depth, heads, index, q, k, v, w, *refs):
    kv_out, q_out, refs = refs[:SPLIT], refs[SPLIT : 2 * SPLIT], refs[2 * SPLIT :]
    v_here, w_here, projected, sem = refs
    tokens = q.shape[0]
    group = heads * depth
    place = (index[0] >> 2) & 3
    whole = [
        pltpu.make_async_copy(source, target, sem.at[at])
        for at, (source, target) in enumerate(((v, v_here), (w, w_here)))
    ]
    parts = []
    for step in range(SPLIT):
        columns = pl.ds(pl.multiple_of((place ^ step) * group, 128), group)
        at = len(whole) + 2 * step
        parts.append(pltpu.make_async_copy(k.at[:, columns], kv_out[step].at[:, :group], sem.at[at]))
        parts.append(pltpu.make_async_copy(q.at[:, columns], q_out[step], sem.at[at + 1]))
    for copy in whole + parts:
        copy.start()
    half = w.shape[0]
    wide = 2 * half
    pair_row = lax.broadcasted_iota(jnp.int32, (wide, 2 * depth), 0) // half
    pair_column = lax.broadcasted_iota(jnp.int32, (wide, 2 * depth), 1) // depth
    own = (pair_row == pair_column).astype(jnp.bfloat16)

    def pair_through(columns):
        weight = w_here[:, columns]
        weight = jnp.concatenate([weight, weight], axis=0) * own
        return lax.dot_general(
            v_here[:, columns], weight, (((1,), (1,)), ((), ())), preferred_element_type=jnp.float32
        )

    for copy in whole:
        copy.wait()
    for owner in range(SPLIT):
        for pair in range((heads + 1) // 2):
            at = (owner * heads + 2 * pair) * depth
            if 2 * pair + 1 < heads:
                both = pair_through(slice(at, at + 2 * depth))
            else:
                both = through_twice(v_here, w_here, slice(at, at + depth))
            projected[owner, :, pair * wide : (pair + 1) * wide] = both.astype(jnp.bfloat16)
    for step in range(SPLIT):
        kv_out[step][:, group:] = projected[place ^ step]
    for copy in parts:
        copy.wait()


def stream_kernel(s, w, out):
    out[...] = through_twice(s, w, slice(None))


def attend_kernel(depth, heads, first, last, *refs):
    q, refs = refs[0], refs[1:]
    if last:
        refs, out = refs[:-1], refs[-1]
        refs, stream = refs[:-1], refs[-1]
    else:
        refs, (top_out, mixed_out) = refs[:-2], refs[-2:]
    if first:
        kv = refs
    else:
        kv, (top_in, mixed_in) = refs[:-2], refs[-2:]
    group = heads * depth
    wide = 128
    factor = 1.4426950408889634 / depth**0.5
    rows = q.shape[0]
    tokens = rows // SPLIT
    half = rows // 2
    low = lax.broadcasted_iota(jnp.int32, (rows, wide), 1) < wide // 2
    keys = sum(piece.shape[0] for piece in kv)
    ones = jnp.ones((keys, wide), jnp.bfloat16)

    def scores_of(head):
        columns = slice(head * depth, (head + 1) * depth)
        query = q[:, columns]
        key = jnp.concatenate([piece[:, columns] for piece in kv], axis=0)
        return lax.dot_general(query, key, (((1,), (1,)), ((), ())), preferred_element_type=jnp.float32)

    summed = jnp.zeros((rows, wide), jnp.float32)
    upcoming = scores_of(0)
    for head in range(heads):
        scores = upcoming
        if head + 1 < heads:
            upcoming = scores_of(head + 1)
        top = jnp.broadcast_to(jnp.max(scores, axis=1, keepdims=True), (rows, wide))
        if not first:
            before = top_in[head]
            top = jnp.maximum(top, before)
        expo = jnp.concatenate(
            [
                jnp.exp2((scores[:, at : at + wide] - top[:, : min(wide, keys - at)]) * factor).astype(jnp.bfloat16)
                for at in range(0, keys, wide)
            ],
            axis=1,
        )
        at = group + (head // 2) * wide
        value = jnp.concatenate([piece[:, at : at + wide] for piece in kv], axis=0)
        mixed = dot(expo, jnp.concatenate([value, ones], axis=1))
        weighed, total = mixed[:, :wide], mixed[:, wide:]
        if not first:
            decay = jnp.exp2((before - top) * factor)
            weighed = weighed + mixed_in[head, :, :wide] * decay
            total = total + mixed_in[head, :, wide:] * decay
        if not last:
            top_out[head] = top
            mixed_out[head, :, :wide] = weighed
            mixed_out[head, :, wide:] = total
            continue
        mine = low if head % 2 == 0 else jnp.logical_not(low)
        summed = summed + jnp.where(mine, weighed / total, 0.0)
    if not last:
        return
    summed = summed + pltpu.roll(summed, wide // 2, 1)
    upper = summed[:half]
    upper = jnp.concatenate([upper[:tokens] + stream[...], upper[tokens:]], axis=0)
    out[...] = jnp.where(low[:half], upper, summed[half:]).astype(out.dtype)


def collect_kernel(*refs):
    pieces, out = refs[:-1], refs[-1]
    tokens = pieces[0].shape[0]
    for at, piece in zip((0, 1, 3, 2), pieces):
        out[at * tokens : (at + 1) * tokens, :] = piece[...]


def gather_kernel(own, three, two, one, out):
    rows, wide = own.shape
    half = rows // 2

    def swap_rows(x):
        return jnp.concatenate([x[half:], x[:half]], axis=0)

    own, one, two, three = (ref[...].astype(jnp.float32) for ref in (own, one, two, three))
    far = two + swap_rows(three)
    latent = (own + swap_rows(one)) + pltpu.roll(far, wide // 2, 1)
    out[...] = latent.astype(jnp.bfloat16)


def finish_kernel(frames, n, cols, order, index, *refs):
    members = n // SPLIT
    patches, refs = refs[:members], refs[members:]
    (chosen, in_weight, held, grouped, gain, shift, out, grid, stacked, first, taps, merged) = refs
    channels = gain.shape[1]
    wide = grid.shape[-1]
    half = wide // 2
    me = index[0]
    grid[:, 0] = jnp.zeros((frames, cols, wide), jnp.bfloat16)
    grid[:, n + 1] = jnp.zeros((frames, cols, wide), jnp.bfloat16)
    tokens = frames * cols
    for member in range(members):
        latent = patches[member][...].astype(jnp.float32)
        rows = latent.shape[0]
        column = lax.broadcasted_iota(jnp.int32, latent.shape, 0) % cols
        before = jnp.where(column == 0, 0.0, pltpu.roll(latent, 1, 0))
        after = jnp.where(column == cols - 1, 0.0, pltpu.roll(latent, rows - 1, 0))
        around = jnp.concatenate([before, latent, after], axis=1).astype(jnp.bfloat16)
        patch = dot(around, chosen[...]).astype(jnp.bfloat16)
        for step in range(SPLIT):
            row = me ^ (rest_mask(order[member]) | (step << 2))
            at, lanes = (step % 2) * tokens, (step // 2) * wide
            for t in range(frames):
                grid[t, row + 1] = patch[at + t * cols : at + (t + 1) * cols, lanes : lanes + wide]

    cells = n * cols
    chunk = min(cells, 256)
    rows_in = chunk // cols
    upper = lax.broadcasted_iota(jnp.int32, (rows_in, cols, wide), 2) < half
    depth = 2 * wide
    for t in range(frames):
        for r in range(0, n, rows_in):
            near = grid[t, r + 1 : r + 1 + rows_in]
            far = jnp.where(upper, grid[t, r + 2 : r + 2 + rows_in], grid[t, r : r + rows_in])
            stacked[r * cols : r * cols + chunk, t * depth : t * depth + wide] = near.reshape(chunk, wide)
            stacked[r * cols : r * cols + chunk, t * depth + wide : (t + 1) * depth] = far.reshape(chunk, wide)

    counted = 4.0 * frames * cells
    members_of = channels // GROUPS
    sums = jnp.zeros((8, channels), jnp.float32)
    squares = jnp.zeros((8, channels), jnp.float32)
    pivot = None
    for t in range(frames):
        for r in range(0, n, rows_in):
            for row in range(2):
                lanes = slice(row * 2 * channels, (row + 1) * 2 * channels)
                both = dot(
                    stacked[r * cols : r * cols + chunk, : (t + 1) * depth],
                    in_weight[(frames - 1 - t) * depth :, lanes],
                )
                first[t, r : r + rows_in, :, lanes] = both.reshape(rows_in, cols, 2 * channels)
                for here in (both[:, :channels], both[:, channels:]):
                    if pivot is None:
                        pivot = jnp.sum(here, axis=0, keepdims=True) / chunk
                    off = (here - pivot).reshape(chunk // 8, 8, channels)
                    sums = sums + jnp.sum(off, axis=0)
                    squares = squares + jnp.sum(off * off, axis=0)

    def over_group(line):
        high = line.astype(jnp.bfloat16)
        rest = line - high.astype(jnp.float32)
        middle = rest.astype(jnp.bfloat16)
        lower = (rest - middle.astype(jnp.float32)).astype(jnp.bfloat16)
        none = jnp.zeros((13, channels), jnp.bfloat16)
        terms = jnp.concatenate([high, middle, lower, none], axis=0)
        return jnp.sum(dot(terms, grouped[...])[:8], axis=0, keepdims=True)

    offset = jnp.sum(sums, axis=0, keepdims=True) / counted
    channel_mean = pivot + offset
    mean = over_group(channel_mean) / members_of
    apart = channel_mean - mean
    within = jnp.sum(squares, axis=0, keepdims=True) / counted - offset * offset
    variance = over_group(within + apart * apart) / members_of
    slope = gain[...] / jnp.sqrt(variance + EPS)
    bias = shift[...]

    place = lax.broadcasted_iota(jnp.int32, (cols, channels), 0)
    for t in range(frames):
        for line in range(4):
            sub = 1 if line in (0, 2) else 0
            token_row = me - 1 if line == 0 else (me + 1 if line == 3 else me)
            inside = jnp.logical_and(token_row >= 0, token_row < n)
            token_row = jnp.clip(token_row, 0, n - 1)
            keep = jnp.where(inside, 0.5, 0.0)
            pair = []
            for side in range(2):
                part = sub * 2 + side
                x = first[t, token_row, :, part * channels : (part + 1) * channels]
                y = (x - mean) * slope + bias
                pair.append((y * keep) * (1.0 + jnp.tanh(0.5 * y)))
            even, odd = pair
            taps[t, line, 0] = jnp.where(place == 0, 0.0, pltpu.roll(odd, 1, 0)).astype(jnp.bfloat16)
            taps[t, line, 1] = even.astype(jnp.bfloat16)
            taps[t, line, 2] = odd.astype(jnp.bfloat16)
            taps[t, line, 3] = jnp.where(place == cols - 1, 0.0, pltpu.roll(even, cols - 1, 0)).astype(jnp.bfloat16)

    here = 4 * cols
    totals = [jnp.zeros((here, channels), jnp.float32) for _ in range(frames)]
    left = jnp.concatenate(
        [taps[:, b : b + 2, w : w + 2].reshape(frames * here, channels) for b in range(3) for w in range(3)], axis=1
    )
    deep = 9 * channels
    now = held[2].reshape(deep, channels)
    then = held[1].reshape(deep, channels)
    got = dot(left, jnp.concatenate([now, then], axis=1))
    first_got = dot(left[:here], held[0].reshape(deep, channels))
    for t in range(frames):
        totals[t] = totals[t] + got[t * here : (t + 1) * here, :channels]
        if t + 1 < frames:
            totals[t + 1] = totals[t + 1] + got[t * here : (t + 1) * here, channels:]
    totals[2] = totals[2] + first_got
    for t in range(frames):
        for part in range(4):
            kept = first[t, me, :, part * channels : (part + 1) * channels]
            block = totals[t][part * cols : (part + 1) * cols] + kept
            for lane in range(channels // 128):
                tile = block[:, lane * 128 : (lane + 1) * 128]
                merged[t, part // 2, lane, pl.ds(part % 2, cols, stride=2), :] = tile
    for t in range(frames):
        for sub in range(2):
            for lane in range(channels // 128):
                out[t, sub, :, lane * 128 : (lane + 1) * 128] = merged[t, sub, lane].astype(jnp.bfloat16)


def widened(weight):
    blocks = []
    for row in range(2):
        for col in range(2):
            blocks.append(jnp.pad(weight, ((0, 0), (row, 1 - row), (col, 1 - col), (0, 0), (0, 0))))
    whole = jnp.concatenate(blocks, axis=-1)
    whole = jnp.concatenate([whole[:, 1:], whole[:, :1]], axis=1)
    return whole.reshape(-1, whole.shape[-1])


def chooser(latent):
    source = jnp.arange(3 * 8 * latent)
    target = jnp.arange(2 * 8 * latent)
    offset, lane = source // (8 * latent), source % (8 * latent)
    side, lane = lane // (4 * latent), lane % (4 * latent)
    row, col, channel = lane // (2 * latent), lane // latent % 2, lane % latent
    cell = 2 * (offset - 1) + col + 1
    to_side, to_lane = target // (8 * latent), target % (8 * latent)
    to_row, to_cell, to_channel = to_lane // (4 * latent), to_lane // latent % 4, to_lane % latent
    same = (
        (side[:, None] == to_side)
        & (row[:, None] == to_row)
        & (cell[:, None] == to_cell)
        & (channel[:, None] == to_channel)
    )
    return same.astype(jnp.bfloat16)


def shards(
    queries, keys, values, stream, head_weight, conv_in_weight, norm_gain, norm_shift, conv_mid_weight
):
    frames, _, cols, width = queries.shape
    n = lax.axis_size("seq")
    members = n // SPLIT
    depth = width // HEADS
    heads = HEADS // SPLIT
    tokens = frames * cols
    group = heads * depth
    latent = head_weight.shape[1] // 4
    wide = 2 * head_weight.shape[1]
    channels = norm_gain.shape[0]
    pairs = (heads + 1) // 2
    index = lax.axis_index("seq").astype(jnp.int32).reshape(1)
    bf16, f32 = jnp.bfloat16, jnp.float32

    head_lanes = head_weight.T
    prepared = pl.pallas_call(
        functools.partial(prepare_kernel, depth, heads),
        out_shape=[jax.ShapeDtypeStruct((tokens, group + pairs * wide), bf16)] * SPLIT
        + [jax.ShapeDtypeStruct((tokens, group), bf16)] * SPLIT,
        in_specs=[SMEM] + [HBM] * 4,
        out_specs=[VMEM] * (2 * SPLIT),
        scratch_shapes=[
            pltpu.VMEM((tokens, width), bf16),
            pltpu.VMEM((wide // 2, width), bf16),
            pltpu.VMEM((SPLIT, tokens, pairs * wide), bf16),
            pltpu.SemaphoreType.DMA((2 + 2 * SPLIT,)),
        ],
        compiler_params=pltpu.CompilerParams(vmem_limit_bytes=int(53.2 * 2**20)),
        name="prepare",
    )(
        index,
        queries.reshape(tokens, width),
        keys.reshape(tokens, width),
        values.reshape(tokens, width),
        head_lanes,
    )
    streamed = pl.pallas_call(
        stream_kernel,
        out_shape=jax.ShapeDtypeStruct((tokens, wide), f32),
        in_specs=[VMEM] * 2,
        out_specs=VMEM,
        compiler_params=pltpu.CompilerParams(vmem_limit_bytes=4 * 2**20),
        cost_estimate=pl.CostEstimate(flops=2 * 10**8, bytes_accessed=10**6, transcendentals=0),
        name="stream",
    )(stream.reshape(tokens, width), head_lanes)
    kv, q = list(prepared[:SPLIT]), list(prepared[SPLIT:])
    both = exchanged(jnp.concatenate([kv[1], q[1]], axis=1), 1 << 2)
    kv[1], q[1] = both[:, : kv[1].shape[1]], both[:, kv[1].shape[1] :]
    for step in range(2, SPLIT):
        kv[step] = exchanged(kv[step], step << 2)
    q[2:] = lax.optimization_barrier((q[2:], kv[2]))[0]
    for step in range(2, SPLIT):
        q[step] = exchanged(q[step], step << 2)

    def spread(pieces):
        block = jnp.concatenate(pieces, axis=0)
        return [block] + [exchanged(block, rest_mask(member)) for member in range(2, members, 2)]

    near = jnp.concatenate(spread(kv[:2]), axis=0)
    near = [near, exchanged(near, 1)]
    waited = [kv[2]] + lax.optimization_barrier((kv[3:], near[0]))[0]
    far = [exchanged(piece, rest_mask(member)) for piece in waited for member in range(2, members, 2)]
    held = jnp.concatenate(waited, axis=0)
    limit = pltpu.CompilerParams(vmem_limit_bytes=(12 + 2 * members // 4 * 4) * 2**20)
    queried = pl.pallas_call(
        collect_kernel,
        out_shape=jax.ShapeDtypeStruct((SPLIT * tokens, group), bf16),
        in_specs=[VMEM] * SPLIT,
        out_specs=VMEM,
        compiler_params=pltpu.CompilerParams(vmem_limit_bytes=4 * 2**20),
        cost_estimate=pl.CostEstimate(flops=5 * 10**9, bytes_accessed=10**6, transcendentals=0),
        name="collect",
    )(q[0], q[1], q[3], q[2])
    state = [jax.ShapeDtypeStruct((heads, SPLIT * tokens, size), f32) for size in (wide, 2 * wide)]

    def attended(blocks, carried, last, name):
        return pl.pallas_call(
            functools.partial(attend_kernel, depth, heads, not carried, bool(last)),
            out_shape=jax.ShapeDtypeStruct((SPLIT * tokens // 2, wide), bf16) if last else state,
            in_specs=[VMEM] * (1 + len(blocks) + len(carried) + len(last)),
            out_specs=VMEM if last else [VMEM] * 2,
            compiler_params=limit,
            cost_estimate=pl.CostEstimate(flops=10**9, bytes_accessed=4 * 10**6, transcendentals=4 * 10**5),
            name=name,
        )(queried, *blocks, *carried, *last)

    carried = attended(near, [], [], "attend_near")
    beside = exchanged(held, 1)
    middle = carried
    carried = attended([held, beside], carried, [], "attend_middle")
    passed = lax.optimization_barrier((far, middle))[0]
    far = passed
    far = far + [exchanged(block, 1) for block in far]
    part = attended(far, carried, [streamed], "attend_far")

    others = [exchanged(part, step << 2) for step in (3, 2, 1)]
    patch = pl.pallas_call(
        gather_kernel,
        out_shape=jax.ShapeDtypeStruct(part.shape, bf16),
        in_specs=[VMEM] * 4,
        out_specs=VMEM,
        compiler_params=pltpu.CompilerParams(vmem_limit_bytes=4 * 2**20),
        name="gather",
    )(part, *others)
    order = sorted(range(1, members), key=lambda member: -member)
    patches = [patch] + [exchanged(patch, rest_mask(member)) for member in order]

    lane = jnp.arange(channels) // (channels // GROUPS)
    in_weight = widened(conv_in_weight)
    grouped = (lane[:, None] == lane[None, :]).astype(bf16)
    return pl.pallas_call(
        functools.partial(finish_kernel, frames, n, cols, [0] + order),
        out_shape=jax.ShapeDtypeStruct((frames, 2, 2 * cols, channels), bf16),
        in_specs=[SMEM] + [VMEM] * (members + 6),
        out_specs=VMEM,
        scratch_shapes=[
            pltpu.VMEM((frames, n + 2, cols, wide), bf16),
            pltpu.VMEM((n * cols, frames * 2 * wide), bf16),
            pltpu.VMEM((frames, n, cols, 4 * channels), f32),
            pltpu.VMEM((frames, 4, 4, cols, channels), bf16),
            pltpu.VMEM((frames, 2, channels // 128, 2 * cols, 128), f32),
        ],
        compiler_params=pltpu.CompilerParams(vmem_limit_bytes=(16 if n <= 16 else 40) * 2**20),
        name="finish",
    )(
        index,
        *patches,
        chooser(latent),
        in_weight,
        conv_mid_weight,
        grouped,
        norm_gain.reshape(1, channels),
        norm_shift.reshape(1, channels),
    )


def solution(mesh):
    placed = (
        P("groups", "seq", None, None),
        P("groups", "seq", None, None),
        P("groups", "seq", None, None),
        P("groups", "seq", None, None),
        P(),
        P(),
        P(),
        P(),
        P(),
    )
    return jax.shard_map(
        shards,
        mesh=mesh,
        in_specs=placed,
        out_specs=P("groups", "seq", None, None),
        check_vma=False,
    )
```

```python
import functools

import jax
import jax.numpy as jnp
from jax import lax
from jax.experimental import pallas as pl
from jax.experimental.pallas import tpu as pltpu
from jax.sharding import PartitionSpec as P

HEADS = 20
GROUPS = 32
SPLIT = 4
EPS = 1e-06

VMEM = pl.BlockSpec(memory_space=pltpu.VMEM)
SMEM = pl.BlockSpec(memory_space=pltpu.SMEM)
HBM = pl.BlockSpec(memory_space=pltpu.HBM)


def exchanged(value, mask):
    pairs = [(source, source ^ mask) for source in range(lax.axis_size("seq"))]
    return lax.ppermute(value, "seq", pairs)


def rest_mask(member):
    return (member & 3) | ((member >> 2) << 4)


def dot(left, right):
    return jnp.dot(left, right, preferred_element_type=jnp.float32)


def through_twice(rows, weight, columns):
    part = weight[:, columns]
    return lax.dot_general(
        rows[:, columns],
        jnp.concatenate([part, part], axis=0),
        (((1,), (1,)), ((), ())),
        preferred_element_type=jnp.float32,
    )


def prepare_kernel(depth, heads, index, q, k, v, w, *refs):
    kv_out, q_out, refs = refs[:SPLIT], refs[SPLIT : 2 * SPLIT], refs[2 * SPLIT :]
    v_here, w_here, projected, sem = refs
    tokens = q.shape[0]
    group = heads * depth
    place = (index[0] >> 2) & 3
    whole = [
        pltpu.make_async_copy(source, target, sem.at[at])
        for at, (source, target) in enumerate(((v, v_here), (w, w_here)))
    ]
    parts = []
    for step in range(SPLIT):
        columns = pl.ds(pl.multiple_of((place ^ step) * group, 128), group)
        at = len(whole) + 2 * step
        parts.append(pltpu.make_async_copy(k.at[:, columns], kv_out[step].at[:, :group], sem.at[at]))
        parts.append(pltpu.make_async_copy(q.at[:, columns], q_out[step], sem.at[at + 1]))
    for copy in whole + parts:
        copy.start()
    half = w.shape[0]
    wide = 2 * half
    pair_row = lax.broadcasted_iota(jnp.int32, (wide, 2 * depth), 0) // half
    pair_column = lax.broadcasted_iota(jnp.int32, (wide, 2 * depth), 1) // depth
    own = (pair_row == pair_column).astype(jnp.bfloat16)

    def pair_through(columns):
        weight = w_here[:, columns]
        weight = jnp.concatenate([weight, weight], axis=0) * own
        return lax.dot_general(
            v_here[:, columns], weight, (((1,), (1,)), ((), ())), preferred_element_type=jnp.float32
        )

    for copy in whole:
        copy.wait()
    for owner in range(SPLIT):
        for pair in range((heads + 1) // 2):
            at = (owner * heads + 2 * pair) * depth
            if 2 * pair + 1 < heads:
                both = pair_through(slice(at, at + 2 * depth))
            else:
                both = through_twice(v_here, w_here, slice(at, at + depth))
            projected[owner, :, pair * wide : (pair + 1) * wide] = both.astype(jnp.bfloat16)
    for step in range(SPLIT):
        kv_out[step][:, group:] = projected[place ^ step]
    for copy in parts:
        copy.wait()


def stream_kernel(s, w, out):
    out[...] = through_twice(s, w, slice(None))


def attend_kernel(depth, heads, first, last, *refs):
    q, refs = refs[0], refs[1:]
    if last:
        refs, out = refs[:-1], refs[-1]
        refs, stream = refs[:-1], refs[-1]
    else:
        refs, (top_out, mixed_out) = refs[:-2], refs[-2:]
    if first:
        kv = refs
    else:
        kv, (top_in, mixed_in) = refs[:-2], refs[-2:]
    group = heads * depth
    wide = 128
    factor = 1.4426950408889634 / depth**0.5
    rows = q.shape[0]
    tokens = rows // SPLIT
    half = rows // 2
    low = lax.broadcasted_iota(jnp.int32, (rows, wide), 1) < wide // 2
    keys = sum(piece.shape[0] for piece in kv)
    ones = jnp.ones((keys, wide), jnp.bfloat16)

    def scores_of(head):
        columns = slice(head * depth, (head + 1) * depth)
        query = q[:, columns]
        key = jnp.concatenate([piece[:, columns] for piece in kv], axis=0)
        return lax.dot_general(query, key, (((1,), (1,)), ((), ())), preferred_element_type=jnp.float32)

    summed = jnp.zeros((rows, wide), jnp.float32)
    upcoming = scores_of(0)
    for head in range(heads):
        scores = upcoming
        if head + 1 < heads:
            upcoming = scores_of(head + 1)
        top = jnp.broadcast_to(jnp.max(scores, axis=1, keepdims=True), (rows, wide))
        if not first:
            before = top_in[head]
            top = jnp.maximum(top, before)
        expo = jnp.concatenate(
            [
                jnp.exp2((scores[:, at : at + wide] - top[:, : min(wide, keys - at)]) * factor).astype(jnp.bfloat16)
                for at in range(0, keys, wide)
            ],
            axis=1,
        )
        at = group + (head // 2) * wide
        value = jnp.concatenate([piece[:, at : at + wide] for piece in kv], axis=0)
        mixed = dot(expo, jnp.concatenate([value, ones], axis=1))
        weighed, total = mixed[:, :wide], mixed[:, wide:]
        if not first:
            decay = jnp.exp2((before - top) * factor)
            weighed = weighed + mixed_in[head, :, :wide] * decay
            total = total + mixed_in[head, :, wide:] * decay
        if not last:
            top_out[head] = top
            mixed_out[head, :, :wide] = weighed
            mixed_out[head, :, wide:] = total
            continue
        mine = low if head % 2 == 0 else jnp.logical_not(low)
        summed = summed + jnp.where(mine, weighed / total, 0.0)
    if not last:
        return
    summed = summed + pltpu.roll(summed, wide // 2, 1)
    upper = summed[:half]
    upper = jnp.concatenate([upper[:tokens] + stream[...], upper[tokens:]], axis=0)
    out[...] = jnp.where(low[:half], upper, summed[half:]).astype(out.dtype)


def collect_kernel(*refs):
    pieces, out = refs[:-1], refs[-1]
    tokens = pieces[0].shape[0]
    for at, piece in zip((0, 1, 3, 2), pieces):
        out[at * tokens : (at + 1) * tokens, :] = piece[...]


def gather_kernel(own, three, two, one, out):
    rows, wide = own.shape
    half = rows // 2

    def swap_rows(x):
        return jnp.concatenate([x[half:], x[:half]], axis=0)

    own, one, two, three = (ref[...].astype(jnp.float32) for ref in (own, one, two, three))
    far = two + swap_rows(three)
    latent = (own + swap_rows(one)) + pltpu.roll(far, wide // 2, 1)
    out[...] = latent.astype(jnp.bfloat16)


def finish_kernel(frames, n, cols, order, index, *refs):
    members = n // SPLIT
    patches, refs = refs[:members], refs[members:]
    (chosen, in_weight, held, grouped, gain, shift, out, grid, stacked, first, taps, merged) = refs
    channels = gain.shape[1]
    wide = grid.shape[-1]
    half = wide // 2
    me = index[0]
    grid[:, 0] = jnp.zeros((frames, cols, wide), jnp.bfloat16)
    grid[:, n + 1] = jnp.zeros((frames, cols, wide), jnp.bfloat16)
    tokens = frames * cols
    for member in range(members):
        latent = patches[member][...].astype(jnp.float32)
        rows = latent.shape[0]
        column = lax.broadcasted_iota(jnp.int32, latent.shape, 0) % cols
        before = jnp.where(column == 0, 0.0, pltpu.roll(latent, 1, 0))
        after = jnp.where(column == cols - 1, 0.0, pltpu.roll(latent, rows - 1, 0))
        around = jnp.concatenate([before, latent, after], axis=1).astype(jnp.bfloat16)
        patch = dot(around, chosen[...]).astype(jnp.bfloat16)
        for step in range(SPLIT):
            row = me ^ (rest_mask(order[member]) | (step << 2))
            at, lanes = (step % 2) * tokens, (step // 2) * wide
            for t in range(frames):
                grid[t, row + 1] = patch[at + t * cols : at + (t + 1) * cols, lanes : lanes + wide]

    cells = n * cols
    chunk = min(cells, 256)
    rows_in = chunk // cols
    upper = lax.broadcasted_iota(jnp.int32, (rows_in, cols, wide), 2) < half
    depth = 2 * wide
    for t in range(frames):
        for r in range(0, n, rows_in):
            near = grid[t, r + 1 : r + 1 + rows_in]
            far = jnp.where(upper, grid[t, r + 2 : r + 2 + rows_in], grid[t, r : r + rows_in])
            stacked[r * cols : r * cols + chunk, t * depth : t * depth + wide] = near.reshape(chunk, wide)
            stacked[r * cols : r * cols + chunk, t * depth + wide : (t + 1) * depth] = far.reshape(chunk, wide)

    counted = 4.0 * frames * cells
    members_of = channels // GROUPS
    sums = jnp.zeros((8, channels), jnp.float32)
    squares = jnp.zeros((8, channels), jnp.float32)
    pivot = None
    for t in range(frames):
        for r in range(0, n, rows_in):
            for row in range(2):
                lanes = slice(row * 2 * channels, (row + 1) * 2 * channels)
                both = dot(
                    stacked[r * cols : r * cols + chunk, : (t + 1) * depth],
                    in_weight[(frames - 1 - t) * depth :, lanes],
                )
                first[t, r : r + rows_in, :, lanes] = both.reshape(rows_in, cols, 2 * channels)
                for here in (both[:, :channels], both[:, channels:]):
                    if pivot is None:
                        pivot = jnp.sum(here, axis=0, keepdims=True) / chunk
                    off = (here - pivot).reshape(chunk // 8, 8, channels)
                    sums = sums + jnp.sum(off, axis=0)
                    squares = squares + jnp.sum(off * off, axis=0)

    def over_group(line):
        high = line.astype(jnp.bfloat16)
        rest = line - high.astype(jnp.float32)
        middle = rest.astype(jnp.bfloat16)
        lower = (rest - middle.astype(jnp.float32)).astype(jnp.bfloat16)
        none = jnp.zeros((13, channels), jnp.bfloat16)
        terms = jnp.concatenate([high, middle, lower, none], axis=0)
        return jnp.sum(dot(terms, grouped[...])[:8], axis=0, keepdims=True)

    offset = jnp.sum(sums, axis=0, keepdims=True) / counted
    channel_mean = pivot + offset
    mean = over_group(channel_mean) / members_of
    apart = channel_mean - mean
    within = jnp.sum(squares, axis=0, keepdims=True) / counted - offset * offset
    variance = over_group(within + apart * apart) / members_of
    slope = gain[...] / jnp.sqrt(variance + EPS)
    bias = shift[...]

    place = lax.broadcasted_iota(jnp.int32, (cols, channels), 0)
    for t in range(frames):
        for line in range(4):
            sub = 1 if line in (0, 2) else 0
            token_row = me - 1 if line == 0 else (me + 1 if line == 3 else me)
            inside = jnp.logical_and(token_row >= 0, token_row < n)
            token_row = jnp.clip(token_row, 0, n - 1)
            keep = jnp.where(inside, 0.5, 0.0)
            pair = []
            for side in range(2):
                part = sub * 2 + side
                x = first[t, token_row, :, part * channels : (part + 1) * channels]
                y = (x - mean) * slope + bias
                pair.append((y * keep) * (1.0 + jnp.tanh(0.5 * y)))
            even, odd = pair
            taps[t, line, 0] = jnp.where(place == 0, 0.0, pltpu.roll(odd, 1, 0)).astype(jnp.bfloat16)
            taps[t, line, 1] = even.astype(jnp.bfloat16)
            taps[t, line, 2] = odd.astype(jnp.bfloat16)
            taps[t, line, 3] = jnp.where(place == cols - 1, 0.0, pltpu.roll(even, cols - 1, 0)).astype(jnp.bfloat16)

    here = 4 * cols
    totals = [jnp.zeros((here, channels), jnp.float32) for _ in range(frames)]
    left = jnp.concatenate(
        [taps[:, b : b + 2, w : w + 2].reshape(frames * here, channels) for b in range(3) for w in range(3)], axis=1
    )
    deep = 9 * channels
    now = held[2].reshape(deep, channels)
    then = held[1].reshape(deep, channels)
    got = dot(left, jnp.concatenate([now, then], axis=1))
    first_got = dot(left[:here], held[0].reshape(deep, channels))
    for t in range(frames):
        totals[t] = totals[t] + got[t * here : (t + 1) * here, :channels]
        if t + 1 < frames:
            totals[t + 1] = totals[t + 1] + got[t * here : (t + 1) * here, channels:]
    totals[2] = totals[2] + first_got
    for t in range(frames):
        for part in range(4):
            kept = first[t, me, :, part * channels : (part + 1) * channels]
            block = totals[t][part * cols : (part + 1) * cols] + kept
            for lane in range(channels // 128):
                tile = block[:, lane * 128 : (lane + 1) * 128]
                merged[t, part // 2, lane, pl.ds(part % 2, cols, stride=2), :] = tile
    for t in range(frames):
        for sub in range(2):
            for lane in range(channels // 128):
                out[t, sub, :, lane * 128 : (lane + 1) * 128] = merged[t, sub, lane].astype(jnp.bfloat16)


def widened(weight):
    blocks = []
    for row in range(2):
        for col in range(2):
            blocks.append(jnp.pad(weight, ((0, 0), (row, 1 - row), (col, 1 - col), (0, 0), (0, 0))))
    whole = jnp.concatenate(blocks, axis=-1)
    whole = jnp.concatenate([whole[:, 1:], whole[:, :1]], axis=1)
    return whole.reshape(-1, whole.shape[-1])


def chooser(latent):
    source = jnp.arange(3 * 8 * latent)
    target = jnp.arange(2 * 8 * latent)
    offset, lane = source // (8 * latent), source % (8 * latent)
    side, lane = lane // (4 * latent), lane % (4 * latent)
    row, col, channel = lane // (2 * latent), lane // latent % 2, lane % latent
    cell = 2 * (offset - 1) + col + 1
    to_side, to_lane = target // (8 * latent), target % (8 * latent)
    to_row, to_cell, to_channel = to_lane // (4 * latent), to_lane // latent % 4, to_lane % latent
    same = (
        (side[:, None] == to_side)
        & (row[:, None] == to_row)
        & (cell[:, None] == to_cell)
        & (channel[:, None] == to_channel)
    )
    return same.astype(jnp.bfloat16)


def shards(
    queries, keys, values, stream, head_weight, conv_in_weight, norm_gain, norm_shift, conv_mid_weight
):
    frames, _, cols, width = queries.shape
    n = lax.axis_size("seq")
    members = n // SPLIT
    depth = width // HEADS
    heads = HEADS // SPLIT
    tokens = frames * cols
    group = heads * depth
    latent = head_weight.shape[1] // 4
    wide = 2 * head_weight.shape[1]
    channels = norm_gain.shape[0]
    pairs = (heads + 1) // 2
    index = lax.axis_index("seq").astype(jnp.int32).reshape(1)
    bf16, f32 = jnp.bfloat16, jnp.float32

    head_lanes = head_weight.T
    prepared = pl.pallas_call(
        functools.partial(prepare_kernel, depth, heads),
        out_shape=[jax.ShapeDtypeStruct((tokens, group + pairs * wide), bf16)] * SPLIT
        + [jax.ShapeDtypeStruct((tokens, group), bf16)] * SPLIT,
        in_specs=[SMEM] + [HBM] * 4,
        out_specs=[VMEM] * (2 * SPLIT),
        scratch_shapes=[
            pltpu.VMEM((tokens, width), bf16),
            pltpu.VMEM((wide // 2, width), bf16),
            pltpu.VMEM((SPLIT, tokens, pairs * wide), bf16),
            pltpu.SemaphoreType.DMA((2 + 2 * SPLIT,)),
        ],
        compiler_params=pltpu.CompilerParams(vmem_limit_bytes=int(53.2 * 2**20)),
        name="prepare",
    )(
        index,
        queries.reshape(tokens, width),
        keys.reshape(tokens, width),
        values.reshape(tokens, width),
        head_lanes,
    )
    streamed = pl.pallas_call(
        stream_kernel,
        out_shape=jax.ShapeDtypeStruct((tokens, wide), f32),
        in_specs=[VMEM] * 2,
        out_specs=VMEM,
        compiler_params=pltpu.CompilerParams(vmem_limit_bytes=4 * 2**20),
        cost_estimate=pl.CostEstimate(flops=2 * 10**8, bytes_accessed=10**6, transcendentals=0),
        name="stream",
    )(stream.reshape(tokens, width), head_lanes)
    kv, q = list(prepared[:SPLIT]), list(prepared[SPLIT:])
    both = exchanged(jnp.concatenate([kv[1], q[1]], axis=1), 1 << 2)
    kv[1], q[1] = both[:, : kv[1].shape[1]], both[:, kv[1].shape[1] :]
    for step in range(2, SPLIT):
        kv[step] = exchanged(kv[step], step << 2)
    q[2:] = lax.optimization_barrier((q[2:], kv[2]))[0]
    for step in range(2, SPLIT):
        q[step] = exchanged(q[step], step << 2)

    def spread(pieces):
        block = jnp.concatenate(pieces, axis=0)
        return [block] + [exchanged(block, rest_mask(member)) for member in range(2, members, 2)]

    near = jnp.concatenate(spread(kv[:2]), axis=0)
    near = [near, exchanged(near, 1)]
    waited = [kv[2]] + lax.optimization_barrier((kv[3:], near[0]))[0]
    far = [exchanged(piece, rest_mask(member)) for piece in waited for member in range(2, members, 2)]
    held = jnp.concatenate(waited, axis=0)
    limit = pltpu.CompilerParams(vmem_limit_bytes=(12 + 2 * members // 4 * 4) * 2**20)
    queried = pl.pallas_call(
        collect_kernel,
        out_shape=jax.ShapeDtypeStruct((SPLIT * tokens, group), bf16),
        in_specs=[VMEM] * SPLIT,
        out_specs=VMEM,
        compiler_params=pltpu.CompilerParams(vmem_limit_bytes=4 * 2**20),
        cost_estimate=pl.CostEstimate(flops=5 * 10**9, bytes_accessed=10**6, transcendentals=0),
        name="collect",
    )(q[0], q[1], q[3], q[2])
    state = [jax.ShapeDtypeStruct((heads, SPLIT * tokens, size), f32) for size in (wide, 2 * wide)]

    def attended(blocks, carried, last, name):
        return pl.pallas_call(
            functools.partial(attend_kernel, depth, heads, not carried, bool(last)),
            out_shape=jax.ShapeDtypeStruct((SPLIT * tokens // 2, wide), bf16) if last else state,
            in_specs=[VMEM] * (1 + len(blocks) + len(carried) + len(last)),
            out_specs=VMEM if last else [VMEM] * 2,
            compiler_params=limit,
            cost_estimate=pl.CostEstimate(flops={'attend_near': 100000000, 'attend_middle': 100000000, 'attend_far': 100000000}[name], bytes_accessed=10**5, transcendentals=0),
            name=name,
        )(queried, *blocks, *carried, *last)

    carried = attended(near, [], [], "attend_near")
    beside = exchanged(held, 1)
    some = len(far) // 2
    passed = far[:some] + lax.optimization_barrier((far[some:], carried))[0]
    crossed = [exchanged(block, 1) for block in passed]
    some = len(passed) // 2
    carried = attended([held, beside] + passed[:some] + crossed[:some], carried, [], "attend_middle")
    part = attended(passed[some:] + crossed[some:], carried, [streamed], "attend_far")

    others = [exchanged(part, step << 2) for step in (3, 2, 1)]
    patch = pl.pallas_call(
        gather_kernel,
        out_shape=jax.ShapeDtypeStruct(part.shape, bf16),
        in_specs=[VMEM] * 4,
        out_specs=VMEM,
        compiler_params=pltpu.CompilerParams(vmem_limit_bytes=4 * 2**20),
        name="gather",
    )(part, *others)
    order = sorted(range(1, members), key=lambda member: -member)
    patches = [patch] + [exchanged(patch, rest_mask(member)) for member in order]

    lane = jnp.arange(channels) // (channels // GROUPS)
    in_weight = widened(conv_in_weight)
    grouped = (lane[:, None] == lane[None, :]).astype(bf16)
    return pl.pallas_call(
        functools.partial(finish_kernel, frames, n, cols, [0] + order),
        out_shape=jax.ShapeDtypeStruct((frames, 2, 2 * cols, channels), bf16),
        in_specs=[SMEM] + [VMEM] * (members + 6),
        out_specs=VMEM,
        scratch_shapes=[
            pltpu.VMEM((frames, n + 2, cols, wide), bf16),
            pltpu.VMEM((n * cols, frames * 2 * wide), bf16),
            pltpu.VMEM((frames, n, cols, 4 * channels), f32),
            pltpu.VMEM((frames, 4, 4, cols, channels), bf16),
            pltpu.VMEM((frames, 2, channels // 128, 2 * cols, 128), f32),
        ],
        compiler_params=pltpu.CompilerParams(vmem_limit_bytes=(16 if n <= 16 else 40) * 2**20),
        name="finish",
    )(
        index,
        *patches,
        chooser(latent),
        in_weight,
        conv_mid_weight,
        grouped,
        norm_gain.reshape(1, channels),
        norm_shift.reshape(1, channels),
    )


def solution(mesh):
    placed = (
        P("groups", "seq", None, None),
        P("groups", "seq", None, None),
        P("groups", "seq", None, None),
        P("groups", "seq", None, None),
        P(),
        P(),
        P(),
        P(),
        P(),
    )
    return jax.shard_map(
        shards,
        mesh=mesh,
        in_specs=placed,
        out_specs=P("groups", "seq", None, None),
        check_vma=False,
    )
```

```python
import functools

import jax
import jax.numpy as jnp
from jax import lax
from jax.experimental import pallas as pl
from jax.experimental.pallas import tpu as pltpu
from jax.sharding import PartitionSpec as P

HEADS = 20
GROUPS = 32
SPLIT = 4
EPS = 1e-06

VMEM = pl.BlockSpec(memory_space=pltpu.VMEM)
SMEM = pl.BlockSpec(memory_space=pltpu.SMEM)
HBM = pl.BlockSpec(memory_space=pltpu.HBM)


def exchanged(value, mask):
    pairs = [(source, source ^ mask) for source in range(lax.axis_size("seq"))]
    return lax.ppermute(value, "seq", pairs)


def rest_mask(member):
    return (member & 3) | ((member >> 2) << 4)


def dot(left, right):
    return jnp.dot(left, right, preferred_element_type=jnp.float32)


def through_twice(rows, weight, columns):
    part = weight[:, columns]
    return lax.dot_general(
        rows[:, columns],
        jnp.concatenate([part, part], axis=0),
        (((1,), (1,)), ((), ())),
        preferred_element_type=jnp.float32,
    )


def prepare_kernel(depth, heads, index, q, k, v, w, *refs):
    kv_out, q_out, refs = refs[:SPLIT], refs[SPLIT : 2 * SPLIT], refs[2 * SPLIT :]
    v_here, w_here, projected, sem = refs
    tokens = q.shape[0]
    group = heads * depth
    place = (index[0] >> 2) & 3
    whole = [
        pltpu.make_async_copy(source, target, sem.at[at])
        for at, (source, target) in enumerate(((v, v_here), (w, w_here)))
    ]
    parts = []
    for step in range(SPLIT):
        columns = pl.ds(pl.multiple_of((place ^ step) * group, 128), group)
        at = len(whole) + 2 * step
        parts.append(pltpu.make_async_copy(k.at[:, columns], kv_out[step].at[:, :group], sem.at[at]))
        parts.append(pltpu.make_async_copy(q.at[:, columns], q_out[step], sem.at[at + 1]))
    for copy in whole + parts:
        copy.start()
    half = w.shape[0]
    wide = 2 * half
    pair_row = lax.broadcasted_iota(jnp.int32, (wide, 2 * depth), 0) // half
    pair_column = lax.broadcasted_iota(jnp.int32, (wide, 2 * depth), 1) // depth
    own = (pair_row == pair_column).astype(jnp.bfloat16)

    def pair_through(columns):
        weight = w_here[:, columns]
        weight = jnp.concatenate([weight, weight], axis=0) * own
        return lax.dot_general(
            v_here[:, columns], weight, (((1,), (1,)), ((), ())), preferred_element_type=jnp.float32
        )

    for copy in whole:
        copy.wait()
    for owner in range(SPLIT):
        for pair in range((heads + 1) // 2):
            at = (owner * heads + 2 * pair) * depth
            if 2 * pair + 1 < heads:
                both = pair_through(slice(at, at + 2 * depth))
            else:
                both = through_twice(v_here, w_here, slice(at, at + depth))
            projected[owner, :, pair * wide : (pair + 1) * wide] = both.astype(jnp.bfloat16)
    for step in range(SPLIT):
        kv_out[step][:, group:] = projected[place ^ step]
    for copy in parts:
        copy.wait()


def stream_kernel(s, w, out):
    out[...] = through_twice(s, w, slice(None))


def attend_kernel(depth, heads, first, last, *refs):
    q, refs = refs[0], refs[1:]
    if last:
        refs, out = refs[:-1], refs[-1]
        refs, stream = refs[:-1], refs[-1]
    else:
        refs, (top_out, mixed_out) = refs[:-2], refs[-2:]
    if first:
        kv = refs
    else:
        kv, (top_in, mixed_in) = refs[:-2], refs[-2:]
    group = heads * depth
    wide = 128
    factor = 1.4426950408889634 / depth**0.5
    rows = q.shape[0]
    tokens = rows // SPLIT
    half = rows // 2
    low = lax.broadcasted_iota(jnp.int32, (rows, wide), 1) < wide // 2
    keys = sum(piece.shape[0] for piece in kv)
    ones = jnp.ones((keys, wide), jnp.bfloat16)

    def scores_of(head):
        columns = slice(head * depth, (head + 1) * depth)
        query = q[:, columns]
        key = jnp.concatenate([piece[:, columns] for piece in kv], axis=0)
        return lax.dot_general(query, key, (((1,), (1,)), ((), ())), preferred_element_type=jnp.float32)

    summed = jnp.zeros((rows, wide), jnp.float32)
    upcoming = scores_of(0)
    for head in range(heads):
        scores = upcoming
        if head + 1 < heads:
            upcoming = scores_of(head + 1)
        top = jnp.broadcast_to(jnp.max(scores, axis=1, keepdims=True), (rows, wide))
        if not first:
            before = top_in[head]
            top = jnp.maximum(top, before)
        expo = jnp.concatenate(
            [
                jnp.exp2((scores[:, at : at + wide] - top[:, : min(wide, keys - at)]) * factor).astype(jnp.bfloat16)
                for at in range(0, keys, wide)
            ],
            axis=1,
        )
        at = group + (head // 2) * wide
        value = jnp.concatenate([piece[:, at : at + wide] for piece in kv], axis=0)
        mixed = dot(expo, jnp.concatenate([value, ones], axis=1))
        weighed, total = mixed[:, :wide], mixed[:, wide:]
        if not first:
            decay = jnp.exp2((before - top) * factor)
            weighed = weighed + mixed_in[head, :, :wide] * decay
            total = total + mixed_in[head, :, wide:] * decay
        if not last:
            top_out[head] = top
            mixed_out[head, :, :wide] = weighed
            mixed_out[head, :, wide:] = total
            continue
        mine = low if head % 2 == 0 else jnp.logical_not(low)
        summed = summed + jnp.where(mine, weighed / total, 0.0)
    if not last:
        return
    summed = summed + pltpu.roll(summed, wide // 2, 1)
    upper = summed[:half]
    upper = jnp.concatenate([upper[:tokens] + stream[...], upper[tokens:]], axis=0)
    out[...] = jnp.where(low[:half], upper, summed[half:]).astype(out.dtype)


def collect_kernel(*refs):
    pieces, out = refs[:-1], refs[-1]
    tokens = pieces[0].shape[0]
    for at, piece in zip((0, 1, 3, 2), pieces):
        out[at * tokens : (at + 1) * tokens, :] = piece[...]


def gather_kernel(own, three, two, one, out):
    rows, wide = own.shape
    half = rows // 2

    def swap_rows(x):
        return jnp.concatenate([x[half:], x[:half]], axis=0)

    own, one, two, three = (ref[...].astype(jnp.float32) for ref in (own, one, two, three))
    far = two + swap_rows(three)
    latent = (own + swap_rows(one)) + pltpu.roll(far, wide // 2, 1)
    out[...] = latent.astype(jnp.bfloat16)


def finish_kernel(frames, n, cols, order, index, *refs):
    members = n // SPLIT
    patches, refs = refs[:members], refs[members:]
    (chosen, in_weight, held, grouped, gain, shift, out, grid, stacked, first, taps, merged) = refs
    channels = gain.shape[1]
    wide = grid.shape[-1]
    half = wide // 2
    me = index[0]
    grid[:, 0] = jnp.zeros((frames, cols, wide), jnp.bfloat16)
    grid[:, n + 1] = jnp.zeros((frames, cols, wide), jnp.bfloat16)
    tokens = frames * cols
    for member in range(members):
        latent = patches[member][...].astype(jnp.float32)
        rows = latent.shape[0]
        column = lax.broadcasted_iota(jnp.int32, latent.shape, 0) % cols
        before = jnp.where(column == 0, 0.0, pltpu.roll(latent, 1, 0))
        after = jnp.where(column == cols - 1, 0.0, pltpu.roll(latent, rows - 1, 0))
        around = jnp.concatenate([before, latent, after], axis=1).astype(jnp.bfloat16)
        patch = dot(around, chosen[...]).astype(jnp.bfloat16)
        for step in range(SPLIT):
            row = me ^ (rest_mask(order[member]) | (step << 2))
            at, lanes = (step % 2) * tokens, (step // 2) * wide
            for t in range(frames):
                grid[t, row + 1] = patch[at + t * cols : at + (t + 1) * cols, lanes : lanes + wide]

    cells = n * cols
    chunk = min(cells, 256)
    rows_in = chunk // cols
    upper = lax.broadcasted_iota(jnp.int32, (rows_in, cols, wide), 2) < half
    depth = 2 * wide
    for t in range(frames):
        for r in range(0, n, rows_in):
            near = grid[t, r + 1 : r + 1 + rows_in]
            far = jnp.where(upper, grid[t, r + 2 : r + 2 + rows_in], grid[t, r : r + rows_in])
            stacked[r * cols : r * cols + chunk, t * depth : t * depth + wide] = near.reshape(chunk, wide)
            stacked[r * cols : r * cols + chunk, t * depth + wide : (t + 1) * depth] = far.reshape(chunk, wide)

    counted = 4.0 * frames * cells
    members_of = channels // GROUPS
    sums = jnp.zeros((8, channels), jnp.float32)
    squares = jnp.zeros((8, channels), jnp.float32)
    pivot = None
    for t in range(frames):
        for r in range(0, n, rows_in):
            for row in range(2):
                lanes = slice(row * 2 * channels, (row + 1) * 2 * channels)
                both = dot(
                    stacked[r * cols : r * cols + chunk, : (t + 1) * depth],
                    in_weight[(frames - 1 - t) * depth :, lanes],
                )
                first[t, r : r + rows_in, :, lanes] = both.reshape(rows_in, cols, 2 * channels)
                for here in (both[:, :channels], both[:, channels:]):
                    if pivot is None:
                        pivot = jnp.sum(here, axis=0, keepdims=True) / chunk
                    off = (here - pivot).reshape(chunk // 8, 8, channels)
                    sums = sums + jnp.sum(off, axis=0)
                    squares = squares + jnp.sum(off * off, axis=0)

    def over_group(line):
        high = line.astype(jnp.bfloat16)
        rest = line - high.astype(jnp.float32)
        middle = rest.astype(jnp.bfloat16)
        lower = (rest - middle.astype(jnp.float32)).astype(jnp.bfloat16)
        none = jnp.zeros((13, channels), jnp.bfloat16)
        terms = jnp.concatenate([high, middle, lower, none], axis=0)
        return jnp.sum(dot(terms, grouped[...])[:8], axis=0, keepdims=True)

    offset = jnp.sum(sums, axis=0, keepdims=True) / counted
    channel_mean = pivot + offset
    mean = over_group(channel_mean) / members_of
    apart = channel_mean - mean
    within = jnp.sum(squares, axis=0, keepdims=True) / counted - offset * offset
    variance = over_group(within + apart * apart) / members_of
    slope = gain[...] / jnp.sqrt(variance + EPS)
    bias = shift[...]

    place = lax.broadcasted_iota(jnp.int32, (cols, channels), 0)
    for t in range(frames):
        for line in range(4):
            sub = 1 if line in (0, 2) else 0
            token_row = me - 1 if line == 0 else (me + 1 if line == 3 else me)
            inside = jnp.logical_and(token_row >= 0, token_row < n)
            token_row = jnp.clip(token_row, 0, n - 1)
            keep = jnp.where(inside, 0.5, 0.0)
            pair = []
            for side in range(2):
                part = sub * 2 + side
                x = first[t, token_row, :, part * channels : (part + 1) * channels]
                y = (x - mean) * slope + bias
                pair.append((y * keep) * (1.0 + jnp.tanh(0.5 * y)))
            even, odd = pair
            taps[t, line, 0] = jnp.where(place == 0, 0.0, pltpu.roll(odd, 1, 0)).astype(jnp.bfloat16)
            taps[t, line, 1] = even.astype(jnp.bfloat16)
            taps[t, line, 2] = odd.astype(jnp.bfloat16)
            taps[t, line, 3] = jnp.where(place == cols - 1, 0.0, pltpu.roll(even, cols - 1, 0)).astype(jnp.bfloat16)

    here = 4 * cols
    totals = [jnp.zeros((here, channels), jnp.float32) for _ in range(frames)]
    left = jnp.concatenate(
        [taps[:, b : b + 2, w : w + 2].reshape(frames * here, channels) for b in range(3) for w in range(3)], axis=1
    )
    deep = 9 * channels
    now = held[2].reshape(deep, channels)
    then = held[1].reshape(deep, channels)
    got = dot(left, jnp.concatenate([now, then], axis=1))
    first_got = dot(left[:here], held[0].reshape(deep, channels))
    for t in range(frames):
        totals[t] = totals[t] + got[t * here : (t + 1) * here, :channels]
        if t + 1 < frames:
            totals[t + 1] = totals[t + 1] + got[t * here : (t + 1) * here, channels:]
    totals[2] = totals[2] + first_got
    for t in range(frames):
        for part in range(4):
            kept = first[t, me, :, part * channels : (part + 1) * channels]
            block = totals[t][part * cols : (part + 1) * cols] + kept
            for lane in range(channels // 128):
                tile = block[:, lane * 128 : (lane + 1) * 128]
                merged[t, part // 2, lane, pl.ds(part % 2, cols, stride=2), :] = tile
    for t in range(frames):
        for sub in range(2):
            for lane in range(channels // 128):
                out[t, sub, :, lane * 128 : (lane + 1) * 128] = merged[t, sub, lane].astype(jnp.bfloat16)


def widened(weight):
    blocks = []
    for row in range(2):
        for col in range(2):
            blocks.append(jnp.pad(weight, ((0, 0), (row, 1 - row), (col, 1 - col), (0, 0), (0, 0))))
    whole = jnp.concatenate(blocks, axis=-1)
    whole = jnp.concatenate([whole[:, 1:], whole[:, :1]], axis=1)
    return whole.reshape(-1, whole.shape[-1])


def chooser(latent):
    source = jnp.arange(3 * 8 * latent)
    target = jnp.arange(2 * 8 * latent)
    offset, lane = source // (8 * latent), source % (8 * latent)
    side, lane = lane // (4 * latent), lane % (4 * latent)
    row, col, channel = lane // (2 * latent), lane // latent % 2, lane % latent
    cell = 2 * (offset - 1) + col + 1
    to_side, to_lane = target // (8 * latent), target % (8 * latent)
    to_row, to_cell, to_channel = to_lane // (4 * latent), to_lane // latent % 4, to_lane % latent
    same = (
        (side[:, None] == to_side)
        & (row[:, None] == to_row)
        & (cell[:, None] == to_cell)
        & (channel[:, None] == to_channel)
    )
    return same.astype(jnp.bfloat16)


def shards(
    queries, keys, values, stream, head_weight, conv_in_weight, norm_gain, norm_shift, conv_mid_weight
):
    frames, _, cols, width = queries.shape
    n = lax.axis_size("seq")
    members = n // SPLIT
    depth = width // HEADS
    heads = HEADS // SPLIT
    tokens = frames * cols
    group = heads * depth
    latent = head_weight.shape[1] // 4
    wide = 2 * head_weight.shape[1]
    channels = norm_gain.shape[0]
    pairs = (heads + 1) // 2
    index = lax.axis_index("seq").astype(jnp.int32).reshape(1)
    bf16, f32 = jnp.bfloat16, jnp.float32

    head_lanes = head_weight.T
    prepared = pl.pallas_call(
        functools.partial(prepare_kernel, depth, heads),
        out_shape=[jax.ShapeDtypeStruct((tokens, group + pairs * wide), bf16)] * SPLIT
        + [jax.ShapeDtypeStruct((tokens, group), bf16)] * SPLIT,
        in_specs=[SMEM] + [HBM] * 4,
        out_specs=[VMEM] * (2 * SPLIT),
        scratch_shapes=[
            pltpu.VMEM((tokens, width), bf16),
            pltpu.VMEM((wide // 2, width), bf16),
            pltpu.VMEM((SPLIT, tokens, pairs * wide), bf16),
            pltpu.SemaphoreType.DMA((2 + 2 * SPLIT,)),
        ],
        compiler_params=pltpu.CompilerParams(vmem_limit_bytes=int(53.2 * 2**20)),
        name="prepare",
    )(
        index,
        queries.reshape(tokens, width),
        keys.reshape(tokens, width),
        values.reshape(tokens, width),
        head_lanes,
    )
    streamed = pl.pallas_call(
        stream_kernel,
        out_shape=jax.ShapeDtypeStruct((tokens, wide), f32),
        in_specs=[VMEM] * 2,
        out_specs=VMEM,
        compiler_params=pltpu.CompilerParams(vmem_limit_bytes=4 * 2**20),
        cost_estimate=pl.CostEstimate(flops=2 * 10**8, bytes_accessed=10**6, transcendentals=0),
        name="stream",
    )(stream.reshape(tokens, width), head_lanes)
    kv, q = list(prepared[:SPLIT]), list(prepared[SPLIT:])
    both = exchanged(jnp.concatenate([kv[1], q[1]], axis=1), 1 << 2)
    kv[1], q[1] = both[:, : kv[1].shape[1]], both[:, kv[1].shape[1] :]
    for step in range(2, SPLIT):
        kv[step] = exchanged(kv[step], step << 2)
    q[2:] = lax.optimization_barrier((q[2:], kv[2]))[0]
    for step in range(2, SPLIT):
        q[step] = exchanged(q[step], step << 2)

    def spread(pieces):
        block = jnp.concatenate(pieces, axis=0)
        return [block] + [exchanged(block, rest_mask(member)) for member in range(2, members, 2)]

    near = jnp.concatenate(spread(kv[:2]), axis=0)
    near = [near, exchanged(near, 1)]
    waited = [kv[2]] + lax.optimization_barrier((kv[3:], near[0]))[0]
    far = [exchanged(piece, rest_mask(member)) for piece in waited for member in range(2, members, 2)]
    held = jnp.concatenate(waited, axis=0)
    limit = pltpu.CompilerParams(vmem_limit_bytes=(12 + 2 * members // 4 * 4) * 2**20)
    queried = pl.pallas_call(
        collect_kernel,
        out_shape=jax.ShapeDtypeStruct((SPLIT * tokens, group), bf16),
        in_specs=[VMEM] * SPLIT,
        out_specs=VMEM,
        compiler_params=pltpu.CompilerParams(vmem_limit_bytes=4 * 2**20),
        cost_estimate=pl.CostEstimate(flops=5 * 10**9, bytes_accessed=10**6, transcendentals=0),
        name="collect",
    )(q[0], q[1], q[3], q[2])
    state = [jax.ShapeDtypeStruct((heads, SPLIT * tokens, size), f32) for size in (wide, 2 * wide)]

    def attended(blocks, carried, last, name):
        return pl.pallas_call(
            functools.partial(attend_kernel, depth, heads, not carried, bool(last)),
            out_shape=jax.ShapeDtypeStruct((SPLIT * tokens // 2, wide), bf16) if last else state,
            in_specs=[VMEM] * (1 + len(blocks) + len(carried) + len(last)),
            out_specs=VMEM if last else [VMEM] * 2,
            compiler_params=limit,
            cost_estimate=pl.CostEstimate(flops=10**8, bytes_accessed=10**5, transcendentals=0),
            name=name,
        )(queried, *blocks, *carried, *last)

    carried = attended(near, [], [], "attend_near")
    beside = exchanged(held, 1)
    middle = carried
    carried = attended([held, beside], carried, [], "attend_middle")
    passed = lax.optimization_barrier((far, middle))[0]
    far = passed
    far = far + [exchanged(block, 1) for block in far]
    part = attended(far, carried, [streamed], "attend_far")

    others = [exchanged(part, step << 2) for step in (3, 2, 1)]
    patch = pl.pallas_call(
        gather_kernel,
        out_shape=jax.ShapeDtypeStruct(part.shape, bf16),
        in_specs=[VMEM] * 4,
        out_specs=VMEM,
        compiler_params=pltpu.CompilerParams(vmem_limit_bytes=4 * 2**20),
        name="gather",
    )(part, *others)
    order = sorted(range(1, members), key=lambda member: -member)
    patches = [patch] + [exchanged(patch, rest_mask(member)) for member in order]

    lane = jnp.arange(channels) // (channels // GROUPS)
    in_weight = widened(conv_in_weight)
    grouped = (lane[:, None] == lane[None, :]).astype(bf16)
    return pl.pallas_call(
        functools.partial(finish_kernel, frames, n, cols, [0] + order),
        out_shape=jax.ShapeDtypeStruct((frames, 2, 2 * cols, channels), bf16),
        in_specs=[SMEM] + [VMEM] * (members + 6),
        out_specs=VMEM,
        scratch_shapes=[
            pltpu.VMEM((frames, n + 2, cols, wide), bf16),
            pltpu.VMEM((n * cols, frames * 2 * wide), bf16),
            pltpu.VMEM((frames, n, cols, 4 * channels), f32),
            pltpu.VMEM((frames, 4, 4, cols, channels), bf16),
            pltpu.VMEM((frames, 2, channels // 128, 2 * cols, 128), f32),
        ],
        compiler_params=pltpu.CompilerParams(vmem_limit_bytes=(16 if n <= 16 else 40) * 2**20),
        name="finish",
    )(
        index,
        *patches,
        chooser(latent),
        in_weight,
        conv_mid_weight,
        grouped,
        norm_gain.reshape(1, channels),
        norm_shift.reshape(1, channels),
    )


def solution(mesh):
    placed = (
        P("groups", "seq", None, None),
        P("groups", "seq", None, None),
        P("groups", "seq", None, None),
        P("groups", "seq", None, None),
        P(),
        P(),
        P(),
        P(),
        P(),
    )
    return jax.shard_map(
        shards,
        mesh=mesh,
        in_specs=placed,
        out_specs=P("groups", "seq", None, None),
        check_vma=False,
    )
```

```python
import functools

import jax
import jax.numpy as jnp
from jax import lax
from jax.experimental import pallas as pl
from jax.experimental.pallas import tpu as pltpu
from jax.sharding import PartitionSpec as P

HEADS = 20
GROUPS = 32
SPLIT = 4
EPS = 1e-06

VMEM = pl.BlockSpec(memory_space=pltpu.VMEM)
SMEM = pl.BlockSpec(memory_space=pltpu.SMEM)
HBM = pl.BlockSpec(memory_space=pltpu.HBM)


def exchanged(value, mask):
    pairs = [(source, source ^ mask) for source in range(lax.axis_size("seq"))]
    return lax.ppermute(value, "seq", pairs)


def rest_mask(member):
    return (member & 3) | ((member >> 2) << 4)


def dot(left, right):
    return jnp.dot(left, right, preferred_element_type=jnp.float32)


def through_twice(rows, weight, columns):
    part = weight[:, columns]
    return lax.dot_general(
        rows[:, columns],
        jnp.concatenate([part, part], axis=0),
        (((1,), (1,)), ((), ())),
        preferred_element_type=jnp.float32,
    )


def prepare_kernel(depth, heads, index, q, k, v, w, *refs):
    kv_out, q_out, refs = refs[:SPLIT], refs[SPLIT : 2 * SPLIT], refs[2 * SPLIT :]
    v_here, w_here, projected, sem = refs
    tokens = q.shape[0]
    group = heads * depth
    place = (index[0] >> 2) & 3
    whole = [
        pltpu.make_async_copy(source, target, sem.at[at])
        for at, (source, target) in enumerate(((v, v_here), (w, w_here)))
    ]
    parts = []
    for step in range(SPLIT):
        columns = pl.ds(pl.multiple_of((place ^ step) * group, 128), group)
        at = len(whole) + 2 * step
        parts.append(pltpu.make_async_copy(k.at[:, columns], kv_out[step].at[:, :group], sem.at[at]))
        parts.append(pltpu.make_async_copy(q.at[:, columns], q_out[step], sem.at[at + 1]))
    for copy in whole + parts:
        copy.start()
    half = w.shape[0]
    wide = 2 * half
    pair_row = lax.broadcasted_iota(jnp.int32, (wide, 2 * depth), 0) // half
    pair_column = lax.broadcasted_iota(jnp.int32, (wide, 2 * depth), 1) // depth
    own = (pair_row == pair_column).astype(jnp.bfloat16)

    def pair_through(columns):
        weight = w_here[:, columns]
        weight = jnp.concatenate([weight, weight], axis=0) * own
        return lax.dot_general(
            v_here[:, columns], weight, (((1,), (1,)), ((), ())), preferred_element_type=jnp.float32
        )

    for copy in whole:
        copy.wait()
    for owner in range(SPLIT):
        for pair in range((heads + 1) // 2):
            at = (owner * heads + 2 * pair) * depth
            if 2 * pair + 1 < heads:
                both = pair_through(slice(at, at + 2 * depth))
            else:
                both = through_twice(v_here, w_here, slice(at, at + depth))
            projected[owner, :, pair * wide : (pair + 1) * wide] = both.astype(jnp.bfloat16)
    for step in range(SPLIT):
        kv_out[step][:, group:] = projected[place ^ step]
    for copy in parts:
        copy.wait()


def stream_kernel(s, w, out):
    out[...] = through_twice(s, w, slice(None))


def attend_kernel(depth, heads, first, last, *refs):
    q, refs = refs[0], refs[1:]
    if last:
        refs, out = refs[:-1], refs[-1]
        refs, stream = refs[:-1], refs[-1]
    else:
        refs, (top_out, mixed_out) = refs[:-2], refs[-2:]
    if first:
        kv = refs
    else:
        kv, (top_in, mixed_in) = refs[:-2], refs[-2:]
    group = heads * depth
    wide = 128
    factor = 1.4426950408889634 / depth**0.5
    rows = q.shape[0]
    tokens = rows // SPLIT
    half = rows // 2
    low = lax.broadcasted_iota(jnp.int32, (rows, wide), 1) < wide // 2
    keys = sum(piece.shape[0] for piece in kv)
    ones = jnp.ones((keys, wide), jnp.bfloat16)

    def scores_of(head):
        columns = slice(head * depth, (head + 1) * depth)
        query = q[:, columns]
        key = jnp.concatenate([piece[:, columns] for piece in kv], axis=0)
        return lax.dot_general(query, key, (((1,), (1,)), ((), ())), preferred_element_type=jnp.float32)

    summed = jnp.zeros((rows, wide), jnp.float32)
    upcoming = scores_of(0)
    for head in range(heads):
        scores = upcoming
        if head + 1 < heads:
            upcoming = scores_of(head + 1)
        top = jnp.broadcast_to(jnp.max(scores, axis=1, keepdims=True), (rows, wide))
        if not first:
            before = top_in[head]
            top = jnp.maximum(top, before)
        expo = jnp.concatenate(
            [
                jnp.exp2((scores[:, at : at + wide] - top[:, : min(wide, keys - at)]) * factor).astype(jnp.bfloat16)
                for at in range(0, keys, wide)
            ],
            axis=1,
        )
        at = group + (head // 2) * wide
        value = jnp.concatenate([piece[:, at : at + wide] for piece in kv], axis=0)
        mixed = dot(expo, jnp.concatenate([value, ones], axis=1))
        weighed, total = mixed[:, :wide], mixed[:, wide:]
        if not first:
            decay = jnp.exp2((before - top) * factor)
            weighed = weighed + mixed_in[head, :, :wide] * decay
            total = total + mixed_in[head, :, wide:] * decay
        if not last:
            top_out[head] = top
            mixed_out[head, :, :wide] = weighed
            mixed_out[head, :, wide:] = total
            continue
        mine = low if head % 2 == 0 else jnp.logical_not(low)
        summed = summed + jnp.where(mine, weighed * pl.reciprocal(total), 0.0)
    if not last:
        return
    summed = summed + pltpu.roll(summed, wide // 2, 1)
    upper = summed[:half]
    upper = jnp.concatenate([upper[:tokens] + stream[...], upper[tokens:]], axis=0)
    out[...] = jnp.where(low[:half], upper, summed[half:]).astype(out.dtype)


def collect_kernel(*refs):
    pieces, out = refs[:-1], refs[-1]
    tokens = pieces[0].shape[0]
    for at, piece in zip((0, 1, 3, 2), pieces):
        out[at * tokens : (at + 1) * tokens, :] = piece[...]


def gather_kernel(own, three, two, one, out):
    rows, wide = own.shape
    half = rows // 2

    def swap_rows(x):
        return jnp.concatenate([x[half:], x[:half]], axis=0)

    own, one, two, three = (ref[...].astype(jnp.float32) for ref in (own, one, two, three))
    far = two + swap_rows(three)
    latent = (own + swap_rows(one)) + pltpu.roll(far, wide // 2, 1)
    out[...] = latent.astype(jnp.bfloat16)


def finish_kernel(frames, n, cols, order, index, *refs):
    members = n // SPLIT
    patches, refs = refs[:members], refs[members:]
    (chosen, in_weight, held, grouped, gain, shift, out, grid, stacked, first, taps, merged) = refs
    channels = gain.shape[1]
    wide = grid.shape[-1]
    half = wide // 2
    me = index[0]
    grid[:, 0] = jnp.zeros((frames, cols, wide), jnp.bfloat16)
    grid[:, n + 1] = jnp.zeros((frames, cols, wide), jnp.bfloat16)
    tokens = frames * cols
    for member in range(members):
        latent = patches[member][...].astype(jnp.float32)
        rows = latent.shape[0]
        column = lax.broadcasted_iota(jnp.int32, latent.shape, 0) % cols
        before = jnp.where(column == 0, 0.0, pltpu.roll(latent, 1, 0))
        after = jnp.where(column == cols - 1, 0.0, pltpu.roll(latent, rows - 1, 0))
        around = jnp.concatenate([before, latent, after], axis=1).astype(jnp.bfloat16)
        patch = dot(around, chosen[...]).astype(jnp.bfloat16)
        for step in range(SPLIT):
            row = me ^ (rest_mask(order[member]) | (step << 2))
            at, lanes = (step % 2) * tokens, (step // 2) * wide
            for t in range(frames):
                grid[t, row + 1] = patch[at + t * cols : at + (t + 1) * cols, lanes : lanes + wide]

    cells = n * cols
    chunk = min(cells, 256)
    rows_in = chunk // cols
    upper = lax.broadcasted_iota(jnp.int32, (rows_in, cols, wide), 2) < half
    depth = 2 * wide
    for t in range(frames):
        for r in range(0, n, rows_in):
            near = grid[t, r + 1 : r + 1 + rows_in]
            far = jnp.where(upper, grid[t, r + 2 : r + 2 + rows_in], grid[t, r : r + rows_in])
            stacked[r * cols : r * cols + chunk, t * depth : t * depth + wide] = near.reshape(chunk, wide)
            stacked[r * cols : r * cols + chunk, t * depth + wide : (t + 1) * depth] = far.reshape(chunk, wide)

    counted = 4.0 * frames * cells
    members_of = channels // GROUPS
    sums = jnp.zeros((8, channels), jnp.float32)
    squares = jnp.zeros((8, channels), jnp.float32)
    pivot = None
    for t in range(frames):
        for r in range(0, n, rows_in):
            for row in range(2):
                lanes = slice(row * 2 * channels, (row + 1) * 2 * channels)
                both = dot(
                    stacked[r * cols : r * cols + chunk, : (t + 1) * depth],
                    in_weight[(frames - 1 - t) * depth :, lanes],
                )
                first[t, r : r + rows_in, :, lanes] = both.reshape(rows_in, cols, 2 * channels)
                for here in (both[:, :channels], both[:, channels:]):
                    if pivot is None:
                        pivot = jnp.sum(here, axis=0, keepdims=True) / chunk
                    off = (here - pivot).reshape(chunk // 8, 8, channels)
                    sums = sums + jnp.sum(off, axis=0)
                    squares = squares + jnp.sum(off * off, axis=0)

    def over_group(line):
        high = line.astype(jnp.bfloat16)
        rest = line - high.astype(jnp.float32)
        middle = rest.astype(jnp.bfloat16)
        lower = (rest - middle.astype(jnp.float32)).astype(jnp.bfloat16)
        none = jnp.zeros((13, channels), jnp.bfloat16)
        terms = jnp.concatenate([high, middle, lower, none], axis=0)
        return jnp.sum(dot(terms, grouped[...])[:8], axis=0, keepdims=True)

    offset = jnp.sum(sums, axis=0, keepdims=True) / counted
    channel_mean = pivot + offset
    mean = over_group(channel_mean) / members_of
    apart = channel_mean - mean
    within = jnp.sum(squares, axis=0, keepdims=True) / counted - offset * offset
    variance = over_group(within + apart * apart) / members_of
    slope = gain[...] / jnp.sqrt(variance + EPS)
    bias = shift[...]

    place = lax.broadcasted_iota(jnp.int32, (cols, channels), 0)
    for t in range(frames):
        for line in range(4):
            sub = 1 if line in (0, 2) else 0
            token_row = me - 1 if line == 0 else (me + 1 if line == 3 else me)
            inside = jnp.logical_and(token_row >= 0, token_row < n)
            token_row = jnp.clip(token_row, 0, n - 1)
            keep = jnp.where(inside, 0.5, 0.0)
            pair = []
            for side in range(2):
                part = sub * 2 + side
                x = first[t, token_row, :, part * channels : (part + 1) * channels]
                y = (x - mean) * slope + bias
                pair.append((y * keep) * (1.0 + jnp.tanh(0.5 * y)))
            even, odd = pair
            taps[t, line, 0] = jnp.where(place == 0, 0.0, pltpu.roll(odd, 1, 0)).astype(jnp.bfloat16)
            taps[t, line, 1] = even.astype(jnp.bfloat16)
            taps[t, line, 2] = odd.astype(jnp.bfloat16)
            taps[t, line, 3] = jnp.where(place == cols - 1, 0.0, pltpu.roll(even, cols - 1, 0)).astype(jnp.bfloat16)

    here = 4 * cols
    totals = [jnp.zeros((here, channels), jnp.float32) for _ in range(frames)]
    left = jnp.concatenate(
        [taps[:, b : b + 2, w : w + 2].reshape(frames * here, channels) for b in range(3) for w in range(3)], axis=1
    )
    deep = 9 * channels
    now = held[2].reshape(deep, channels)
    then = held[1].reshape(deep, channels)
    got = dot(left, jnp.concatenate([now, then], axis=1))
    first_got = dot(left[:here], held[0].reshape(deep, channels))
    for t in range(frames):
        totals[t] = totals[t] + got[t * here : (t + 1) * here, :channels]
        if t + 1 < frames:
            totals[t + 1] = totals[t + 1] + got[t * here : (t + 1) * here, channels:]
    totals[2] = totals[2] + first_got
    for t in range(frames):
        for part in range(4):
            kept = first[t, me, :, part * channels : (part + 1) * channels]
            block = totals[t][part * cols : (part + 1) * cols] + kept
            for lane in range(channels // 128):
                tile = block[:, lane * 128 : (lane + 1) * 128]
                merged[t, part // 2, lane, pl.ds(part % 2, cols, stride=2), :] = tile
    for t in range(frames):
        for sub in range(2):
            for lane in range(channels // 128):
                out[t, sub, :, lane * 128 : (lane + 1) * 128] = merged[t, sub, lane].astype(jnp.bfloat16)


def widened(weight):
    blocks = []
    for row in range(2):
        for col in range(2):
            blocks.append(jnp.pad(weight, ((0, 0), (row, 1 - row), (col, 1 - col), (0, 0), (0, 0))))
    whole = jnp.concatenate(blocks, axis=-1)
    whole = jnp.concatenate([whole[:, 1:], whole[:, :1]], axis=1)
    return whole.reshape(-1, whole.shape[-1])


def chooser(latent):
    source = jnp.arange(3 * 8 * latent)
    target = jnp.arange(2 * 8 * latent)
    offset, lane = source // (8 * latent), source % (8 * latent)
    side, lane = lane // (4 * latent), lane % (4 * latent)
    row, col, channel = lane // (2 * latent), lane // latent % 2, lane % latent
    cell = 2 * (offset - 1) + col + 1
    to_side, to_lane = target // (8 * latent), target % (8 * latent)
    to_row, to_cell, to_channel = to_lane // (4 * latent), to_lane // latent % 4, to_lane % latent
    same = (
        (side[:, None] == to_side)
        & (row[:, None] == to_row)
        & (cell[:, None] == to_cell)
        & (channel[:, None] == to_channel)
    )
    return same.astype(jnp.bfloat16)


def shards(
    queries, keys, values, stream, head_weight, conv_in_weight, norm_gain, norm_shift, conv_mid_weight
):
    frames, _, cols, width = queries.shape
    n = lax.axis_size("seq")
    members = n // SPLIT
    depth = width // HEADS
    heads = HEADS // SPLIT
    tokens = frames * cols
    group = heads * depth
    latent = head_weight.shape[1] // 4
    wide = 2 * head_weight.shape[1]
    channels = norm_gain.shape[0]
    pairs = (heads + 1) // 2
    index = lax.axis_index("seq").astype(jnp.int32).reshape(1)
    bf16, f32 = jnp.bfloat16, jnp.float32

    head_lanes = head_weight.T
    prepared = pl.pallas_call(
        functools.partial(prepare_kernel, depth, heads),
        out_shape=[jax.ShapeDtypeStruct((tokens, group + pairs * wide), bf16)] * SPLIT
        + [jax.ShapeDtypeStruct((tokens, group), bf16)] * SPLIT,
        in_specs=[SMEM] + [HBM] * 4,
        out_specs=[VMEM] * (2 * SPLIT),
        scratch_shapes=[
            pltpu.VMEM((tokens, width), bf16),
            pltpu.VMEM((wide // 2, width), bf16),
            pltpu.VMEM((SPLIT, tokens, pairs * wide), bf16),
            pltpu.SemaphoreType.DMA((2 + 2 * SPLIT,)),
        ],
        compiler_params=pltpu.CompilerParams(vmem_limit_bytes=int(53.2 * 2**20)),
        name="prepare",
    )(
        index,
        queries.reshape(tokens, width),
        keys.reshape(tokens, width),
        values.reshape(tokens, width),
        head_lanes,
    )
    streamed = pl.pallas_call(
        stream_kernel,
        out_shape=jax.ShapeDtypeStruct((tokens, wide), f32),
        in_specs=[VMEM] * 2,
        out_specs=VMEM,
        compiler_params=pltpu.CompilerParams(vmem_limit_bytes=4 * 2**20),
        cost_estimate=pl.CostEstimate(flops=2 * 10**8, bytes_accessed=10**6, transcendentals=0),
        name="stream",
    )(stream.reshape(tokens, width), head_lanes)
    kv, q = list(prepared[:SPLIT]), list(prepared[SPLIT:])
    both = exchanged(jnp.concatenate([kv[1], q[1]], axis=1), 1 << 2)
    kv[1], q[1] = both[:, : kv[1].shape[1]], both[:, kv[1].shape[1] :]
    for step in range(2, SPLIT):
        kv[step] = exchanged(kv[step], step << 2)
    q[2:] = lax.optimization_barrier((q[2:], kv[2]))[0]
    for step in range(2, SPLIT):
        q[step] = exchanged(q[step], step << 2)

    def spread(pieces):
        block = jnp.concatenate(pieces, axis=0)
        return [block] + [exchanged(block, rest_mask(member)) for member in range(2, members, 2)]

    near = jnp.concatenate(spread(kv[:2]), axis=0)
    near = [near, exchanged(near, 1)]
    waited = [kv[2]] + lax.optimization_barrier((kv[3:], near[0]))[0]
    far = [exchanged(piece, rest_mask(member)) for piece in waited for member in range(2, members, 2)]
    held = jnp.concatenate(waited, axis=0)
    limit = pltpu.CompilerParams(vmem_limit_bytes=(12 + 2 * members // 4 * 4) * 2**20)
    queried = pl.pallas_call(
        collect_kernel,
        out_shape=jax.ShapeDtypeStruct((SPLIT * tokens, group), bf16),
        in_specs=[VMEM] * SPLIT,
        out_specs=VMEM,
        compiler_params=pltpu.CompilerParams(vmem_limit_bytes=4 * 2**20),
        cost_estimate=pl.CostEstimate(flops=5 * 10**9, bytes_accessed=10**6, transcendentals=0),
        name="collect",
    )(q[0], q[1], q[3], q[2])
    state = [jax.ShapeDtypeStruct((heads, SPLIT * tokens, size), f32) for size in (wide, 2 * wide)]

    def attended(blocks, carried, last, name):
        return pl.pallas_call(
            functools.partial(attend_kernel, depth, heads, not carried, bool(last)),
            out_shape=jax.ShapeDtypeStruct((SPLIT * tokens // 2, wide), bf16) if last else state,
            in_specs=[VMEM] * (1 + len(blocks) + len(carried) + len(last)),
            out_specs=VMEM if last else [VMEM] * 2,
            compiler_params=limit,
            cost_estimate=pl.CostEstimate(flops=10**8, bytes_accessed=10**5, transcendentals=0),
            name=name,
        )(queried, *blocks, *carried, *last)

    carried = attended(near, [], [], "attend_near")
    beside = exchanged(held, 1)
    middle = carried
    carried = attended([held, beside], carried, [], "attend_middle")
    passed = lax.optimization_barrier((far, middle))[0]
    far = passed
    far = far + [exchanged(block, 1) for block in far]
    part = attended(far, carried, [streamed], "attend_far")

    others = [exchanged(part, step << 2) for step in (3, 2, 1)]
    patch = pl.pallas_call(
        gather_kernel,
        out_shape=jax.ShapeDtypeStruct(part.shape, bf16),
        in_specs=[VMEM] * 4,
        out_specs=VMEM,
        compiler_params=pltpu.CompilerParams(vmem_limit_bytes=4 * 2**20),
        name="gather",
    )(part, *others)
    order = sorted(range(1, members), key=lambda member: -member)
    patches = [patch] + [exchanged(patch, rest_mask(member)) for member in order]

    lane = jnp.arange(channels) // (channels // GROUPS)
    in_weight = widened(conv_in_weight)
    grouped = (lane[:, None] == lane[None, :]).astype(bf16)
    return pl.pallas_call(
        functools.partial(finish_kernel, frames, n, cols, [0] + order),
        out_shape=jax.ShapeDtypeStruct((frames, 2, 2 * cols, channels), bf16),
        in_specs=[SMEM] + [VMEM] * (members + 6),
        out_specs=VMEM,
        scratch_shapes=[
            pltpu.VMEM((frames, n + 2, cols, wide), bf16),
            pltpu.VMEM((n * cols, frames * 2 * wide), bf16),
            pltpu.VMEM((frames, n, cols, 4 * channels), f32),
            pltpu.VMEM((frames, 4, 4, cols, channels), bf16),
            pltpu.VMEM((frames, 2, channels // 128, 2 * cols, 128), f32),
        ],
        compiler_params=pltpu.CompilerParams(vmem_limit_bytes=(16 if n <= 16 else 40) * 2**20),
        name="finish",
    )(
        index,
        *patches,
        chooser(latent),
        in_weight,
        conv_mid_weight,
        grouped,
        norm_gain.reshape(1, channels),
        norm_shift.reshape(1, channels),
    )


def solution(mesh):
    placed = (
        P("groups", "seq", None, None),
        P("groups", "seq", None, None),
        P("groups", "seq", None, None),
        P("groups", "seq", None, None),
        P(),
        P(),
        P(),
        P(),
        P(),
    )
    return jax.shard_map(
        shards,
        mesh=mesh,
        in_specs=placed,
        out_specs=P("groups", "seq", None, None),
        check_vma=False,
    )
```
